512 devices in a mesh: elem: 16 (over x, z_hi), freq: 32 (over z_lo, y, core).
Axes of the slice: x: 4, y: 8, z: 8 (z_hi: 4, z_lo: 2; z = z_hi * 2 + z_lo), core: 2. Of those that a mesh axis runs over, the one named last changes fastest.
Arguments:
- pole_freq: float32 [16], replicated, may hold values from 0.05 to 0.95, as said below
- pole_damp: float32 [16], replicated, may hold values from 0.01 to 0.05
- samples: float32 [2, 32768, 6144], P(None, 'freq', 'elem'), may hold values from -30 to 30
Outputs:
- reduced: float32 [33, 33, 6144], P(None, None, ('elem', 'freq'))
- system: float32 [33, 33], replicated
- norm_row: float32 [33], replicated
The draws below stay inside these ranges and needn't reach their ends.
Inputs may be any that keep to these rules, and one draw needn't show every extreme that they name: `pole_freq`: increasing; neighbours lie at least 0.54 / 16 apart.
All inputs are finite; a program needn't handle non-finite values.
Results may differ from the reference program's by a relative error of at most 0.0003.
Values sent between devices are 32-bit elements; how exact they have to be, the bound alone decides.
A program may use at most 64 MiB of HBM per device.

```python
import math
import jax
import jax.numpy as jnp
from jax import lax

NP = 32
NPAIR = 16
ELEMS = 6144
NF = 32768


def draw_pole_freq(key, part):
    key = jax.random.fold_in(key, 7)
    jitter = jax.random.uniform(key, (NPAIR,), jnp.float32, -0.2, 0.2)
    return 0.05 + 0.9 * (jnp.arange(NPAIR, dtype=jnp.float32) + 0.5 + jitter) / NPAIR


def draw_samples(key, part):
    omega = 0.02 + 0.98 * (jnp.arange(NF, dtype=jnp.float32) + 0.5) / NF
    key = jax.random.fold_in(key, 5)
    keys = jax.random.split(key, 7)
    data_freq = jax.random.uniform(keys[0], (8,), jnp.float32, 0.05, 0.95)
    data_damp = jnp.exp(jax.random.uniform(keys[1], (8,), jnp.float32, jnp.log(0.01), jnp.log(0.05)))
    residues = jax.random.uniform(keys[2], (2, 8, ELEMS), jnp.float32, -1.0, 1.0)
    freq_col = omega[:, None]
    smooth_re = jnp.zeros((NF, ELEMS), jnp.float32)
    smooth_im = jnp.zeros((NF, ELEMS), jnp.float32)
    for member in range(8):
        offset = freq_col - data_freq[member]
        denom = data_damp[member] * data_damp[member] + offset * offset
        term_re = data_damp[member] * data_damp[member] / denom
        term_im = -data_damp[member] * offset / denom
        smooth_re = smooth_re + term_re * residues[0, member][None, :] - term_im * residues[1, member][None, :]
        smooth_im = smooth_im + term_re * residues[1, member][None, :] + term_im * residues[0, member][None, :]
    column_scale = jnp.exp(jax.random.uniform(keys[3], (NF,), jnp.float32, -1.15, 1.15))
    ramp = 1.0 + 2.0 * jnp.arange(ELEMS, dtype=jnp.float32) / max(ELEMS - 1, 1)
    noise = jax.random.normal(keys[5], (2, NF, ELEMS), jnp.float32)
    elem_scale = ramp * jnp.exp(jax.random.uniform(keys[6], (ELEMS,), jnp.float32, -1.15, 1.15))
    values = jnp.stack([smooth_re, smooth_im]) + 0.3 * noise * column_scale[None, :, None]
    return jnp.clip(values * elem_scale[None, None, :], -30.0, 30.0)


def setup_inputs(seed: int = 0) -> dict:
    key_of = jax.random.split(jax.random.key(seed), 4)
    pole_freq = draw_pole_freq(jax.random.fold_in(key_of[3], 71), 0)
    pole_damp = jnp.clip(jnp.exp(jax.random.uniform(key_of[1], (NPAIR,), jnp.float32, math.log(0.01), math.log(0.05))), 0.01, 0.05)
    samples = draw_samples(jax.random.fold_in(key_of[3], 71), 0)
    return dict(pole_freq=pole_freq, pole_damp=pole_damp, samples=samples)


HIGH = lax.Precision.HIGHEST

def pole_basis(omega, pole_freq, pole_damp):
    freq_col = omega[:, None]
    damp = pole_damp[None, :]
    centre = pole_freq[None, :]
    below = freq_col - centre
    above = freq_col + centre
    first_den = damp * damp + below * below
    second_den = damp * damp + above * above
    sum_re = damp * (damp / first_den + damp / second_den)
    sum_im = damp * (-below / first_den - above / second_den)
    dif_re = damp * (below / first_den - above / second_den)
    dif_im = damp * (damp / first_den - damp / second_den)
    ones_col = jnp.ones_like(omega)[:, None]
    zero_col = jnp.zeros_like(omega)[:, None]
    real_rows = jnp.concatenate([sum_re, dif_re, ones_col], axis=1)
    imag_rows = jnp.concatenate([sum_im, dif_im, zero_col], axis=1)
    return (real_rows.T, imag_rows.T)

def gram_tables(real_t, imag_t):
    count = real_t.shape[1]
    re_q = real_t[:, None, :] * real_t[None, :, :] + imag_t[:, None, :] * imag_t[None, :, :]
    im_q = real_t[:, None, :] * imag_t[None, :, :] - imag_t[:, None, :] * real_t[None, :, :]
    return (re_q.reshape(-1, count), im_q.reshape(-1, count))

def reference(pole_freq, pole_damp, samples):
    width = NP + 1
    freq_total = samples.shape[1]
    elem_total = samples.shape[2]
    inv_nf = 1.0 / freq_total
    position = jnp.arange(freq_total, dtype=jnp.int32).astype(jnp.float32)
    omega = 0.02 + 0.98 * (position + 0.5) / freq_total
    real_t, imag_t = pole_basis(omega, pole_freq, pole_damp)
    re_q, im_q = gram_tables(real_t, imag_t)
    basis_gram = (lax.optimization_barrier(jnp.sum(re_q, axis=1)) * inv_nf).reshape(width, width)
    row_mean = lax.optimization_barrier(jnp.sum(real_t, axis=1)) * inv_nf
    table = jnp.concatenate([re_q, -im_q], axis=1)
    stacked = samples.reshape(2 * freq_total, elem_total)
    coupling = -jnp.dot(table.astype(jnp.float32), stacked.astype(jnp.float32), precision=HIGH, preferred_element_type=jnp.float32) * inv_nf
    power = lax.optimization_barrier(jnp.sum(samples * samples, axis=(0, 2)))
    data_gram = jnp.dot(re_q.astype(jnp.float32), power.astype(jnp.float32), precision=HIGH, preferred_element_type=jnp.float32) * inv_nf
    total_sq = jnp.sum(power)
    factor = jnp.linalg.cholesky(basis_gram)
    solved = lax.linalg.triangular_solve(factor, coupling.reshape(width, width * elem_total), left_side=True, lower=True)
    reduced = solved.reshape(width, width, elem_total)
    correction = jnp.einsum('ijk,ilk->jl', reduced, reduced, precision=HIGH)
    system = (data_gram.reshape(width, width) - correction) / (total_sq * inv_nf)
    norm_row = row_mean * jnp.sqrt(total_sq * inv_nf / elem_total)
    return (reduced, system, norm_row)
```

```python
import jax
import jax.numpy as jnp
from jax import lax
from jax.experimental import pallas as pl
from jax.experimental.pallas import tpu as pltpu
from jax.sharding import PartitionSpec as P

HIGH = lax.Precision.HIGHEST
MESH = pl.DeviceIdType.MESH
F32 = jnp.float32

NX, NZH, NZL, NY, NC = 4, 4, 2, 8, 2
NZ = NZH * NZL
NZY = NZL * NY
NFREQ = NZY * NC
PAIRS = 16
WIDTH = 2 * PAIRS + 1
ROWS = 40
OWN = 12
SLOT = 16
LANES = 128
FREQ_LOCAL = 1024
ELEM_LOCAL = OWN * NFREQ
FREQ_TOTAL = FREQ_LOCAL * NFREQ
ELEM_TOTAL = ELEM_LOCAL * NX * NZH
INV_NF = 1.0 / FREQ_TOTAL


def iota(shape, dim):
    return lax.broadcasted_iota(jnp.int32, shape, dim)


def omega_of(position):
    return 0.02 + 0.98 * (position.astype(F32) + 0.5) / FREQ_TOTAL


def pick(ref, index, shape):
    out = jnp.zeros(shape, F32)
    for m in range(PAIRS):
        out = jnp.where(index == m, ref[m], out)
    return out


def pair_coefs(ci, di, cj, dj, row_sum, col_sum):
    both = di + dj
    gap = cj - ci
    tot = ci + cj
    n1 = both * both + gap * gap
    n2 = both * both + tot * tot
    r1 = 1.0 / n1
    r2 = 1.0 / n2
    alpha, beta = both * r1, gap * r1
    gamma, delta = both * r2, -tot * r2
    ss = di * (alpha + gamma)
    bd = di * (beta - delta)
    bs = di * (beta + delta)
    am = di * (alpha - gamma)
    cr = jnp.where(row_sum, jnp.where(col_sum, ss, -bd), jnp.where(col_sum, bs, am))
    ce = jnp.where(row_sum, jnp.where(col_sum, bd, ss), jnp.where(col_sum, -am, bs))
    return cr, ce


def coef_tables(pf, pd):
    shape = (ROWS, LANES)
    row, col = iota(shape, 0), iota(shape, 1)
    ci = pick(pf, row % PAIRS, shape)
    di = pick(pd, row % PAIRS, shape)
    cj = pick(pf, col % PAIRS, shape)
    dj = pick(pd, col % PAIRS, shape)
    inside = (row < 2 * PAIRS) & (col < 2 * PAIRS)
    row_sum, col_sum = row < PAIRS, col < PAIRS
    cr, ce = pair_coefs(ci, di, cj, dj, row_sum, col_sum)
    crt, cet = pair_coefs(cj, dj, ci, di, col_sum, row_sum)
    last_row = row == 2 * PAIRS
    last_col = col == 2 * PAIRS
    one = lambda cond: jnp.where(cond, 1.0, 0.0).astype(F32)
    cr = jnp.where(inside, cr, one(last_row & ((col < PAIRS) | last_col)))
    ce = jnp.where(inside, ce, one(last_row & (col >= PAIRS) & (col < 2 * PAIRS)))
    crt = jnp.where(inside, crt, one(last_col & (row < PAIRS)))
    cet = jnp.where(inside, cet, one(last_col & (row >= PAIRS) & (row < 2 * PAIRS)))
    return cr, ce, crt, cet


def assemble(tables, r_row, e_row, r_col, e_col):
    cr, ce, crt, cet = tables
    zero = jnp.zeros((8, LANES), F32)
    rp = jnp.concatenate([r_col, r_col, zero], axis=0)
    ep = jnp.concatenate([e_col, e_col, zero], axis=0)
    return cr * r_row + ce * e_row + crt * rp + cet * ep


def col_to_row(col):
    row, lane = iota((PAIRS, LANES), 0), iota((PAIRS, LANES), 1)
    keep = (lane % PAIRS == row) & (lane < 2 * PAIRS)
    return jnp.sum(jnp.where(keep, col, 0.0), axis=0, keepdims=True)


def row_to_col(row_vec, first):
    row, lane = iota((PAIRS, LANES), 0), iota((PAIRS, LANES), 1)
    kept = jnp.where(lane == row + first, jnp.broadcast_to(row_vec, (PAIRS, LANES)), 0.0)
    return jnp.broadcast_to(jnp.sum(kept, axis=1, keepdims=True), (PAIRS, LANES))


def rows_from(values, const):
    lane = iota(values.shape, 1)
    r_row = jnp.where(
        lane < PAIRS,
        values,
        jnp.where(
            lane < 2 * PAIRS,
            pltpu.roll(values, PAIRS, 1),
            jnp.where(lane == 2 * PAIRS, const, 0.0),
        ),
    )
    e_row = jnp.where(
        lane < PAIRS,
        pltpu.roll(values, LANES - PAIRS, 1),
        jnp.where(lane < 2 * PAIRS, values, 0.0),
    )
    return r_row, e_row


def kernel(
    pf, pd, s_hbm, red_hbm, sys_ref, nrm_ref,
    s_buf, re_buf, im_buf, xt_buf, pieces, recv_a, sum_a, recv_b,
    red_buf, pk_buf, recv_c, buf_y, buf_z, buf_x,
    load_sem, out_sem, send_sem, recv_sem,
):
    elem, freq = lax.axis_index("elem"), lax.axis_index("freq")
    x, z_hi = elem // NZH, elem % NZH
    zy, core = freq // NC, freq % NC
    z_lo, y = zy // NY, zy % NY
    z = z_hi * NZL + z_lo

    def at_zy(other):
        return {"elem": elem, "freq": other * NC + core}

    def at_y(other):
        return {"elem": elem, "freq": (z_lo * NY + other) * NC + core}

    def at_z(other):
        return {
            "elem": x * NZH + other // NZL,
            "freq": ((other % NZL) * NY + y) * NC + core,
        }

    def at_x(other):
        return {"elem": other * NZH + z_hi, "freq": freq}

    sibling = {"elem": elem, "freq": zy * NC + (1 - core)}

    loads = [
        pltpu.make_async_copy(s_hbm.at[part], s_buf.at[part], load_sem.at[part])
        for part in range(2)
    ]
    for load in loads:
        load.start()

    barrier = pltpu.get_barrier_semaphore()

    def greet(device):
        pl.semaphore_signal(barrier, inc=1, device_id=device, device_id_type=MESH)

    greet(sibling)
    for step in range(1, NZY):
        greet(at_zy((zy + step) % NZY))
    for step in range(1, NZH):
        for low in range(NZL):
            greet(at_z(((z_hi + step) % NZH) * NZL + low))
    for step in range(1, NX):
        greet(at_x((x + step) % NX))
    greeted = 1 + (NZY - 1) + (NZH - 1) * NZL + (NX - 1)

    column = iota((PAIRS, LANES), 0)
    c_col = pick(pf, column, (PAIRS, LANES))
    d_col = pick(pd, column, (PAIRS, LANES))
    d_sq = d_col * d_col
    lane8 = iota((8, LANES), 1)
    lane16 = iota((PAIRS, LANES), 1)
    re_buf[2 * PAIRS :, :] = jnp.where(iota((8, FREQ_LOCAL), 0) == 0, 1.0, 0.0).astype(F32)
    for tile in range(FREQ_LOCAL // LANES):
        at = pl.ds(tile * LANES, LANES)
        w = omega_of(freq * FREQ_LOCAL + tile * LANES + lane16)
        below, above = w - c_col, w + c_col
        i1 = 1.0 / (d_sq + below * below)
        i2 = 1.0 / (d_sq + above * above)
        re_buf[0:PAIRS, at] = d_sq * (i1 + i2)
        re_buf[PAIRS : 2 * PAIRS, at] = d_col * (below * i1 - above * i2)
        im_buf[0:PAIRS, at] = -d_col * (below * i1 + above * i2)
        im_buf[PAIRS : 2 * PAIRS, at] = d_sq * (i1 - i2)

    loads[0].wait()
    x0 = jnp.dot(re_buf[...], s_buf[0], precision=HIGH, preferred_element_type=F32)
    loads[1].wait()
    x1 = jnp.dot(im_buf[...], s_buf[1], precision=HIGH, preferred_element_type=F32)

    stacked = jnp.concatenate(
        [
            x0[0 : 2 * PAIRS],
            x1,
            x0[2 * PAIRS : ROWS],
            jnp.zeros((LANES - 4 * PAIRS - 8, ELEM_LOCAL), F32),
        ],
        axis=0,
    )
    for tile in range(ELEM_LOCAL // LANES):
        xt_buf[tile * LANES : (tile + 1) * LANES, :] = stacked[
            :, tile * LANES : (tile + 1) * LANES
        ].T
    xt_buf[ELEM_LOCAL:, :] = jnp.zeros((8, LANES), F32)
    for f in range(NFREQ):
        pieces[f % NC, f // NC] = xt_buf[OWN * f : OWN * f + SLOT, :]

    pl.semaphore_wait(barrier, greeted)

    copy_a = pltpu.make_async_remote_copy(
        src_ref=pieces.at[1 - core],
        dst_ref=recv_a,
        send_sem=send_sem.at[0],
        recv_sem=recv_sem.at[0],
        device_id=sibling,
        device_id_type=MESH,
    )
    copy_a.start()

    c_half = [c_col[0:8], c_col[8:16]]
    q_half = [d_sq[0:8], d_sq[8:16]]

    def mean_step(chunk, acc):
        acc = list(acc)
        for tile in range(FREQ_LOCAL // LANES):
            w = omega_of(chunk * FREQ_LOCAL + tile * LANES + lane8)
            for h in range(2):
                below, above = w - c_half[h], w + c_half[h]
                n1 = q_half[h] + below * below
                n2 = q_half[h] + above * above
                r = 1.0 / (n1 * n2)
                i1, i2 = r * n2, r * n1
                acc[2 * h] = acc[2 * h] + (i1 + i2)
                acc[2 * h + 1] = acc[2 * h + 1] + (below * i1 - above * i2)
        return tuple(acc)

    zero8 = jnp.zeros((8, LANES), F32)
    acc = lax.fori_loop(0, NFREQ, mean_step, (zero8,) * 4)

    def lane_sum(v):
        return jnp.broadcast_to(jnp.sum(v, axis=1, keepdims=True), v.shape)

    mean_r = d_sq * lane_sum(jnp.concatenate([acc[0], acc[2]], axis=0)) * INV_NF
    mean_e = d_col * lane_sum(jnp.concatenate([acc[1], acc[3]], axis=0)) * INV_NF

    copy_a.wait_recv()
    for k in range(NZY):
        sum_a[k] = pieces[core, k] + recv_a[k]

    sends_b = []
    for step in range(1, NZY):
        other = (zy + step) % NZY
        copy = pltpu.make_async_remote_copy(
            src_ref=sum_a.at[other],
            dst_ref=recv_b.at[zy],
            send_sem=send_sem.at[1],
            recv_sem=recv_sem.at[1],
            device_id=at_zy(other),
            device_id_type=MESH,
        )
        copy.start()
    recv_b[zy] = sum_a[zy]

    tables = coef_tables(pf, pd)
    lane1 = iota((1, LANES), 1)
    mean_r_row, mean_e_row = col_to_row(mean_r), col_to_row(mean_e)
    gram = assemble(
        tables,
        jnp.where(lane1 == 2 * PAIRS, 1.0, mean_r_row),
        mean_e_row,
        mean_r,
        mean_e,
    )
    row, lane = iota((ROWS, LANES), 0), iota((ROWS, LANES), 1)
    work = gram + jnp.where((lane == row + 64) & (row < WIDTH), 1.0, 0.0)
    for k in range(WIDTH):
        pivot_row = work[k : k + 1, :]
        scale = 1.0 / work[k : k + 1, k : k + 1]
        factor = jnp.where(row > k, jnp.broadcast_to(work[:, k : k + 1], (ROWS, LANES)), 0.0)
        work = work - factor * (pivot_row * scale)
    pivots = jnp.sum(jnp.where((lane == row) & (row < WIDTH), work, 0.0), axis=1, keepdims=True)
    pivots = jnp.where(iota((ROWS, 1), 0) < WIDTH, pivots, 1.0)
    inverse = pltpu.roll(work, 64, 1) * (1.0 / jnp.sqrt(pivots))
    inverse = jnp.where(lane < WIDTH, inverse, 0.0)

    power = jnp.zeros((FREQ_LOCAL, LANES), F32)
    for tile in range(ELEM_LOCAL // LANES):
        at = pl.ds(tile * LANES, LANES)
        a, b = s_buf[0, :, at], s_buf[1, :, at]
        power = power + (a * a + b * b)
    q = jnp.dot(re_buf[...], power, precision=HIGH, preferred_element_type=F32)
    q = jnp.broadcast_to(jnp.sum(q, axis=1, keepdims=True), (ROWS, LANES))
    q_row = jnp.sum(jnp.where(lane == row, q, 0.0), axis=0, keepdims=True)

    pltpu.make_async_copy(
        recv_b.at[pl.ds(0, NZY - 1)], recv_b.at[pl.ds(0, NZY - 1)], recv_sem.at[1]
    ).wait()
    owned = recv_b[0]
    for k in range(1, NZY):
        owned = owned + recv_b[k]
    owned = owned * (-INV_NF)

    shifted = pltpu.roll(owned, LANES - 2 * PAIRS, 1)
    plus, minus = owned + shifted, owned - shifted
    r_rows, e_rows = rows_from(minus, shifted)
    plus_t = jnp.concatenate([plus, jnp.zeros((LANES - SLOT, LANES), F32)], axis=0).T
    blocks = []
    for k in range(OWN):
        r_col = jnp.broadcast_to(plus_t[0:PAIRS, k : k + 1], (PAIRS, LANES))
        e_col = jnp.broadcast_to(plus_t[PAIRS : 2 * PAIRS, k : k + 1], (PAIRS, LANES))
        blocks.append(
            assemble(tables, r_rows[k : k + 1, :], e_rows[k : k + 1, :], r_col, e_col)
        )
    coupling = jnp.concatenate(blocks, axis=1)
    reduced = jnp.dot(
        inverse[:, 0:ROWS], coupling, precision=HIGH, preferred_element_type=F32
    )
    parts = [reduced[:, k * LANES : (k + 1) * LANES] for k in range(OWN)]
    tall = jnp.concatenate(parts, axis=0)
    corr = lax.dot_general(
        tall[:, 0:ROWS], tall, (((0,), (0,)), ((), ())),
        precision=HIGH, preferred_element_type=F32,
    )

    sub8, ln8 = iota((8, LANES), 0), iota((8, LANES), 1)
    quarter = ln8 // 32
    square = jnp.where(ln8 < 32, corr[0:8], 0.0)
    for g in range(1, 4):
        square = jnp.where(quarter == g, pltpu.roll(corr[8 * g : 8 * g + 8], 32 * g, 1), square)
    border = jnp.where(
        sub8 == 0,
        jnp.broadcast_to(corr[32:33, :], (8, LANES)),
        jnp.where(sub8 == 1, jnp.broadcast_to(q_row, (8, LANES)), 0.0),
    )
    mine = jnp.concatenate([square, border], axis=0)
    pk_buf[...] = mine
    copy_c = pltpu.make_async_remote_copy(
        src_ref=pk_buf,
        dst_ref=recv_c,
        send_sem=send_sem.at[2],
        recv_sem=recv_sem.at[2],
        device_id=sibling,
        device_id_type=MESH,
    )
    copy_c.start()

    for k in range(OWN):
        red_buf[k] = parts[k][0:WIDTH, 0:WIDTH]
    out = pltpu.make_async_copy(red_buf, red_hbm, out_sem)
    out.start()

    copy_c.wait_recv()
    total = mine + recv_c[...]

    def stage(buf, count, me, place, index, total):
        buf[me] = total
        for step in range(1, count):
            pltpu.make_async_remote_copy(
                src_ref=buf.at[me],
                dst_ref=buf.at[me],
                send_sem=send_sem.at[index],
                recv_sem=recv_sem.at[index],
                device_id=place((me + step) % count),
                device_id_type=MESH,
            ).start()
        rest = buf.at[pl.ds(0, count - 1)]
        pltpu.make_async_copy(rest, rest, recv_sem.at[index]).wait()
        total = buf[0]
        for k in range(1, count):
            total = total + buf[k]
        return total

    total = stage(buf_y, NY, y, at_y, 3, total)
    total = stage(buf_z, NZ, z, at_z, 4, total)
    total = stage(buf_x, NX, x, at_x, 5, total)

    square = total[0:8]
    last = jnp.where(lane1 < WIDTH, total[8:9], 0.0)
    moments = total[9:10] * INV_NF
    mean_sq = moments[:, 2 * PAIRS : 2 * PAIRS + 1]
    r_row, e_row = rows_from(moments, moments)
    data_gram = assemble(
        tables, r_row, e_row, row_to_col(moments, 0), row_to_col(moments, PAIRS)
    )
    full = jnp.concatenate(
        [square] + [pltpu.roll(square, LANES - 32 * g, 1) for g in range(1, 4)]
        + [jnp.broadcast_to(last, (8, LANES))],
        axis=0,
    )
    last_col = jnp.sum(
        jnp.where(lane == row, jnp.broadcast_to(last, (ROWS, LANES)), 0.0),
        axis=1,
        keepdims=True,
    )
    full = jnp.where(lane == 2 * PAIRS, last_col, full)
    system = (data_gram - full) / mean_sq
    sys_ref[...] = system[0:WIDTH, 0:WIDTH]
    mean_row = jnp.where(
        lane1 < PAIRS,
        mean_r_row,
        jnp.where(lane1 < 2 * PAIRS, mean_e_row, 1.0),
    )
    nrm_ref[...] = (mean_row * jnp.sqrt(mean_sq * (1.0 / ELEM_TOTAL)))[:, 0:WIDTH]

    out.wait()
    copy_a.wait_send()
    rest = sum_a.at[pl.ds(0, NZY - 1)]
    pltpu.make_async_copy(rest, rest, send_sem.at[1]).wait()
    copy_c.wait_send()
    for buf, count, index in ((buf_y, NY, 3), (buf_z, NZ, 4), (buf_x, NX, 5)):
        rest = buf.at[pl.ds(0, count - 1)]
        pltpu.make_async_copy(rest, rest, send_sem.at[index]).wait()


def per_device(pole_freq, pole_damp, samples):
    vmem = lambda *shape: pltpu.VMEM(shape, F32)
    reduced, system, norm_row = pl.pallas_call(
        kernel,
        out_shape=(
            jax.ShapeDtypeStruct((OWN, WIDTH, WIDTH), F32),
            jax.ShapeDtypeStruct((WIDTH, WIDTH), F32),
            jax.ShapeDtypeStruct((1, WIDTH), F32),
        ),
        in_specs=[
            pl.BlockSpec(memory_space=pltpu.SMEM),
            pl.BlockSpec(memory_space=pltpu.SMEM),
            pl.BlockSpec(memory_space=pl.ANY),
        ],
        out_specs=(
            pl.BlockSpec(memory_space=pl.ANY),
            pl.BlockSpec(memory_space=pltpu.VMEM),
            pl.BlockSpec(memory_space=pltpu.VMEM),
        ),
        scratch_shapes=[
            vmem(2, FREQ_LOCAL, ELEM_LOCAL),
            vmem(ROWS, FREQ_LOCAL),
            vmem(2 * PAIRS, FREQ_LOCAL),
            vmem(ELEM_LOCAL + 8, LANES),
            vmem(NC, NZY, SLOT, LANES),
            vmem(NZY, SLOT, LANES),
            vmem(NZY, SLOT, LANES),
            vmem(NZY, SLOT, LANES),
            vmem(OWN, WIDTH, WIDTH),
            vmem(16, LANES),
            vmem(16, LANES),
            vmem(NY, 16, LANES),
            vmem(NZ, 16, LANES),
            vmem(NX, 16, LANES),
            pltpu.SemaphoreType.DMA((2,)),
            pltpu.SemaphoreType.DMA,
            pltpu.SemaphoreType.DMA((6,)),
            pltpu.SemaphoreType.DMA((6,)),
        ],
        compiler_params=pltpu.CompilerParams(
            collective_id=0, has_side_effects=True, vmem_limit_bytes=40 * 1024 * 1024
        ),
    )(pole_freq, pole_damp, samples)
    return jnp.transpose(reduced, (1, 2, 0)), system, norm_row.reshape(WIDTH)


def solution(mesh):
    placed = (P(), P(), P(None, "freq", "elem"))
    return jax.shard_map(
        per_device,
        mesh=mesh,
        in_specs=placed,
        out_specs=(P(None, None, ("elem", "freq")), P(), P()),
        check_vma=False,
    )
```

```python
import jax
import jax.numpy as jnp
from jax import lax
from jax.experimental import pallas as pl
from jax.experimental.pallas import tpu as pltpu
from jax.sharding import PartitionSpec as P

HIGH = lax.Precision.HIGHEST
MESH = pl.DeviceIdType.MESH
F32 = jnp.float32

NX, NZH, NZL, NY, NC = 4, 4, 2, 8, 2
NZ = NZH * NZL
NZY = NZL * NY
NFREQ = NZY * NC
PAIRS = 16
WIDTH = 2 * PAIRS + 1
ROWS = 40
BASIS = 48
OWN = 12
GROUP = 3
STRIDE = 40
TILES = OWN // GROUP
CHUNK = 256
CHUNKS = 4
LANES = 128
FREQ_LOCAL = 1024
ELEM_LOCAL = OWN * NFREQ
FREQ_TOTAL = FREQ_LOCAL * NFREQ
ELEM_TOTAL = ELEM_LOCAL * NX * NZH
INV_NF = 1.0 / FREQ_TOTAL


def iota(shape, dim):
    return lax.broadcasted_iota(jnp.int32, shape, dim)


def omega_of(half_position):
    return 0.02 + 0.98 * half_position / FREQ_TOTAL


def inverse_of(value):
    r = pltpu.reciprocal(value, approx=True)
    r = r * (2.0 - value * r)
    return r * (2.0 - value * r)


def split(value):
    high = value.astype(jnp.bfloat16)
    return high, (value - high.astype(F32)).astype(jnp.bfloat16)


def bf_dot(a, b):
    return jnp.dot(a, b, preferred_element_type=F32)


def pick(ref, index, shape):
    out = jnp.zeros(shape, F32)
    for m in range(PAIRS):
        out = jnp.where(index == m, ref[m], out)
    return out


def over_rows(col):
    return jnp.concatenate([col, col, jnp.zeros((8, LANES), F32)], axis=0)


def pair_coefs(ci, di, cj, dj, row_sum, col_sum):
    both = di + dj
    gap = cj - ci
    tot = ci + cj
    sq = both * both
    r1 = inverse_of(sq + gap * gap)
    r2 = inverse_of(sq + tot * tot)
    alpha, beta = both * r1, gap * r1
    gamma, delta = both * r2, -tot * r2
    ap, am = alpha + gamma, alpha - gamma
    bm, bp = beta - delta, beta + delta

    def table(di, bm, bp, row_sum, col_sum):
        ss, bd, bs, da = di * ap, di * bm, di * bp, di * am
        cr = jnp.where(row_sum, jnp.where(col_sum, ss, -bd), jnp.where(col_sum, bs, da))
        ce = jnp.where(row_sum, jnp.where(col_sum, bd, ss), jnp.where(col_sum, -da, bs))
        return cr, ce

    return table(di, bm, bp, row_sum, col_sum) + table(dj, -bp, -bm, col_sum, row_sum)


def coef_tables(c_col, d_col, pf, pd):
    shape = (ROWS, LANES)
    row, col = iota(shape, 0), iota(shape, 1)
    small = iota((8, LANES), 1) % PAIRS
    cj, dj = pick(pf, small, (8, LANES)), pick(pd, small, (8, LANES))
    tall = lambda v: jnp.concatenate([v] * (ROWS // 8), axis=0)
    inside = (row < 2 * PAIRS) & (col < 2 * PAIRS)
    cr, ce, crt, cet = pair_coefs(
        over_rows(c_col), over_rows(d_col), tall(cj), tall(dj), row < PAIRS, col < PAIRS
    )
    last_row = row == 2 * PAIRS
    last_col = col == 2 * PAIRS
    one = lambda cond: jnp.where(cond, 1.0, 0.0).astype(F32)
    cr = jnp.where(inside, cr, one(last_row & ((col < PAIRS) | last_col)))
    ce = jnp.where(inside, ce, one(last_row & (col >= PAIRS) & (col < 2 * PAIRS)))
    crt = jnp.where(inside, crt, one(last_col & (row < PAIRS)))
    cet = jnp.where(inside, cet, one(last_col & (row >= PAIRS) & (row < 2 * PAIRS)))
    return cr, ce, crt, cet


def assemble(tables, r_row, e_row, r_col, e_col):
    cr, ce, crt, cet = tables
    return cr * r_row + ce * e_row + crt * over_rows(r_col) + cet * over_rows(e_col)


def col_to_row(col):
    row, lane = iota((PAIRS, LANES), 0), iota((PAIRS, LANES), 1)
    keep = (lane % PAIRS == row) & (lane < 2 * PAIRS)
    return jnp.sum(jnp.where(keep, col, 0.0), axis=0, keepdims=True)


def row_to_col(row_vec, first):
    row, lane = iota((PAIRS, LANES), 0), iota((PAIRS, LANES), 1)
    kept = jnp.where(lane == row + first, jnp.broadcast_to(row_vec, (PAIRS, LANES)), 0.0)
    return jnp.broadcast_to(jnp.sum(kept, axis=1, keepdims=True), (PAIRS, LANES))


def rows_from(values):
    j = iota(values.shape, 1) % STRIDE
    r_row = jnp.where(
        j < PAIRS,
        values,
        jnp.where(j < 2 * PAIRS, pltpu.roll(values, PAIRS, 1), jnp.where(j == 2 * PAIRS, values, 0.0)),
    )
    e_row = jnp.where(
        j < PAIRS,
        pltpu.roll(values, LANES - PAIRS, 1),
        jnp.where(j < 2 * PAIRS, values, 0.0),
    )
    return r_row, e_row


def eliminate(work):
    parts = [work[8 * b : 8 * b + 8] for b in range(ROWS // 8)]
    sub = iota((8, LANES), 0)
    for first in range(0, WIDTH, 8):
        count = min(8, WIDTH - first)
        b0 = first // 8
        live = range(b0, len(parts))
        cols = [
            [jnp.broadcast_to(parts[b][:, first + t : first + t + 1], (8, LANES)) for b in live]
            for t in range(count)
        ]
        rows = [parts[b0][t : t + 1, :] for t in range(count)]
        for t in range(count):
            inv = inverse_of(cols[t][0][t : t + 1, :])
            factor = [v * inv for v in cols[t]]
            factor[0] = jnp.where(sub > t, factor[0], 0.0)
            for u in range(t + 1, count):
                lead = cols[u][0][t : t + 1, :]
                cols[u] = [v - f * lead for v, f in zip(cols[u], factor)]
                rows[u] = rows[u] - factor[0][u : u + 1, :] * rows[t]
            for n, b in enumerate(live):
                parts[b] = parts[b] - factor[n] * rows[t]
    return jnp.concatenate(parts, axis=0)


def kernel(
    pf_hbm, pd_hbm, s_hbm, red_hbm, sys_ref, nrm_ref,
    pf, pd, s_buf, re_buf, im_buf, xt_buf, pieces, recv_a, sum_a, recv_b,
    red_ref, buf_x, buf_y, buf_z,
    pole_sem, load_sem, out_sem, send_sem, recv_sem,
):
    elem, freq = lax.axis_index("elem"), lax.axis_index("freq")
    x, z_hi = elem // NZH, elem % NZH
    zy, core = freq // NC, freq % NC
    z_lo, y = zy // NY, zy % NY
    z = z_hi * NZL + z_lo

    def at_zy(other):
        return {"elem": elem, "freq": other * NC + core}

    def at_y(other):
        return {"elem": elem, "freq": (z_lo * NY + other) * NC + core}

    def at_z(other):
        return {
            "elem": x * NZH + other // NZL,
            "freq": ((other % NZL) * NY + y) * NC + core,
        }

    def at_x(other):
        return {"elem": (other // NC) * NZH + z_hi, "freq": zy * NC + other % NC}

    sibling = {"elem": elem, "freq": zy * NC + (1 - core)}

    pole_loads = [
        pltpu.make_async_copy(pf_hbm, pf, pole_sem.at[0]),
        pltpu.make_async_copy(pd_hbm, pd, pole_sem.at[1]),
    ]
    for load in pole_loads:
        load.start()
    loads = {}
    for k in range(CHUNKS):
        for part in range(2):
            at = pl.ds(k * CHUNK, CHUNK)
            loads[part, k] = pltpu.make_async_copy(
                s_hbm.at[part, at], s_buf.at[part, at], load_sem.at[part, k]
            )
            loads[part, k].start()

    barrier = pltpu.get_barrier_semaphore()

    def greet(device):
        pl.semaphore_signal(barrier, inc=1, device_id=device, device_id_type=MESH)

    greet(sibling)
    for step in range(1, NZY):
        greet(at_zy((zy + step) % NZY))
    for step in range(1, NZH):
        for low in range(NZL):
            greet(at_z(((z_hi + step) % NZH) * NZL + low))
    for step in range(1, NX):
        for c in range(NC):
            greet(at_x(((x + step) % NX) * NC + c))
    greeted = 1 + (NZY - 1) + (NZH - 1) * NZL + (NX - 1) * NC

    for load in pole_loads:
        load.wait()

    column = iota((PAIRS, LANES), 0)
    c_col = pick(pf, column, (PAIRS, LANES))
    d_col = pick(pd, column, (PAIRS, LANES))
    d_sq = d_col * d_col
    half8 = iota((8, LANES), 1).astype(F32) + 0.5
    half16 = iota((PAIRS, LANES), 1).astype(F32) + 0.5
    base = (freq * FREQ_LOCAL).astype(F32)
    ones = jnp.where(iota((PAIRS, FREQ_LOCAL), 0) == 0, 1.0, 0.0)
    re_buf[2 * PAIRS : BASIS, :] = ones.astype(jnp.bfloat16)
    re_buf[BASIS + 2 * PAIRS :, :] = jnp.zeros((PAIRS, FREQ_LOCAL), jnp.bfloat16)
    for tile in range(FREQ_LOCAL // LANES):
        at = pl.ds(tile * LANES, LANES)
        w = omega_of(half16 + (base + tile * LANES))
        below, above = w - c_col, w + c_col
        i1 = inverse_of(d_sq + below * below)
        i2 = inverse_of(d_sq + above * above)
        first, second = below * i1, above * i2
        re_buf[0:PAIRS, at], re_buf[BASIS : BASIS + PAIRS, at] = split(d_sq * (i1 + i2))
        re_buf[PAIRS : 2 * PAIRS, at], re_buf[BASIS + PAIRS : BASIS + 2 * PAIRS, at] = split(
            d_col * (first - second)
        )
        im_buf[0:PAIRS, at], im_buf[2 * PAIRS : 3 * PAIRS, at] = split(-d_col * (first + second))
        im_buf[PAIRS : 2 * PAIRS, at], im_buf[3 * PAIRS :, at] = split(d_sq * (i1 - i2))

    c_half = [c_col[0:8], c_col[8:16]]
    q_half = [d_sq[0:8], d_sq[8:16]]

    def mean_step(chunk, acc):
        acc = list(acc)
        start = (chunk * FREQ_LOCAL).astype(F32)
        for tile in range(FREQ_LOCAL // LANES):
            w = omega_of(half8 + (start + tile * LANES))
            for h in range(2):
                below, above = w - c_half[h], w + c_half[h]
                n1 = q_half[h] + below * below
                n2 = q_half[h] + above * above
                r = inverse_of(n1 * n2)
                acc[2 * h] = acc[2 * h] + r * (n1 + n2)
                acc[2 * h + 1] = acc[2 * h + 1] + r * (below * n2 - above * n1)
        return tuple(acc)

    acc = (jnp.zeros((8, LANES), F32),) * 4
    acc = lax.fori_loop(0, NFREQ // 2, mean_step, acc)

    x0 = jnp.zeros((BASIS, ELEM_LOCAL), F32)
    x1 = jnp.zeros((2 * PAIRS, ELEM_LOCAL), F32)
    for k in range(CHUNKS):
        at = pl.ds(k * CHUNK, CHUNK)
        loads[0, k].wait()
        high, low = split(s_buf[0, at, :])
        both = bf_dot(re_buf[:, at], high)
        x0 = x0 + (both[0:BASIS] + both[BASIS:] + bf_dot(re_buf[0:BASIS, at], low))
        loads[1, k].wait()
        high, low = split(s_buf[1, at, :])
        both = bf_dot(im_buf[:, at], high)
        x1 = x1 + (both[0 : 2 * PAIRS] + both[2 * PAIRS :] + bf_dot(im_buf[0 : 2 * PAIRS, at], low))

    stacked = jnp.concatenate(
        [
            x0,
            jnp.zeros((64 - BASIS, ELEM_LOCAL), F32),
            x1,
            jnp.zeros((LANES - 64 - 2 * PAIRS, ELEM_LOCAL), F32),
        ],
        axis=0,
    )
    for tile in range(ELEM_LOCAL // LANES):
        at = slice(tile * LANES, (tile + 1) * LANES)
        xt_buf[at, :] = stacked[:, at].T
    count = ELEM_LOCAL // GROUP
    thirds = [xt_buf[pl.ds(q, count, stride=GROUP), :] for q in range(GROUP)]
    lane_c = iota((count, LANES), 1)

    def spread(shift):
        rolled = [
            pltpu.roll(thirds[q], (STRIDE * q + shift) % LANES, 1) if (STRIDE * q + shift) % LANES else thirds[q]
            for q in range(GROUP)
        ]
        return jnp.where(
            lane_c < STRIDE, rolled[0], jnp.where(lane_c < 2 * STRIDE, rolled[1], rolled[2])
        )

    part0, part1 = spread(0), spread(64)
    upper = iota((8, LANES), 0) < 4
    for k in range(NZY):
        v0, v1 = part0[8 * k : 8 * k + 8], part1[8 * k : 8 * k + 8]
        pieces[0, k] = jnp.where(upper, v0, pltpu.roll(v1, 4, 0))
        pieces[1, k] = jnp.where(upper, pltpu.roll(v0, 4, 0), v1)

    pl.semaphore_wait(barrier, greeted)

    copy_a = pltpu.make_async_remote_copy(
        src_ref=pieces.at[1 - core],
        dst_ref=recv_a,
        send_sem=send_sem.at[0],
        recv_sem=recv_sem.at[0],
        device_id=sibling,
        device_id_type=MESH,
    )
    copy_a.start()

    acc = lax.fori_loop(NFREQ // 2, NFREQ, mean_step, acc)

    def lane_sum(v):
        return jnp.broadcast_to(jnp.sum(v, axis=1, keepdims=True), v.shape)

    mean_r = d_sq * lane_sum(jnp.concatenate([acc[0], acc[2]], axis=0)) * INV_NF
    mean_e = d_col * lane_sum(jnp.concatenate([acc[1], acc[3]], axis=0)) * INV_NF
    tables = coef_tables(c_col, d_col, pf, pd)

    copy_a.wait_recv()
    for k in range(NZY):
        sum_a[k] = pieces[core, k] + recv_a[k]

    for step in range(1, NZY):
        other = (zy + step) % NZY
        pltpu.make_async_remote_copy(
            src_ref=sum_a.at[other],
            dst_ref=recv_b.at[zy],
            send_sem=send_sem.at[1],
            recv_sem=recv_sem.at[1],
            device_id=at_zy(other),
            device_id_type=MESH,
        ).start()
    recv_b[zy] = sum_a[zy]

    lane1 = iota((1, LANES), 1)
    mean_r_row, mean_e_row = col_to_row(mean_r), col_to_row(mean_e)
    gram = assemble(
        tables,
        jnp.where(lane1 == 2 * PAIRS, 1.0, mean_r_row),
        mean_e_row,
        mean_r,
        mean_e,
    )
    row, lane = iota((ROWS, LANES), 0), iota((ROWS, LANES), 1)
    work = gram + jnp.where((lane == row + 64) & (row < WIDTH), 1.0, 0.0)
    work = eliminate(work)
    pivots = jnp.sum(jnp.where((lane == row) & (row < WIDTH), work, 0.0), axis=1, keepdims=True)
    pivots = jnp.where(iota((ROWS, 1), 0) < WIDTH, pivots, 1.0)
    inverse = pltpu.roll(work, 64, 1) * (1.0 / jnp.sqrt(pivots))
    inverse = jnp.where(lane < WIDTH, inverse, 0.0)

    power = jnp.zeros((FREQ_LOCAL, LANES), F32)
    for tile in range(ELEM_LOCAL // LANES):
        at = pl.ds(tile * LANES, LANES)
        a, b = s_buf[0, :, at], s_buf[1, :, at]
        power = power + (a * a + b * b)
    high, low = split(power)
    both = bf_dot(re_buf[...], high)
    q = (both[0:BASIS] + both[BASIS:] + bf_dot(re_buf[0:BASIS, :], low))[0:ROWS]
    q = jnp.broadcast_to(jnp.sum(q, axis=1, keepdims=True), (ROWS, LANES))
    q_row = jnp.sum(jnp.where(lane == row, q, 0.0), axis=0, keepdims=True)

    triple = [
        v + pltpu.roll(v, STRIDE, 1) + pltpu.roll(v, 2 * STRIDE, 1) for v in tables
    ]

    rest_b = recv_b.at[pl.ds(0, NZY - 1)]
    pltpu.make_async_copy(rest_b, rest_b, recv_sem.at[1]).wait()
    owned = recv_b[0]
    for k in range(1, NZY):
        owned = owned + recv_b[k]
    owned = owned * (-INV_NF)

    other_part = pltpu.roll(owned, 4, 0)
    plus, minus = owned + other_part, owned - other_part
    r_rows, e_rows = rows_from(minus)
    plus_t = jnp.concatenate([plus, jnp.zeros((LANES - 8, LANES), F32)], axis=0).T
    lane16 = iota((PAIRS, LANES), 1)

    def columns(g, first):
        spread_col = [
            jnp.broadcast_to(
                plus_t[STRIDE * q + first : STRIDE * q + first + PAIRS, g : g + 1], (PAIRS, LANES)
            )
            for q in range(GROUP)
        ]
        return jnp.where(
            lane16 < STRIDE, spread_col[0], jnp.where(lane16 < 2 * STRIDE, spread_col[1], spread_col[2])
        )

    coupling = jnp.concatenate(
        [
            assemble(triple, r_rows[g : g + 1, :], e_rows[g : g + 1, :], columns(g, 0), columns(g, PAIRS))
            for g in range(TILES)
        ],
        axis=1,
    )
    reduced = jnp.dot(
        inverse[:, 0:ROWS], coupling, precision=HIGH, preferred_element_type=F32
    )
    parts = [reduced[:, g * LANES : (g + 1) * LANES] for g in range(TILES)]
    tall = jnp.concatenate(parts, axis=0)
    wide = lax.dot_general(
        tall, tall, (((0,), (0,)), ((), ())), precision=HIGH, preferred_element_type=F32
    )
    corr = wide[0:ROWS]
    for q in range(1, GROUP):
        at = STRIDE * q
        corr = corr + pltpu.roll(wide[at : at + ROWS], LANES - at, 1)

    sub8, ln8 = iota((8, LANES), 0), iota((8, LANES), 1)
    spread8 = lambda v: jnp.broadcast_to(v, (8, LANES))
    border = jnp.where(
        sub8 == 0, spread8(corr[32:33]), jnp.where(sub8 == 1, spread8(q_row), 0.0)
    )
    packed = pltpu.roll(border, 80, 1)
    for g, first, shift in ((3, 80, 48), (2, 72, 40), (1, 56, 24)):
        packed = jnp.where(ln8 < first, pltpu.roll(corr[8 * g : 8 * g + 8], shift, 1), packed)
    total = jnp.where(ln8 < 32, corr[0:8], packed)

    def send(buf, count, me, place, index, value):
        buf[me] = value
        for step in range(1, count):
            pltpu.make_async_remote_copy(
                src_ref=buf.at[me],
                dst_ref=buf.at[me],
                send_sem=send_sem.at[index],
                recv_sem=recv_sem.at[index],
                device_id=place((me + step) % count),
                device_id_type=MESH,
            ).start()

    def receive(buf, count, index):
        rest = buf.at[pl.ds(0, count - 1)]
        pltpu.make_async_copy(rest, rest, recv_sem.at[index]).wait()
        total = buf[0]
        for k in range(1, count):
            total = total + buf[k]
        return total

    send(buf_x, NX * NC, x * NC + core, at_x, 2, total)

    for g in range(TILES):
        for q in range(GROUP):
            block = pltpu.roll(parts[g], LANES - STRIDE * q, 1) if q else parts[g]
            red_ref[GROUP * g + q] = block[0:WIDTH, 0:WIDTH]
    out = pltpu.make_async_copy(red_ref, red_hbm, out_sem)
    out.start()

    total = receive(buf_x, NX * NC, 2)
    send(buf_y, NY, y, at_y, 3, total)
    total = receive(buf_y, NY, 3)
    send(buf_z, NZ, z, at_z, 4, total)
    mean_row = jnp.where(
        lane1 < PAIRS,
        mean_r_row,
        jnp.where(lane1 < 2 * PAIRS, mean_e_row, 1.0),
    )
    total = receive(buf_z, NZ, 4)

    border = pltpu.roll(total, LANES - 80, 1)
    moments = jnp.where(lane1 < WIDTH, border[1:2], 0.0) * INV_NF
    mean_sq = moments[:, 2 * PAIRS : 2 * PAIRS + 1]
    r_row, e_row = rows_from(moments)
    data_gram = assemble(
        tables, r_row, e_row, row_to_col(moments, 0), row_to_col(moments, PAIRS)
    )
    half = jnp.concatenate(
        [total]
        + [pltpu.roll(total, LANES - shift, 1) for shift in (24, 40, 48)]
        + [spread8(border[0:1])],
        axis=0,
    )
    square = jnp.concatenate([half, jnp.zeros((LANES - ROWS, LANES), F32)], axis=0)
    stored = ((lane < 2 * PAIRS) & (lane // 8 >= row // 8)) | (row >= 2 * PAIRS)
    correction = jnp.where(stored, half, square.T[0:ROWS])
    system = (data_gram - correction) / mean_sq
    sys_ref[...] = system[0:WIDTH, 0:WIDTH]
    nrm_ref[...] = (mean_row * jnp.sqrt(mean_sq * (1.0 / ELEM_TOTAL)))[:, 0:WIDTH]

    out.wait()
    copy_a.wait_send()
    rest = sum_a.at[pl.ds(0, NZY - 1)]
    pltpu.make_async_copy(rest, rest, send_sem.at[1]).wait()
    for buf, count, index in ((buf_x, NX * NC, 2), (buf_y, NY, 3), (buf_z, NZ, 4)):
        rest = buf.at[pl.ds(0, count - 1)]
        pltpu.make_async_copy(rest, rest, send_sem.at[index]).wait()


def per_device(pole_freq, pole_damp, samples):
    vmem = lambda *shape: pltpu.VMEM(shape, F32)
    half = lambda *shape: pltpu.VMEM(shape, jnp.bfloat16)
    reduced, system, norm_row = pl.pallas_call(
        kernel,
        out_shape=(
            jax.ShapeDtypeStruct((OWN, WIDTH, WIDTH), F32),
            jax.ShapeDtypeStruct((WIDTH, WIDTH), F32),
            jax.ShapeDtypeStruct((1, WIDTH), F32),
        ),
        in_specs=[pl.BlockSpec(memory_space=pltpu.HBM)] * 3,
        out_specs=(
            pl.BlockSpec(memory_space=pltpu.HBM),
            pl.BlockSpec(memory_space=pltpu.VMEM),
            pl.BlockSpec(memory_space=pltpu.VMEM),
        ),
        scratch_shapes=[
            pltpu.SMEM((PAIRS,), F32),
            pltpu.SMEM((PAIRS,), F32),
            vmem(2, FREQ_LOCAL, ELEM_LOCAL),
            half(2 * BASIS, FREQ_LOCAL),
            half(4 * PAIRS, FREQ_LOCAL),
            vmem(ELEM_LOCAL, LANES),
            vmem(NC, NZY, 8, LANES),
            vmem(NZY, 8, LANES),
            vmem(NZY, 8, LANES),
            vmem(NZY, 8, LANES),
            vmem(OWN, WIDTH, WIDTH),
            vmem(NX * NC, 8, LANES),
            vmem(NY, 8, LANES),
            vmem(NZ, 8, LANES),
            pltpu.SemaphoreType.DMA((2,)),
            pltpu.SemaphoreType.DMA((2, CHUNKS)),
            pltpu.SemaphoreType.DMA,
            pltpu.SemaphoreType.DMA((5,)),
            pltpu.SemaphoreType.DMA((5,)),
        ],
        compiler_params=pltpu.CompilerParams(
            collective_id=0, has_side_effects=True, vmem_limit_bytes=60 * 1024 * 1024
        ),
    )(pole_freq, pole_damp, samples)
    return jnp.transpose(reduced, (1, 2, 0)), system, norm_row.reshape(WIDTH)


def solution(mesh):
    placed = (P(), P(), P(None, "freq", "elem"))
    return jax.shard_map(
        per_device,
        mesh=mesh,
        in_specs=placed,
        out_specs=(P(None, None, ("elem", "freq")), P(), P()),
        check_vma=False,
    )
```

```python
import jax
import jax.numpy as jnp
from jax import lax
from jax.experimental import pallas as pl
from jax.experimental.pallas import tpu as pltpu
from jax.sharding import PartitionSpec as P

HIGH = lax.Precision.HIGHEST
MESH = pl.DeviceIdType.MESH
F32 = jnp.float32

NX, NZH, NZL, NY, NC = 4, 4, 2, 8, 2
NZ = NZH * NZL
NZY = NZL * NY
NFREQ = NZY * NC
PAIRS = 16
WIDTH = 2 * PAIRS + 1
ROWS = 40
BASIS = 48
OWN = 12
GROUP = 3
STRIDE = 40
TILES = OWN // GROUP
CHUNK = 256
CHUNKS = 4
LANES = 128
FREQ_LOCAL = 1024
ELEM_LOCAL = OWN * NFREQ
FREQ_TOTAL = FREQ_LOCAL * NFREQ
ELEM_TOTAL = ELEM_LOCAL * NX * NZH
INV_NF = 1.0 / FREQ_TOTAL


def iota(shape, dim):
    return lax.broadcasted_iota(jnp.int32, shape, dim)


def omega_of(half_position):
    return 0.02 + 0.98 * half_position / FREQ_TOTAL


def inverse_of(value):
    r = pltpu.reciprocal(value, approx=True)
    r = r * (2.0 - value * r)
    return r * (2.0 - value * r)


def split(value):
    high = value.astype(jnp.bfloat16)
    return high, (value - high.astype(F32)).astype(jnp.bfloat16)


def bf_dot(a, b):
    return jnp.dot(a, b, preferred_element_type=F32)


def wrap(value, size):
    return jnp.where(value >= size, value - size, value)


def tree_sum(values):
    values = list(values)
    while len(values) > 1:
        values = [a + b for a, b in zip(values[::2], values[1::2])] + values[len(values) & ~1 :]
    return values[0]


def pick(ref, index, shape):
    out = jnp.zeros(shape, F32)
    for m in range(PAIRS):
        out = jnp.where(index == m, ref[m], out)
    return out


def over_rows(col):
    return jnp.concatenate([col, col, jnp.zeros((8, LANES), F32)], axis=0)


def pair_coefs(ci, di, cj, dj, row_sum, col_sum):
    both = di + dj
    gap = cj - ci
    tot = ci + cj
    sq = both * both
    r1 = inverse_of(sq + gap * gap)
    r2 = inverse_of(sq + tot * tot)
    alpha, beta = both * r1, gap * r1
    gamma, delta = both * r2, -tot * r2
    ap, am = alpha + gamma, alpha - gamma
    bm, bp = beta - delta, beta + delta

    def table(di, bm, bp, row_sum, col_sum):
        ss, bd, bs, da = di * ap, di * bm, di * bp, di * am
        cr = jnp.where(row_sum, jnp.where(col_sum, ss, -bd), jnp.where(col_sum, bs, da))
        ce = jnp.where(row_sum, jnp.where(col_sum, bd, ss), jnp.where(col_sum, -da, bs))
        return cr, ce

    return table(di, bm, bp, row_sum, col_sum) + table(dj, -bp, -bm, col_sum, row_sum)


def coef_tables(c_col, d_col, pf, pd):
    shape = (ROWS, LANES)
    row, col = iota(shape, 0), iota(shape, 1)
    small = iota((8, LANES), 1) & (PAIRS - 1)
    cj, dj = pick(pf, small, (8, LANES)), pick(pd, small, (8, LANES))
    tall = lambda v: jnp.concatenate([v] * (ROWS // 8), axis=0)
    inside = (row < 2 * PAIRS) & (col < 2 * PAIRS)
    cr, ce, crt, cet = pair_coefs(
        over_rows(c_col), over_rows(d_col), tall(cj), tall(dj), row < PAIRS, col < PAIRS
    )
    last_row = row == 2 * PAIRS
    last_col = col == 2 * PAIRS
    one = lambda cond: jnp.where(cond, 1.0, 0.0).astype(F32)
    cr = jnp.where(inside, cr, one(last_row & ((col < PAIRS) | last_col)))
    ce = jnp.where(inside, ce, one(last_row & (col >= PAIRS) & (col < 2 * PAIRS)))
    crt = jnp.where(inside, crt, one(last_col & (row < PAIRS)))
    cet = jnp.where(inside, cet, one(last_col & (row >= PAIRS) & (row < 2 * PAIRS)))
    return cr, ce, crt, cet


def assemble(tables, r_row, e_row, r_col, e_col):
    cr, ce, crt, cet = tables
    return cr * r_row + ce * e_row + crt * over_rows(r_col) + cet * over_rows(e_col)


def col_to_row(col):
    row, lane = iota((PAIRS, LANES), 0), iota((PAIRS, LANES), 1)
    keep = ((lane & (PAIRS - 1)) == row) & (lane < 2 * PAIRS)
    return jnp.sum(jnp.where(keep, col, 0.0), axis=0, keepdims=True)


def row_to_col(row_vec, first):
    row, lane = iota((PAIRS, LANES), 0), iota((PAIRS, LANES), 1)
    kept = jnp.where(lane == row + first, jnp.broadcast_to(row_vec, (PAIRS, LANES)), 0.0)
    return jnp.broadcast_to(jnp.sum(kept, axis=1, keepdims=True), (PAIRS, LANES))


def rows_from(values):
    lane = iota(values.shape, 1)
    j = lane - jnp.where(lane >= 2 * STRIDE, 2 * STRIDE, jnp.where(lane >= STRIDE, STRIDE, 0))
    r_row = jnp.where(
        j < PAIRS,
        values,
        jnp.where(j < 2 * PAIRS, pltpu.roll(values, PAIRS, 1), jnp.where(j == 2 * PAIRS, values, 0.0)),
    )
    e_row = jnp.where(
        j < PAIRS,
        pltpu.roll(values, LANES - PAIRS, 1),
        jnp.where(j < 2 * PAIRS, values, 0.0),
    )
    return r_row, e_row


def eliminate(work):
    parts = [work[8 * b : 8 * b + 8] for b in range(ROWS // 8)]
    sub = iota((8, LANES), 0)
    for first in range(0, WIDTH, 8):
        count = min(8, WIDTH - first)
        b0 = first // 8
        live = range(b0, len(parts))
        cols = [
            [jnp.broadcast_to(parts[b][:, first + t : first + t + 1], (8, LANES)) for b in live]
            for t in range(count)
        ]
        rows = [parts[b0][t : t + 1, :] for t in range(count)]
        for t in range(count):
            inv = inverse_of(cols[t][0][t : t + 1, :])
            factor = [v * inv for v in cols[t]]
            factor[0] = jnp.where(sub > t, factor[0], 0.0)
            for u in range(t + 1, count):
                lead = cols[u][0][t : t + 1, :]
                cols[u] = [v - f * lead for v, f in zip(cols[u], factor)]
                rows[u] = rows[u] - factor[0][u : u + 1, :] * rows[t]
            for n, b in enumerate(live):
                parts[b] = parts[b] - factor[n] * rows[t]
    return jnp.concatenate(parts, axis=0)


def kernel(
    pf_hbm, pd_hbm, s_hbm, red_hbm, sys_ref, nrm_ref,
    pf, pd, s_buf, re_buf, im_buf, xt_buf, pieces, recv_b,
    red_ref, buf_x, buf_y, buf_z,
    pole_sem, load_sem, out_sem, send_sem, recv_sem,
):
    elem, freq = lax.axis_index("elem"), lax.axis_index("freq")
    x, z_hi = elem // NZH, elem % NZH
    zy, core = freq // NC, freq % NC
    z_lo, y = zy // NY, zy % NY
    z = z_hi * NZL + z_lo

    def at_freq(other):
        return {"elem": elem, "freq": other}

    def at_y(other):
        return {"elem": elem, "freq": (z_lo * NY + other) * NC + core}

    z_peers = []
    for dz in range(NZH):
        for low in range(NZL):
            if dz or low:
                hi, lo = wrap(z_hi + dz, NZH), wrap(z_lo + low, NZL)
                z_peers.append({"elem": x * NZH + hi, "freq": (lo * NY + y) * NC + core})
    x_peers = []
    for dx in range(NX):
        for c in range(NC):
            if dx or c:
                to = wrap(x + dx, NX)
                x_peers.append({"elem": to * NZH + z_hi, "freq": zy * NC + wrap(core + c, NC)})
    y_peers = [at_y(wrap(y + dy, NY)) for dy in range(1, NY)]

    pole_loads = [
        pltpu.make_async_copy(pf_hbm, pf, pole_sem.at[0]),
        pltpu.make_async_copy(pd_hbm, pd, pole_sem.at[1]),
    ]
    for load in pole_loads:
        load.start()
    loads = {}
    for k in range(CHUNKS):
        for part in range(2):
            at = pl.ds(k * CHUNK, CHUNK)
            loads[part, k] = pltpu.make_async_copy(
                s_hbm.at[part, at], s_buf.at[part, at], load_sem.at[part, k]
            )
            loads[part, k].start()

    barrier = pltpu.get_barrier_semaphore()

    def greet(device):
        pl.semaphore_signal(barrier, inc=1, device_id=device, device_id_type=MESH)

    for step in range(1, NFREQ):
        greet(at_freq(wrap(freq + step, NFREQ)))
    for device in z_peers[NZL - 1 :] + x_peers[NC - 1 :]:
        greet(device)
    greeted = NFREQ - 1 + len(z_peers) - (NZL - 1) + len(x_peers) - (NC - 1)

    for load in pole_loads:
        load.wait()

    column = iota((PAIRS, LANES), 0)
    c_col = pick(pf, column, (PAIRS, LANES))
    d_col = pick(pd, column, (PAIRS, LANES))
    d_sq = d_col * d_col
    half8 = iota((8, LANES), 1).astype(F32) + 0.5
    half16 = iota((PAIRS, LANES), 1).astype(F32) + 0.5
    base = (freq * FREQ_LOCAL).astype(F32)
    ones = jnp.where(iota((PAIRS, FREQ_LOCAL), 0) == 0, 1.0, 0.0)
    re_buf[2 * PAIRS : BASIS, :] = ones.astype(jnp.bfloat16)
    re_buf[BASIS + 2 * PAIRS :, :] = jnp.zeros((PAIRS, FREQ_LOCAL), jnp.bfloat16)
    for tile in range(FREQ_LOCAL // LANES):
        at = pl.ds(tile * LANES, LANES)
        w = omega_of(half16 + (base + tile * LANES))
        below, above = w - c_col, w + c_col
        i1 = inverse_of(d_sq + below * below)
        i2 = inverse_of(d_sq + above * above)
        first, second = below * i1, above * i2
        re_buf[0:PAIRS, at], re_buf[BASIS : BASIS + PAIRS, at] = split(d_sq * (i1 + i2))
        re_buf[PAIRS : 2 * PAIRS, at], re_buf[BASIS + PAIRS : BASIS + 2 * PAIRS, at] = split(
            d_col * (first - second)
        )
        im_buf[0:PAIRS, at], im_buf[2 * PAIRS : 3 * PAIRS, at] = split(-d_col * (first + second))
        im_buf[PAIRS : 2 * PAIRS, at], im_buf[3 * PAIRS :, at] = split(d_sq * (i1 - i2))

    c_half = [c_col[0:8], c_col[8:16]]
    q_half = [d_sq[0:8], d_sq[8:16]]

    def mean_step(chunk, acc):
        acc = list(acc)
        start = (chunk * FREQ_LOCAL).astype(F32)
        for tile in range(FREQ_LOCAL // LANES):
            w = omega_of(half8 + (start + tile * LANES))
            for h in range(2):
                below, above = w - c_half[h], w + c_half[h]
                n1 = q_half[h] + below * below
                n2 = q_half[h] + above * above
                r = inverse_of(n1 * n2)
                acc[2 * h] = acc[2 * h] + r * (n1 + n2)
                acc[2 * h + 1] = acc[2 * h + 1] + r * (below * n2 - above * n1)
        return tuple(acc)

    acc = (jnp.zeros((8, LANES), F32),) * 4
    acc = lax.fori_loop(0, NFREQ // 2, mean_step, acc)

    x0 = jnp.zeros((BASIS, ELEM_LOCAL + LANES), F32)
    x1 = jnp.zeros((2 * PAIRS, ELEM_LOCAL), F32)
    for k in range(CHUNKS):
        at = pl.ds(k * CHUNK, CHUNK)
        loads[0, k].wait()
        loads[1, k].wait()
        s0, s1 = s_buf[0, at, :], s_buf[1, at, :]
        squares = s0 * s0 + s1 * s1
        power = tree_sum(squares[:, t * LANES : (t + 1) * LANES] for t in range(ELEM_LOCAL // LANES))
        high, low = split(jnp.concatenate([s0, power], axis=1))
        both = bf_dot(re_buf[:, at], high)
        x0 = x0 + (both[0:BASIS] + both[BASIS:] + bf_dot(re_buf[0:BASIS, at], low))
        high, low = split(s1)
        both = bf_dot(im_buf[:, at], high)
        x1 = x1 + (both[0 : 2 * PAIRS] + both[2 * PAIRS :] + bf_dot(im_buf[0 : 2 * PAIRS, at], low))
    x0, q = x0[:, 0:ELEM_LOCAL], x0[0:ROWS, ELEM_LOCAL:]

    stacked = jnp.concatenate(
        [
            x0,
            jnp.zeros((64 - BASIS, ELEM_LOCAL), F32),
            x1,
            jnp.zeros((LANES - 64 - 2 * PAIRS, ELEM_LOCAL), F32),
        ],
        axis=0,
    )
    for tile in range(ELEM_LOCAL // LANES):
        at = slice(tile * LANES, (tile + 1) * LANES)
        xt_buf[at, :] = stacked[:, at].T
    count = ELEM_LOCAL // GROUP
    thirds = [xt_buf[pl.ds(q, count, stride=GROUP), :] for q in range(GROUP)]
    lane_c = iota((count, LANES), 1)

    def spread(shift):
        rolled = [
            pltpu.roll(thirds[q], (STRIDE * q + shift) % LANES, 1) if (STRIDE * q + shift) % LANES else thirds[q]
            for q in range(GROUP)
        ]
        return jnp.where(
            lane_c < STRIDE, rolled[0], jnp.where(lane_c < 2 * STRIDE, rolled[1], rolled[2])
        )

    part0, part1 = spread(0), spread(64)
    upper = iota((8, LANES), 0) < 4
    for k in range(NZY):
        v0, v1 = part0[8 * k : 8 * k + 8], part1[8 * k : 8 * k + 8]
        pieces[NC * k] = jnp.where(upper, v0, pltpu.roll(v1, 4, 0))
        pieces[NC * k + 1] = jnp.where(upper, pltpu.roll(v0, 4, 0), v1)

    pl.semaphore_wait(barrier, greeted)

    for step in range(1, NFREQ):
        other = wrap(freq + step, NFREQ)
        pltpu.make_async_remote_copy(
            src_ref=pieces.at[other],
            dst_ref=recv_b.at[freq],
            send_sem=send_sem.at[0],
            recv_sem=recv_sem.at[0],
            device_id=at_freq(other),
            device_id_type=MESH,
        ).start()
    recv_b[freq] = pieces[freq]

    acc = lax.fori_loop(NFREQ // 2, NFREQ, mean_step, acc)

    def lane_sum(v):
        return jnp.broadcast_to(jnp.sum(v, axis=1, keepdims=True), v.shape)

    mean_r = d_sq * lane_sum(jnp.concatenate([acc[0], acc[2]], axis=0)) * INV_NF
    mean_e = d_col * lane_sum(jnp.concatenate([acc[1], acc[3]], axis=0)) * INV_NF
    tables = coef_tables(c_col, d_col, pf, pd)

    lane1 = iota((1, LANES), 1)
    mean_r_row, mean_e_row = col_to_row(mean_r), col_to_row(mean_e)
    gram = assemble(
        tables,
        jnp.where(lane1 == 2 * PAIRS, 1.0, mean_r_row),
        mean_e_row,
        mean_r,
        mean_e,
    )
    row, lane = iota((ROWS, LANES), 0), iota((ROWS, LANES), 1)
    work = gram + jnp.where((lane == row + 64) & (row < WIDTH), 1.0, 0.0)
    work = eliminate(work)
    pivots = jnp.sum(jnp.where((lane == row) & (row < WIDTH), work, 0.0), axis=1, keepdims=True)
    pivots = jnp.where(iota((ROWS, 1), 0) < WIDTH, pivots, 1.0)
    inverse = pltpu.roll(work, 64, 1) * (1.0 / jnp.sqrt(pivots))
    inverse = jnp.where(lane < WIDTH, inverse, 0.0)
    inverse = jnp.concatenate([inverse, jnp.zeros((BASIS - ROWS, LANES), F32)], axis=0)[:, 0:BASIS]
    inv_high, inv_low = split(inverse)
    inv_both = jnp.concatenate([inv_high, inv_low], axis=0)

    q = jnp.broadcast_to(jnp.sum(q, axis=1, keepdims=True), (ROWS, LANES))
    q_row = jnp.sum(jnp.where(lane == row, q, 0.0), axis=0, keepdims=True)

    triple = [
        v + pltpu.roll(v, STRIDE, 1) + pltpu.roll(v, 2 * STRIDE, 1) for v in tables
    ]

    rest_b = recv_b.at[pl.ds(0, NFREQ - 1)]
    pltpu.make_async_copy(rest_b, rest_b, recv_sem.at[0]).wait()
    owned = tree_sum(recv_b[k] for k in range(NFREQ))
    owned = owned * (-INV_NF)

    other_part = pltpu.roll(owned, 4, 0)
    plus, minus = owned + other_part, owned - other_part
    r_rows, e_rows = rows_from(minus)
    plus_t = jnp.concatenate([plus, jnp.zeros((LANES - 8, LANES), F32)], axis=0).T
    lane16 = iota((PAIRS, LANES), 1)

    def columns(g, first):
        spread_col = [
            jnp.broadcast_to(
                plus_t[STRIDE * q + first : STRIDE * q + first + PAIRS, g : g + 1], (PAIRS, LANES)
            )
            for q in range(GROUP)
        ]
        return jnp.where(
            lane16 < STRIDE, spread_col[0], jnp.where(lane16 < 2 * STRIDE, spread_col[1], spread_col[2])
        )

    coupling = jnp.concatenate(
        [
            assemble(triple, r_rows[g : g + 1, :], e_rows[g : g + 1, :], columns(g, 0), columns(g, PAIRS))
            for g in range(TILES)
        ],
        axis=1,
    )
    coupling = jnp.concatenate([coupling, jnp.zeros((BASIS - ROWS, TILES * LANES), F32)], axis=0)
    high, low = split(coupling)
    both = bf_dot(inv_both, high)
    reduced = (both[0:BASIS] + both[BASIS:] + bf_dot(inv_high, low))[0:ROWS]
    parts = [reduced[:, g * LANES : (g + 1) * LANES] for g in range(TILES)]
    tall = jnp.concatenate(parts, axis=0)
    high, low = split(tall)
    flipped = jnp.concatenate(split(tall.T), axis=0)
    wide = bf_dot(flipped, jnp.concatenate([high, low], axis=1))
    wide = wide[0:LANES, 0:LANES] + (wide[0:LANES, LANES:] + wide[LANES:, 0:LANES])
    corr = wide[0:ROWS]
    for q in range(1, GROUP):
        at = STRIDE * q
        corr = corr + pltpu.roll(wide[at : at + ROWS], LANES - at, 1)

    sub8, ln8 = iota((8, LANES), 0), iota((8, LANES), 1)
    spread8 = lambda v: jnp.broadcast_to(v, (8, LANES))
    border = jnp.where(
        sub8 == 0, spread8(corr[32:33]), jnp.where(sub8 == 1, spread8(q_row), 0.0)
    )
    packed = pltpu.roll(border, 80, 1)
    for g, first, shift in ((3, 80, 48), (2, 72, 40), (1, 56, 24)):
        packed = jnp.where(ln8 < first, pltpu.roll(corr[8 * g : 8 * g + 8], shift, 1), packed)
    total = jnp.where(ln8 < 32, corr[0:8], packed)

    def send(buf, me, peers, index, value):
        buf[me] = value
        for device in peers:
            pltpu.make_async_remote_copy(
                src_ref=buf.at[me],
                dst_ref=buf.at[me],
                send_sem=send_sem.at[index],
                recv_sem=recv_sem.at[index],
                device_id=device,
                device_id_type=MESH,
            ).start()

    def receive(buf, count, index):
        rest = buf.at[pl.ds(0, count - 1)]
        pltpu.make_async_copy(rest, rest, recv_sem.at[index]).wait()
        return tree_sum(buf[k] for k in range(count))

    send(buf_x, x * NC + core, x_peers, 1, total)

    for g in range(TILES):
        for q in range(GROUP):
            block = pltpu.roll(parts[g], LANES - STRIDE * q, 1) if q else parts[g]
            red_ref[GROUP * g + q] = block[0:WIDTH, 0:WIDTH]
    out = pltpu.make_async_copy(red_ref, red_hbm, out_sem)
    out.start()

    total = receive(buf_x, NX * NC, 1)
    send(buf_y, y, y_peers, 2, total)
    total = receive(buf_y, NY, 2)
    send(buf_z, z, z_peers, 3, total)
    mean_row = jnp.where(
        lane1 < PAIRS,
        mean_r_row,
        jnp.where(lane1 < 2 * PAIRS, mean_e_row, 1.0),
    )
    total = receive(buf_z, NZ, 3)

    border = pltpu.roll(total, LANES - 80, 1)
    moments = jnp.where(lane1 < WIDTH, border[1:2], 0.0) * INV_NF
    mean_sq = moments[:, 2 * PAIRS : 2 * PAIRS + 1]
    r_row, e_row = rows_from(moments)
    data_gram = assemble(
        tables, r_row, e_row, row_to_col(moments, 0), row_to_col(moments, PAIRS)
    )
    half = jnp.concatenate(
        [total]
        + [pltpu.roll(total, LANES - shift, 1) for shift in (24, 40, 48)]
        + [spread8(border[0:1])],
        axis=0,
    )
    square = jnp.concatenate([half, jnp.zeros((LANES - ROWS, LANES), F32)], axis=0)
    stored = ((lane < 2 * PAIRS) & (lane >= (row & ~7))) | (row >= 2 * PAIRS)
    correction = jnp.where(stored, half, square.T[0:ROWS])
    system = (data_gram - correction) * (1.0 / mean_sq)
    sys_ref[...] = system[0:WIDTH, 0:WIDTH]
    nrm_ref[...] = (mean_row * jnp.sqrt(mean_sq * (1.0 / ELEM_TOTAL)))[:, 0:WIDTH]

    out.wait()
    for buf, count, index in (
        (pieces, NFREQ, 0), (buf_x, NX * NC, 1), (buf_y, NY, 2), (buf_z, NZ, 3)
    ):
        rest = buf.at[pl.ds(0, count - 1)]
        pltpu.make_async_copy(rest, rest, send_sem.at[index]).wait()


def writer(*refs):
    count = len(refs) // 2
    sems = refs[-1]
    copies = [
        pltpu.make_async_copy(refs[k], refs[count + k], sems.at[k]) for k in range(count)
    ]
    for copy in copies:
        copy.start()
    for copy in copies:
        copy.wait()


def per_device(pole_freq, pole_damp, samples):
    vmem = lambda *shape: pltpu.VMEM(shape, F32)
    half = lambda *shape: pltpu.VMEM(shape, jnp.bfloat16)
    results = (
        jax.ShapeDtypeStruct((OWN, WIDTH, WIDTH), F32),
        jax.ShapeDtypeStruct((WIDTH, WIDTH), F32),
        jax.ShapeDtypeStruct((1, WIDTH), F32),
    )
    reduced, system, norm_row = pl.pallas_call(
        kernel,
        out_shape=results,
        in_specs=[pl.BlockSpec(memory_space=pltpu.HBM)] * 3,
        out_specs=(
            pl.BlockSpec(memory_space=pltpu.HBM),
            pl.BlockSpec(memory_space=pltpu.VMEM),
            pl.BlockSpec(memory_space=pltpu.VMEM),
        ),
        scratch_shapes=[
            pltpu.SMEM((PAIRS,), F32),
            pltpu.SMEM((PAIRS,), F32),
            vmem(2, FREQ_LOCAL, ELEM_LOCAL),
            half(2 * BASIS, FREQ_LOCAL),
            half(4 * PAIRS, FREQ_LOCAL),
            vmem(ELEM_LOCAL, LANES),
            vmem(NFREQ, 8, LANES),
            vmem(NFREQ, 8, LANES),
            vmem(OWN, WIDTH, WIDTH),
            vmem(NX * NC, 8, LANES),
            vmem(NY, 8, LANES),
            vmem(NZ, 8, LANES),
            pltpu.SemaphoreType.DMA((2,)),
            pltpu.SemaphoreType.DMA((2, CHUNKS)),
            pltpu.SemaphoreType.DMA,
            pltpu.SemaphoreType.DMA((4,)),
            pltpu.SemaphoreType.DMA((4,)),
        ],
        compiler_params=pltpu.CompilerParams(
            collective_id=0, has_side_effects=True, vmem_limit_bytes=60 * 1024 * 1024
        ),
    )(pole_freq, pole_damp, samples)
    reduced, system, norm_row = pl.pallas_call(
        writer,
        out_shape=results,
        in_specs=[pl.BlockSpec(memory_space=pltpu.HBM)] * 3,
        out_specs=(pl.BlockSpec(memory_space=pltpu.HBM),) * 3,
        scratch_shapes=[pltpu.SemaphoreType.DMA((3,))],
        compiler_params=pltpu.CompilerParams(vmem_limit_bytes=60 * 1024 * 1024),
    )(reduced, system, norm_row)
    return jnp.transpose(reduced, (1, 2, 0)), system, norm_row.reshape(WIDTH)


def solution(mesh):
    placed = (P(), P(), P(None, "freq", "elem"))
    return jax.shard_map(
        per_device,
        mesh=mesh,
        in_specs=placed,
        out_specs=(P(None, None, ("elem", "freq")), P(), P()),
        check_vma=False,
    )
```

```python
import jax
import jax.numpy as jnp
from jax import lax
from jax.experimental import pallas as pl
from jax.experimental.pallas import tpu as pltpu
from jax.sharding import PartitionSpec as P

HIGH = lax.Precision.HIGHEST
MESH = pl.DeviceIdType.MESH
F32 = jnp.float32

NX, NZH, NZL, NY, NC = 4, 4, 2, 8, 2
NZ = NZH * NZL
NZY = NZL * NY
NFREQ = NZY * NC
PAIRS = 16
WIDTH = 2 * PAIRS + 1
ROWS = 40
BASIS = 48
OWN = 12
GROUP = 3
STRIDE = 40
TILES = OWN // GROUP
CHUNK = 256
CHUNKS = 4
LANES = 128
FREQ_LOCAL = 1024
ELEM_LOCAL = OWN * NFREQ
FREQ_TOTAL = FREQ_LOCAL * NFREQ
ELEM_TOTAL = ELEM_LOCAL * NX * NZH
INV_NF = 1.0 / FREQ_TOTAL


def iota(shape, dim):
    return lax.broadcasted_iota(jnp.int32, shape, dim)


def omega_of(half_position):
    return 0.02 + 0.98 * half_position / FREQ_TOTAL


def inverse_of(value):
    r = pltpu.reciprocal(value, approx=True)
    r = r * (2.0 - value * r)
    return r * (2.0 - value * r)


def split(value):
    high = value.astype(jnp.bfloat16)
    return high, (value - high.astype(F32)).astype(jnp.bfloat16)


def bf_dot(a, b):
    return jnp.dot(a, b, preferred_element_type=F32)


def wrap(value, size):
    return jnp.where(value >= size, value - size, value)


def tree_sum(values):
    values = list(values)
    while len(values) > 1:
        values = [a + b for a, b in zip(values[::2], values[1::2])] + values[len(values) & ~1 :]
    return values[0]


def pick(ref, index, shape):
    out = jnp.zeros(shape, F32)
    for m in range(PAIRS):
        out = jnp.where(index == m, ref[m], out)
    return out


def over_rows(col):
    return jnp.concatenate([col, col, jnp.zeros((8, LANES), F32)], axis=0)


def pair_coefs(ci, di, cj, dj, row_sum, col_sum):
    both = di + dj
    gap = cj - ci
    tot = ci + cj
    sq = both * both
    r1 = inverse_of(sq + gap * gap)
    r2 = inverse_of(sq + tot * tot)
    alpha, beta = both * r1, gap * r1
    gamma, delta = both * r2, -tot * r2
    ap, am = alpha + gamma, alpha - gamma
    bm, bp = beta - delta, beta + delta

    def table(di, bm, bp, row_sum, col_sum):
        ss, bd, bs, da = di * ap, di * bm, di * bp, di * am
        cr = jnp.where(row_sum, jnp.where(col_sum, ss, -bd), jnp.where(col_sum, bs, da))
        ce = jnp.where(row_sum, jnp.where(col_sum, bd, ss), jnp.where(col_sum, -da, bs))
        return cr, ce

    return table(di, bm, bp, row_sum, col_sum) + table(dj, -bp, -bm, col_sum, row_sum)


def coef_tables(c_col, d_col, pf, pd):
    shape = (ROWS, LANES)
    row, col = iota(shape, 0), iota(shape, 1)
    small = iota((8, LANES), 1) & (PAIRS - 1)
    cj, dj = pick(pf, small, (8, LANES)), pick(pd, small, (8, LANES))
    tall = lambda v: jnp.concatenate([v] * (ROWS // 8), axis=0)
    inside = (row < 2 * PAIRS) & (col < 2 * PAIRS)
    cr, ce, crt, cet = pair_coefs(
        over_rows(c_col), over_rows(d_col), tall(cj), tall(dj), row < PAIRS, col < PAIRS
    )
    last_row = row == 2 * PAIRS
    last_col = col == 2 * PAIRS
    one = lambda cond: jnp.where(cond, 1.0, 0.0).astype(F32)
    cr = jnp.where(inside, cr, one(last_row & ((col < PAIRS) | last_col)))
    ce = jnp.where(inside, ce, one(last_row & (col >= PAIRS) & (col < 2 * PAIRS)))
    crt = jnp.where(inside, crt, one(last_col & (row < PAIRS)))
    cet = jnp.where(inside, cet, one(last_col & (row >= PAIRS) & (row < 2 * PAIRS)))
    return cr, ce, crt, cet


def assemble(tables, r_row, e_row, r_col, e_col):
    cr, ce, crt, cet = tables
    return cr * r_row + ce * e_row + crt * over_rows(r_col) + cet * over_rows(e_col)


def col_to_row(col):
    row, lane = iota((PAIRS, LANES), 0), iota((PAIRS, LANES), 1)
    keep = ((lane & (PAIRS - 1)) == row) & (lane < 2 * PAIRS)
    return jnp.sum(jnp.where(keep, col, 0.0), axis=0, keepdims=True)


def row_to_col(row_vec, first):
    row, lane = iota((PAIRS, LANES), 0), iota((PAIRS, LANES), 1)
    kept = jnp.where(lane == row + first, jnp.broadcast_to(row_vec, (PAIRS, LANES)), 0.0)
    return jnp.broadcast_to(jnp.sum(kept, axis=1, keepdims=True), (PAIRS, LANES))


def rows_from(values):
    lane = iota(values.shape, 1)
    j = lane - jnp.where(lane >= 2 * STRIDE, 2 * STRIDE, jnp.where(lane >= STRIDE, STRIDE, 0))
    r_row = jnp.where(
        j < PAIRS,
        values,
        jnp.where(j < 2 * PAIRS, pltpu.roll(values, PAIRS, 1), jnp.where(j == 2 * PAIRS, values, 0.0)),
    )
    e_row = jnp.where(
        j < PAIRS,
        pltpu.roll(values, LANES - PAIRS, 1),
        jnp.where(j < 2 * PAIRS, values, 0.0),
    )
    return r_row, e_row


def eliminate(work):
    parts = [work[8 * b : 8 * b + 8] for b in range(ROWS // 8)]
    sub = iota((8, LANES), 0)
    for first in range(0, WIDTH, 8):
        count = min(8, WIDTH - first)
        b0 = first // 8
        live = range(b0, len(parts))
        cols = [
            [jnp.broadcast_to(parts[b][:, first + t : first + t + 1], (8, LANES)) for b in live]
            for t in range(count)
        ]
        rows = [parts[b0][t : t + 1, :] for t in range(count)]
        for t in range(count):
            inv = inverse_of(cols[t][0][t : t + 1, :])
            factor = [v * inv for v in cols[t]]
            factor[0] = jnp.where(sub > t, factor[0], 0.0)
            for u in range(t + 1, count):
                lead = cols[u][0][t : t + 1, :]
                cols[u] = [v - f * lead for v, f in zip(cols[u], factor)]
                rows[u] = rows[u] - factor[0][u : u + 1, :] * rows[t]
            for n, b in enumerate(live):
                parts[b] = parts[b] - factor[n] * rows[t]
    return jnp.concatenate(parts, axis=0)


def kernel(
    pf_hbm, pd_hbm, s_hbm, red_ref, sys_ref, nrm_ref,
    pf, pd, s_buf, re_buf, im_buf, xt_buf, pieces, recv_b,
    buf_x, buf_y, buf_z,
    pole_sem, load_sem, send_sem, recv_sem,
):
    elem, freq = lax.axis_index("elem"), lax.axis_index("freq")
    x, z_hi = elem // NZH, elem % NZH
    zy, core = freq // NC, freq % NC
    z_lo, y = zy // NY, zy % NY
    z = z_hi * NZL + z_lo

    def at_freq(other):
        return {"elem": elem, "freq": other}

    def at_y(other):
        return {"elem": elem, "freq": (z_lo * NY + other) * NC + core}

    z_peers = []
    for dz in range(NZH):
        for low in range(NZL):
            if dz or low:
                hi, lo = wrap(z_hi + dz, NZH), wrap(z_lo + low, NZL)
                z_peers.append({"elem": x * NZH + hi, "freq": (lo * NY + y) * NC + core})
    x_peers = []
    for dx in range(NX):
        for c in range(NC):
            if dx or c:
                to = wrap(x + dx, NX)
                x_peers.append({"elem": to * NZH + z_hi, "freq": zy * NC + wrap(core + c, NC)})
    y_peers = [at_y(wrap(y + dy, NY)) for dy in range(1, NY)]

    pole_loads = [
        pltpu.make_async_copy(pf_hbm, pf, pole_sem.at[0]),
        pltpu.make_async_copy(pd_hbm, pd, pole_sem.at[1]),
    ]
    for load in pole_loads:
        load.start()
    loads = {}
    for k in range(CHUNKS):
        for part in range(2):
            at = pl.ds(k * CHUNK, CHUNK)
            loads[part, k] = pltpu.make_async_copy(
                s_hbm.at[part, at], s_buf.at[part, at], load_sem.at[part, k]
            )
            loads[part, k].start()

    barrier = pltpu.get_barrier_semaphore()

    def greet(device):
        pl.semaphore_signal(barrier, inc=1, device_id=device, device_id_type=MESH)

    for step in range(1, NFREQ):
        greet(at_freq(wrap(freq + step, NFREQ)))
    for device in z_peers[NZL - 1 :] + x_peers[NC - 1 :]:
        greet(device)
    greeted = NFREQ - 1 + len(z_peers) - (NZL - 1) + len(x_peers) - (NC - 1)

    for load in pole_loads:
        load.wait()

    column = iota((PAIRS, LANES), 0)
    c_col = pick(pf, column, (PAIRS, LANES))
    d_col = pick(pd, column, (PAIRS, LANES))
    d_sq = d_col * d_col
    half8 = iota((8, LANES), 1).astype(F32) + 0.5
    half16 = iota((PAIRS, LANES), 1).astype(F32) + 0.5
    base = (freq * FREQ_LOCAL).astype(F32)
    ones = jnp.where(iota((PAIRS, FREQ_LOCAL), 0) == 0, 1.0, 0.0)
    re_buf[2 * PAIRS : BASIS, :] = ones.astype(jnp.bfloat16)
    re_buf[BASIS + 2 * PAIRS :, :] = jnp.zeros((PAIRS, FREQ_LOCAL), jnp.bfloat16)
    for tile in range(FREQ_LOCAL // LANES):
        at = pl.ds(tile * LANES, LANES)
        w = omega_of(half16 + (base + tile * LANES))
        below, above = w - c_col, w + c_col
        i1 = inverse_of(d_sq + below * below)
        i2 = inverse_of(d_sq + above * above)
        first, second = below * i1, above * i2
        re_buf[0:PAIRS, at], re_buf[BASIS : BASIS + PAIRS, at] = split(d_sq * (i1 + i2))
        re_buf[PAIRS : 2 * PAIRS, at], re_buf[BASIS + PAIRS : BASIS + 2 * PAIRS, at] = split(
            d_col * (first - second)
        )
        im_buf[0:PAIRS, at], im_buf[2 * PAIRS : 3 * PAIRS, at] = split(-d_col * (first + second))
        im_buf[PAIRS : 2 * PAIRS, at], im_buf[3 * PAIRS :, at] = split(d_sq * (i1 - i2))

    c_half = [c_col[0:8], c_col[8:16]]
    q_half = [d_sq[0:8], d_sq[8:16]]

    def mean_step(chunk, acc):
        acc = list(acc)
        start = (chunk * FREQ_LOCAL).astype(F32)
        for tile in range(FREQ_LOCAL // LANES):
            w = omega_of(half8 + (start + tile * LANES))
            for h in range(2):
                below, above = w - c_half[h], w + c_half[h]
                n1 = q_half[h] + below * below
                n2 = q_half[h] + above * above
                r = inverse_of(n1 * n2)
                acc[2 * h] = acc[2 * h] + r * (n1 + n2)
                acc[2 * h + 1] = acc[2 * h + 1] + r * (below * n2 - above * n1)
        return tuple(acc)

    acc = (jnp.zeros((8, LANES), F32),) * 4
    acc = lax.fori_loop(0, NFREQ // 2, mean_step, acc)

    x0 = jnp.zeros((BASIS, ELEM_LOCAL + LANES), F32)
    x1 = jnp.zeros((2 * PAIRS, ELEM_LOCAL), F32)
    for k in range(CHUNKS):
        at = pl.ds(k * CHUNK, CHUNK)
        loads[0, k].wait()
        loads[1, k].wait()
        s0, s1 = s_buf[0, at, :], s_buf[1, at, :]
        squares = s0 * s0 + s1 * s1
        power = tree_sum(squares[:, t * LANES : (t + 1) * LANES] for t in range(ELEM_LOCAL // LANES))
        high, low = split(jnp.concatenate([s0, power], axis=1))
        both = bf_dot(re_buf[:, at], high)
        x0 = x0 + (both[0:BASIS] + both[BASIS:] + bf_dot(re_buf[0:BASIS, at], low))
        high, low = split(s1)
        both = bf_dot(im_buf[:, at], high)
        x1 = x1 + (both[0 : 2 * PAIRS] + both[2 * PAIRS :] + bf_dot(im_buf[0 : 2 * PAIRS, at], low))
    x0, q = x0[:, 0:ELEM_LOCAL], x0[0:ROWS, ELEM_LOCAL:]

    stacked = jnp.concatenate(
        [
            x0,
            jnp.zeros((64 - BASIS, ELEM_LOCAL), F32),
            x1,
            jnp.zeros((LANES - 64 - 2 * PAIRS, ELEM_LOCAL), F32),
        ],
        axis=0,
    )
    for tile in range(ELEM_LOCAL // LANES):
        at = slice(tile * LANES, (tile + 1) * LANES)
        xt_buf[at, :] = stacked[:, at].T
    count = ELEM_LOCAL // GROUP
    thirds = [xt_buf[pl.ds(q, count, stride=GROUP), :] for q in range(GROUP)]
    lane_c = iota((count, LANES), 1)

    def spread(shift):
        rolled = [
            pltpu.roll(thirds[q], (STRIDE * q + shift) % LANES, 1) if (STRIDE * q + shift) % LANES else thirds[q]
            for q in range(GROUP)
        ]
        return jnp.where(
            lane_c < STRIDE, rolled[0], jnp.where(lane_c < 2 * STRIDE, rolled[1], rolled[2])
        )

    part0, part1 = spread(0), spread(64)
    upper = iota((8, LANES), 0) < 4
    for k in range(NZY):
        v0, v1 = part0[8 * k : 8 * k + 8], part1[8 * k : 8 * k + 8]
        pieces[NC * k] = jnp.where(upper, v0, pltpu.roll(v1, 4, 0))
        pieces[NC * k + 1] = jnp.where(upper, pltpu.roll(v0, 4, 0), v1)

    pl.semaphore_wait(barrier, greeted)

    for step in range(1, NFREQ):
        other = wrap(freq + step, NFREQ)
        pltpu.make_async_remote_copy(
            src_ref=pieces.at[other],
            dst_ref=recv_b.at[freq],
            send_sem=send_sem.at[0],
            recv_sem=recv_sem.at[0],
            device_id=at_freq(other),
            device_id_type=MESH,
        ).start()
    recv_b[freq] = pieces[freq]

    acc = lax.fori_loop(NFREQ // 2, NFREQ, mean_step, acc)

    def lane_sum(v):
        return jnp.broadcast_to(jnp.sum(v, axis=1, keepdims=True), v.shape)

    mean_r = d_sq * lane_sum(jnp.concatenate([acc[0], acc[2]], axis=0)) * INV_NF
    mean_e = d_col * lane_sum(jnp.concatenate([acc[1], acc[3]], axis=0)) * INV_NF
    tables = coef_tables(c_col, d_col, pf, pd)

    lane1 = iota((1, LANES), 1)
    mean_r_row, mean_e_row = col_to_row(mean_r), col_to_row(mean_e)
    gram = assemble(
        tables,
        jnp.where(lane1 == 2 * PAIRS, 1.0, mean_r_row),
        mean_e_row,
        mean_r,
        mean_e,
    )
    row, lane = iota((ROWS, LANES), 0), iota((ROWS, LANES), 1)
    work = gram + jnp.where((lane == row + 64) & (row < WIDTH), 1.0, 0.0)
    work = eliminate(work)
    pivots = jnp.sum(jnp.where((lane == row) & (row < WIDTH), work, 0.0), axis=1, keepdims=True)
    pivots = jnp.where(iota((ROWS, 1), 0) < WIDTH, pivots, 1.0)
    inverse = pltpu.roll(work, 64, 1) * (1.0 / jnp.sqrt(pivots))
    inverse = jnp.where(lane < WIDTH, inverse, 0.0)

    q = jnp.broadcast_to(jnp.sum(q, axis=1, keepdims=True), (ROWS, LANES))
    q_row = jnp.sum(jnp.where(lane == row, q, 0.0), axis=0, keepdims=True)

    triple = [
        v + pltpu.roll(v, STRIDE, 1) + pltpu.roll(v, 2 * STRIDE, 1) for v in tables
    ]

    rest_b = recv_b.at[pl.ds(0, NFREQ - 1)]
    pltpu.make_async_copy(rest_b, rest_b, recv_sem.at[0]).wait()
    owned = tree_sum(recv_b[k] for k in range(NFREQ))
    owned = owned * (-INV_NF)

    other_part = pltpu.roll(owned, 4, 0)
    plus, minus = owned + other_part, owned - other_part
    r_rows, e_rows = rows_from(minus)
    plus_t = jnp.concatenate([plus, jnp.zeros((LANES - 8, LANES), F32)], axis=0).T
    lane16 = iota((PAIRS, LANES), 1)

    def columns(g, first):
        spread_col = [
            jnp.broadcast_to(
                plus_t[STRIDE * q + first : STRIDE * q + first + PAIRS, g : g + 1], (PAIRS, LANES)
            )
            for q in range(GROUP)
        ]
        return jnp.where(
            lane16 < STRIDE, spread_col[0], jnp.where(lane16 < 2 * STRIDE, spread_col[1], spread_col[2])
        )

    coupling = jnp.concatenate(
        [
            assemble(triple, r_rows[g : g + 1, :], e_rows[g : g + 1, :], columns(g, 0), columns(g, PAIRS))
            for g in range(TILES)
        ],
        axis=1,
    )
    reduced = jnp.dot(
        inverse[:, 0:ROWS], coupling, precision=HIGH, preferred_element_type=F32
    )
    parts = [reduced[:, g * LANES : (g + 1) * LANES] for g in range(TILES)]
    tall = jnp.concatenate(parts, axis=0)
    wide = jnp.dot(tall.T, tall, precision=HIGH, preferred_element_type=F32)
    corr = wide[0:ROWS]
    for q in range(1, GROUP):
        at = STRIDE * q
        corr = corr + pltpu.roll(wide[at : at + ROWS], LANES - at, 1)

    sub8, ln8 = iota((8, LANES), 0), iota((8, LANES), 1)
    spread8 = lambda v: jnp.broadcast_to(v, (8, LANES))
    border = jnp.where(
        sub8 == 0, spread8(corr[32:33]), jnp.where(sub8 == 1, spread8(q_row), 0.0)
    )
    packed = pltpu.roll(border, 80, 1)
    for g, first, shift in ((3, 80, 48), (2, 72, 40), (1, 56, 24)):
        packed = jnp.where(ln8 < first, pltpu.roll(corr[8 * g : 8 * g + 8], shift, 1), packed)
    total = jnp.where(ln8 < 32, corr[0:8], packed)

    def send(buf, me, peers, index, value):
        buf[me] = value
        for device in peers:
            pltpu.make_async_remote_copy(
                src_ref=buf.at[me],
                dst_ref=buf.at[me],
                send_sem=send_sem.at[index],
                recv_sem=recv_sem.at[index],
                device_id=device,
                device_id_type=MESH,
            ).start()

    def receive(buf, count, index):
        rest = buf.at[pl.ds(0, count - 1)]
        pltpu.make_async_copy(rest, rest, recv_sem.at[index]).wait()
        return tree_sum(buf[k] for k in range(count))

    send(buf_x, x * NC + core, x_peers, 1, total)

    for g in range(TILES):
        for q in range(GROUP):
            block = pltpu.roll(parts[g], LANES - STRIDE * q, 1) if q else parts[g]
            red_ref[GROUP * g + q] = block[0:WIDTH, 0:WIDTH]

    total = receive(buf_x, NX * NC, 1)
    send(buf_y, y, y_peers, 2, total)
    total = receive(buf_y, NY, 2)
    send(buf_z, z, z_peers, 3, total)
    mean_row = jnp.where(
        lane1 < PAIRS,
        mean_r_row,
        jnp.where(lane1 < 2 * PAIRS, mean_e_row, 1.0),
    )
    total = receive(buf_z, NZ, 3)

    border = pltpu.roll(total, LANES - 80, 1)
    moments = jnp.where(lane1 < WIDTH, border[1:2], 0.0) * INV_NF
    mean_sq = moments[:, 2 * PAIRS : 2 * PAIRS + 1]
    r_row, e_row = rows_from(moments)
    data_gram = assemble(
        tables, r_row, e_row, row_to_col(moments, 0), row_to_col(moments, PAIRS)
    )
    half = jnp.concatenate(
        [total]
        + [pltpu.roll(total, LANES - shift, 1) for shift in (24, 40, 48)]
        + [spread8(border[0:1])],
        axis=0,
    )
    square = jnp.concatenate([half, jnp.zeros((LANES - ROWS, LANES), F32)], axis=0)
    stored = ((lane < 2 * PAIRS) & (lane >= (row & ~7))) | (row >= 2 * PAIRS)
    correction = jnp.where(stored, half, square.T[0:ROWS])
    system = (data_gram - correction) * (1.0 / mean_sq)
    sys_ref[...] = system[0:WIDTH, 0:WIDTH]
    nrm_ref[...] = (mean_row * jnp.sqrt(mean_sq * (1.0 / ELEM_TOTAL)))[:, 0:WIDTH]

    for buf, count, index in (
        (pieces, NFREQ, 0), (buf_x, NX * NC, 1), (buf_y, NY, 2), (buf_z, NZ, 3)
    ):
        rest = buf.at[pl.ds(0, count - 1)]
        pltpu.make_async_copy(rest, rest, send_sem.at[index]).wait()


def per_device(pole_freq, pole_damp, samples):
    vmem = lambda *shape: pltpu.VMEM(shape, F32)
    in_hbm = lambda v: pltpu.with_memory_space_constraint(v, pltpu.HBM)
    half = lambda *shape: pltpu.VMEM(shape, jnp.bfloat16)
    results = (
        vmem(OWN, WIDTH, WIDTH),
        vmem(WIDTH, WIDTH),
        vmem(1, WIDTH),
    )
    reduced, system, norm_row = pl.pallas_call(
        kernel,
        out_shape=results,
        in_specs=[pl.BlockSpec(memory_space=pltpu.HBM)] * 3,
        out_specs=(pl.BlockSpec(memory_space=pltpu.VMEM),) * 3,
        scratch_shapes=[
            pltpu.SMEM((PAIRS,), F32),
            pltpu.SMEM((PAIRS,), F32),
            vmem(2, FREQ_LOCAL, ELEM_LOCAL),
            half(2 * BASIS, FREQ_LOCAL),
            half(4 * PAIRS, FREQ_LOCAL),
            vmem(ELEM_LOCAL, LANES),
            vmem(NFREQ, 8, LANES),
            vmem(NFREQ, 8, LANES),
            vmem(NX * NC, 8, LANES),
            vmem(NY, 8, LANES),
            vmem(NZ, 8, LANES),
            pltpu.SemaphoreType.DMA((2,)),
            pltpu.SemaphoreType.DMA((2, CHUNKS)),
            pltpu.SemaphoreType.DMA((4,)),
            pltpu.SemaphoreType.DMA((4,)),
        ],
        compiler_params=pltpu.CompilerParams(
            collective_id=0, has_side_effects=True, vmem_limit_bytes=40 * 1024 * 1024
        ),
    )(*(in_hbm(v) for v in (pole_freq, pole_damp, samples)))
    return jnp.transpose(reduced, (1, 2, 0)), system, norm_row.reshape(WIDTH)


def solution(mesh):
    placed = (P(), P(), P(None, "freq", "elem"))
    return jax.shard_map(
        per_device,
        mesh=mesh,
        in_specs=placed,
        out_specs=(P(None, None, ("elem", "freq")), P(), P()),
        check_vma=False,
    )
```

```python
import jax
import jax.numpy as jnp
from jax import lax
from jax.experimental import pallas as pl
from jax.experimental.pallas import tpu as pltpu
from jax.sharding import PartitionSpec as P

HIGH = lax.Precision.HIGHEST
MESH = pl.DeviceIdType.MESH
F32 = jnp.float32

NX, NZH, NZL, NY, NC = 4, 4, 2, 8, 2
NZ = NZH * NZL
NZY = NZL * NY
NFREQ = NZY * NC
PAIRS = 16
WIDTH = 2 * PAIRS + 1
ROWS = 40
BASIS = 48
OWN = 12
GROUP = 3
STRIDE = 40
TILES = OWN // GROUP
CHUNK = 256
CHUNKS = 4
LANES = 128
FREQ_LOCAL = 1024
ELEM_LOCAL = OWN * NFREQ
FREQ_TOTAL = FREQ_LOCAL * NFREQ
ELEM_TOTAL = ELEM_LOCAL * NX * NZH
INV_NF = 1.0 / FREQ_TOTAL


def iota(shape, dim):
    return lax.broadcasted_iota(jnp.int32, shape, dim)


def omega_of(half_position):
    return 0.02 + 0.98 * half_position / FREQ_TOTAL


def inverse_of(value):
    r = pltpu.reciprocal(value, approx=True)
    r = r * (2.0 - value * r)
    return r * (2.0 - value * r)


def split(value):
    high = value.astype(jnp.bfloat16)
    return high, (value - high.astype(F32)).astype(jnp.bfloat16)


def bf_dot(a, b):
    return jnp.dot(a, b, preferred_element_type=F32)


def wrap(value, size):
    return jnp.where(value >= size, value - size, value)


def tree_sum(values):
    values = list(values)
    while len(values) > 1:
        values = [a + b for a, b in zip(values[::2], values[1::2])] + values[len(values) & ~1 :]
    return values[0]


def pick(ref, index, shape):
    out = jnp.zeros(shape, F32)
    for m in range(PAIRS):
        out = jnp.where(index == m, ref[m], out)
    return out


def over_rows(col):
    return jnp.concatenate([col, col, jnp.zeros((8, LANES), F32)], axis=0)


def pair_coefs(ci, di, cj, dj, row_sum, col_sum):
    both = di + dj
    gap = cj - ci
    tot = ci + cj
    sq = both * both
    r1 = inverse_of(sq + gap * gap)
    r2 = inverse_of(sq + tot * tot)
    alpha, beta = both * r1, gap * r1
    gamma, delta = both * r2, -tot * r2
    ap, am = alpha + gamma, alpha - gamma
    bm, bp = beta - delta, beta + delta

    def table(di, bm, bp, row_sum, col_sum):
        ss, bd, bs, da = di * ap, di * bm, di * bp, di * am
        cr = jnp.where(row_sum, jnp.where(col_sum, ss, -bd), jnp.where(col_sum, bs, da))
        ce = jnp.where(row_sum, jnp.where(col_sum, bd, ss), jnp.where(col_sum, -da, bs))
        return cr, ce

    return table(di, bm, bp, row_sum, col_sum) + table(dj, -bp, -bm, col_sum, row_sum)


def coef_tables(c_col, d_col, pf, pd):
    shape = (ROWS, LANES)
    row, col = iota(shape, 0), iota(shape, 1)
    small = iota((8, LANES), 1) & (PAIRS - 1)
    cj, dj = pick(pf, small, (8, LANES)), pick(pd, small, (8, LANES))
    tall = lambda v: jnp.concatenate([v] * (ROWS // 8), axis=0)
    inside = (row < 2 * PAIRS) & (col < 2 * PAIRS)
    cr, ce, crt, cet = pair_coefs(
        over_rows(c_col), over_rows(d_col), tall(cj), tall(dj), row < PAIRS, col < PAIRS
    )
    last_row = row == 2 * PAIRS
    last_col = col == 2 * PAIRS
    one = lambda cond: jnp.where(cond, 1.0, 0.0).astype(F32)
    cr = jnp.where(inside, cr, one(last_row & ((col < PAIRS) | last_col)))
    ce = jnp.where(inside, ce, one(last_row & (col >= PAIRS) & (col < 2 * PAIRS)))
    crt = jnp.where(inside, crt, one(last_col & (row < PAIRS)))
    cet = jnp.where(inside, cet, one(last_col & (row >= PAIRS) & (row < 2 * PAIRS)))
    return cr, ce, crt, cet


def assemble(tables, r_row, e_row, r_col, e_col):
    cr, ce, crt, cet = tables
    return cr * r_row + ce * e_row + crt * over_rows(r_col) + cet * over_rows(e_col)


def row_to_col(row_vec, first):
    row, lane = iota((PAIRS, LANES), 0), iota((PAIRS, LANES), 1)
    kept = jnp.where(lane == row + first, jnp.broadcast_to(row_vec, (PAIRS, LANES)), 0.0)
    return jnp.broadcast_to(jnp.sum(kept, axis=1, keepdims=True), (PAIRS, LANES))


def rows_from(values):
    lane = iota(values.shape, 1)
    j = lane - jnp.where(lane >= 2 * STRIDE, 2 * STRIDE, jnp.where(lane >= STRIDE, STRIDE, 0))
    r_row = jnp.where(
        j < PAIRS,
        values,
        jnp.where(j < 2 * PAIRS, pltpu.roll(values, PAIRS, 1), jnp.where(j == 2 * PAIRS, values, 0.0)),
    )
    e_row = jnp.where(
        j < PAIRS,
        pltpu.roll(values, LANES - PAIRS, 1),
        jnp.where(j < 2 * PAIRS, values, 0.0),
    )
    return r_row, e_row


def eliminate(work):
    parts = [work[8 * b : 8 * b + 8] for b in range(ROWS // 8)]
    sub = iota((8, LANES), 0)
    for first in range(0, WIDTH, 8):
        count = min(8, WIDTH - first)
        b0 = first // 8
        live = range(b0, len(parts))
        cols = [
            [jnp.broadcast_to(parts[b][:, first + t : first + t + 1], (8, LANES)) for b in live]
            for t in range(count)
        ]
        rows = [parts[b0][t : t + 1, :] for t in range(count)]
        for t in range(count):
            inv = inverse_of(cols[t][0][t : t + 1, :])
            factor = [v * inv for v in cols[t]]
            factor[0] = jnp.where(sub > t, factor[0], 0.0)
            for u in range(t + 1, count):
                lead = cols[u][0][t : t + 1, :]
                cols[u] = [v - f * lead for v, f in zip(cols[u], factor)]
                rows[u] = rows[u] - factor[0][u : u + 1, :] * rows[t]
            for n, b in enumerate(live):
                parts[b] = parts[b] - factor[n] * rows[t]
    return jnp.concatenate(parts, axis=0)


def kernel(
    pf_hbm, pd_hbm, s_hbm, red_ref, sys_ref, nrm_ref,
    pf, pd, s_buf, re_buf, im_buf, xt_buf, pieces, recv_b,
    buf_m, buf_x, buf_y, buf_z,
    pole_sem, load_sem, send_sem, recv_sem,
):
    elem, freq = lax.axis_index("elem"), lax.axis_index("freq")
    x, z_hi = elem // NZH, elem % NZH
    zy, core = freq // NC, freq % NC
    z_lo, y = zy // NY, zy % NY
    z = z_hi * NZL + z_lo

    def at_freq(other):
        return {"elem": elem, "freq": other}

    def at_y(other):
        return {"elem": elem, "freq": (z_lo * NY + other) * NC + core}

    z_peers = []
    for dz in range(NZH):
        for low in range(NZL):
            if dz or low:
                hi, lo = wrap(z_hi + dz, NZH), wrap(z_lo + low, NZL)
                z_peers.append({"elem": x * NZH + hi, "freq": (lo * NY + y) * NC + core})
    x_peers = []
    for dx in range(NX):
        for c in range(NC):
            if dx or c:
                to = wrap(x + dx, NX)
                x_peers.append({"elem": to * NZH + z_hi, "freq": zy * NC + wrap(core + c, NC)})
    y_peers = [at_y(wrap(y + dy, NY)) for dy in range(1, NY)]

    pole_loads = [
        pltpu.make_async_copy(pf_hbm, pf, pole_sem.at[0]),
        pltpu.make_async_copy(pd_hbm, pd, pole_sem.at[1]),
    ]
    for load in pole_loads:
        load.start()
    loads = {}
    for k in range(CHUNKS):
        for part in range(2):
            at = pl.ds(k * CHUNK, CHUNK)
            loads[part, k] = pltpu.make_async_copy(
                s_hbm.at[part, at], s_buf.at[part, at], load_sem.at[part, k]
            )
            loads[part, k].start()

    barrier = pltpu.get_barrier_semaphore()

    def greet(device):
        pl.semaphore_signal(barrier, inc=1, device_id=device, device_id_type=MESH)

    for step in range(1, NFREQ):
        greet(at_freq(wrap(freq + step, NFREQ)))
    for device in z_peers[NZL - 1 :] + x_peers[NC - 1 :]:
        greet(device)
    greeted = NFREQ - 1 + len(z_peers) - (NZL - 1) + len(x_peers) - (NC - 1)

    for load in pole_loads:
        load.wait()

    column = iota((PAIRS, LANES), 0)
    c_col = pick(pf, column, (PAIRS, LANES))
    d_col = pick(pd, column, (PAIRS, LANES))
    d_sq = d_col * d_col
    half16 = iota((PAIRS, LANES), 1).astype(F32) + 0.5
    base = (freq * FREQ_LOCAL).astype(F32)
    ones = jnp.where(iota((PAIRS, FREQ_LOCAL), 0) == 0, 1.0, 0.0)
    re_buf[2 * PAIRS : BASIS, :] = ones.astype(jnp.bfloat16)
    re_buf[BASIS + 2 * PAIRS :, :] = jnp.zeros((PAIRS, FREQ_LOCAL), jnp.bfloat16)
    for tile in range(FREQ_LOCAL // LANES):
        at = pl.ds(tile * LANES, LANES)
        w = omega_of(half16 + (base + tile * LANES))
        below, above = w - c_col, w + c_col
        i1 = inverse_of(d_sq + below * below)
        i2 = inverse_of(d_sq + above * above)
        first, second = below * i1, above * i2
        re_buf[0:PAIRS, at], re_buf[BASIS : BASIS + PAIRS, at] = split(d_sq * (i1 + i2))
        re_buf[PAIRS : 2 * PAIRS, at], re_buf[BASIS + PAIRS : BASIS + 2 * PAIRS, at] = split(
            d_col * (first - second)
        )
        im_buf[0:PAIRS, at], im_buf[2 * PAIRS : 3 * PAIRS, at] = split(-d_col * (first + second))
        im_buf[PAIRS : 2 * PAIRS, at], im_buf[3 * PAIRS :, at] = split(d_sq * (i1 - i2))

    base = (zy * (NC * FREQ_LOCAL)).astype(F32)
    sum_r = jnp.zeros((PAIRS, LANES), F32)
    sum_e = jnp.zeros((PAIRS, LANES), F32)
    for tile in range(NC * FREQ_LOCAL // LANES):
        w = omega_of(half16 + (base + tile * LANES))
        below, above = w - c_col, w + c_col
        n1 = d_sq + below * below
        n2 = d_sq + above * above
        r = inverse_of(n1 * n2)
        sum_r = sum_r + r * (n1 + n2)
        sum_e = sum_e + r * (below * n2 - above * n1)
    lane16 = iota((PAIRS, LANES), 1)
    sum_r = d_sq * jnp.sum(sum_r, axis=1, keepdims=True)
    sum_e = d_col * jnp.sum(sum_e, axis=1, keepdims=True)
    sums = jnp.where(lane16 == column, sum_r, jnp.where(lane16 == column + PAIRS, sum_e, 0.0))
    pl.semaphore_wait(barrier, greeted)
    buf_m[zy] = jnp.sum(sums, axis=0, keepdims=True)
    for step in range(1, NZY):
        pltpu.make_async_remote_copy(
            src_ref=buf_m.at[zy],
            dst_ref=buf_m.at[zy],
            send_sem=send_sem.at[4],
            recv_sem=recv_sem.at[4],
            device_id=at_freq(wrap(zy + step, NZY) * NC + core),
            device_id_type=MESH,
        ).start()

    tables = coef_tables(c_col, d_col, pf, pd)

    x0 = jnp.zeros((BASIS, ELEM_LOCAL + LANES), F32)
    x1 = jnp.zeros((2 * PAIRS, ELEM_LOCAL), F32)
    for k in range(CHUNKS):
        at = pl.ds(k * CHUNK, CHUNK)
        loads[0, k].wait()
        loads[1, k].wait()
        s0, s1 = s_buf[0, at, :], s_buf[1, at, :]
        squares = s0 * s0 + s1 * s1
        power = tree_sum(squares[:, t * LANES : (t + 1) * LANES] for t in range(ELEM_LOCAL // LANES))
        high, low = split(jnp.concatenate([s0, power], axis=1))
        both = bf_dot(re_buf[:, at], high)
        x0 = x0 + (both[0:BASIS] + both[BASIS:] + bf_dot(re_buf[0:BASIS, at], low))
        high, low = split(s1)
        both = bf_dot(im_buf[:, at], high)
        x1 = x1 + (both[0 : 2 * PAIRS] + both[2 * PAIRS :] + bf_dot(im_buf[0 : 2 * PAIRS, at], low))
    x0, q = x0[:, 0:ELEM_LOCAL], x0[0:ROWS, ELEM_LOCAL:]

    stacked = jnp.concatenate(
        [
            x0,
            jnp.zeros((64 - BASIS, ELEM_LOCAL), F32),
            x1,
            jnp.zeros((LANES - 64 - 2 * PAIRS, ELEM_LOCAL), F32),
        ],
        axis=0,
    )
    for tile in range(ELEM_LOCAL // LANES):
        at = slice(tile * LANES, (tile + 1) * LANES)
        xt_buf[at, :] = stacked[:, at].T
    count = ELEM_LOCAL // GROUP
    thirds = [xt_buf[pl.ds(q, count, stride=GROUP), :] for q in range(GROUP)]
    lane_c = iota((count, LANES), 1)

    def spread(shift):
        rolled = [
            pltpu.roll(thirds[q], (STRIDE * q + shift) % LANES, 1) if (STRIDE * q + shift) % LANES else thirds[q]
            for q in range(GROUP)
        ]
        return jnp.where(
            lane_c < STRIDE, rolled[0], jnp.where(lane_c < 2 * STRIDE, rolled[1], rolled[2])
        )

    part0, part1 = spread(0), spread(64)
    upper = iota((8, LANES), 0) < 4
    for k in range(NZY):
        v0, v1 = part0[8 * k : 8 * k + 8], part1[8 * k : 8 * k + 8]
        pieces[NC * k] = jnp.where(upper, v0, pltpu.roll(v1, 4, 0))
        pieces[NC * k + 1] = jnp.where(upper, pltpu.roll(v0, 4, 0), v1)

    for step in range(1, NFREQ):
        other = wrap(freq + step, NFREQ)
        pltpu.make_async_remote_copy(
            src_ref=pieces.at[other],
            dst_ref=recv_b.at[freq],
            send_sem=send_sem.at[0],
            recv_sem=recv_sem.at[0],
            device_id=at_freq(other),
            device_id_type=MESH,
        ).start()
    recv_b[freq] = pieces[freq]

    rest = buf_m.at[pl.ds(0, NZY - 1)]
    pltpu.make_async_copy(rest, rest, recv_sem.at[4]).wait()
    mean = tree_sum(buf_m[k] for k in range(NZY)) * INV_NF
    lane1 = iota((1, LANES), 1)
    mean = jnp.where(lane1 == 2 * PAIRS, 1.0, mean)
    r_row, e_row = rows_from(mean)
    gram = assemble(tables, r_row, e_row, row_to_col(mean, 0), row_to_col(mean, PAIRS))
    row, lane = iota((ROWS, LANES), 0), iota((ROWS, LANES), 1)
    work = gram + jnp.where((lane == row + 64) & (row < WIDTH), 1.0, 0.0)
    work = eliminate(work)
    pivots = jnp.sum(jnp.where((lane == row) & (row < WIDTH), work, 0.0), axis=1, keepdims=True)
    pivots = jnp.where(iota((ROWS, 1), 0) < WIDTH, pivots, 1.0)
    inverse = pltpu.roll(work, 64, 1) * (1.0 / jnp.sqrt(pivots))
    inverse = jnp.where(lane < WIDTH, inverse, 0.0)

    q = jnp.broadcast_to(jnp.sum(q, axis=1, keepdims=True), (ROWS, LANES))
    q_row = jnp.sum(jnp.where(lane == row, q, 0.0), axis=0, keepdims=True)

    triple = [
        v + pltpu.roll(v, STRIDE, 1) + pltpu.roll(v, 2 * STRIDE, 1) for v in tables
    ]

    rest_b = recv_b.at[pl.ds(0, NFREQ - 1)]
    pltpu.make_async_copy(rest_b, rest_b, recv_sem.at[0]).wait()
    owned = tree_sum(recv_b[k] for k in range(NFREQ))
    owned = owned * (-INV_NF)

    other_part = pltpu.roll(owned, 4, 0)
    plus, minus = owned + other_part, owned - other_part
    r_rows, e_rows = rows_from(minus)
    plus_t = jnp.concatenate([plus, jnp.zeros((LANES - 8, LANES), F32)], axis=0).T
    lane16 = iota((PAIRS, LANES), 1)

    def columns(g, first):
        spread_col = [
            jnp.broadcast_to(
                plus_t[STRIDE * q + first : STRIDE * q + first + PAIRS, g : g + 1], (PAIRS, LANES)
            )
            for q in range(GROUP)
        ]
        return jnp.where(
            lane16 < STRIDE, spread_col[0], jnp.where(lane16 < 2 * STRIDE, spread_col[1], spread_col[2])
        )

    coupling = jnp.concatenate(
        [
            assemble(triple, r_rows[g : g + 1, :], e_rows[g : g + 1, :], columns(g, 0), columns(g, PAIRS))
            for g in range(TILES)
        ],
        axis=1,
    )
    reduced = jnp.dot(
        inverse[:, 0:ROWS], coupling, precision=HIGH, preferred_element_type=F32
    )
    parts = [reduced[:, g * LANES : (g + 1) * LANES] for g in range(TILES)]
    tall = jnp.concatenate(parts, axis=0)
    wide = jnp.dot(tall.T, tall, precision=HIGH, preferred_element_type=F32)
    corr = wide[0:ROWS]
    for q in range(1, GROUP):
        at = STRIDE * q
        corr = corr + pltpu.roll(wide[at : at + ROWS], LANES - at, 1)

    sub8, ln8 = iota((8, LANES), 0), iota((8, LANES), 1)
    spread8 = lambda v: jnp.broadcast_to(v, (8, LANES))
    border = jnp.where(
        sub8 == 0, spread8(corr[32:33]), jnp.where(sub8 == 1, spread8(q_row), 0.0)
    )
    packed = pltpu.roll(border, 80, 1)
    for g, first, shift in ((3, 80, 48), (2, 72, 40), (1, 56, 24)):
        packed = jnp.where(ln8 < first, pltpu.roll(corr[8 * g : 8 * g + 8], shift, 1), packed)
    total = jnp.where(ln8 < 32, corr[0:8], packed)

    def send(buf, me, peers, index, value):
        buf[me] = value
        for device in peers:
            pltpu.make_async_remote_copy(
                src_ref=buf.at[me],
                dst_ref=buf.at[me],
                send_sem=send_sem.at[index],
                recv_sem=recv_sem.at[index],
                device_id=device,
                device_id_type=MESH,
            ).start()

    def receive(buf, count, index):
        rest = buf.at[pl.ds(0, count - 1)]
        pltpu.make_async_copy(rest, rest, recv_sem.at[index]).wait()
        return tree_sum(buf[k] for k in range(count))

    send(buf_x, x * NC + core, x_peers, 1, total)

    for g in range(TILES):
        for q in range(GROUP):
            block = pltpu.roll(parts[g], LANES - STRIDE * q, 1) if q else parts[g]
            red_ref[GROUP * g + q] = block[0:WIDTH, 0:WIDTH]

    total = receive(buf_x, NX * NC, 1)
    send(buf_y, y, y_peers, 2, total)
    total = receive(buf_y, NY, 2)
    send(buf_z, z, z_peers, 3, total)
    total = receive(buf_z, NZ, 3)

    border = pltpu.roll(total, LANES - 80, 1)
    moments = jnp.where(lane1 < WIDTH, border[1:2], 0.0) * INV_NF
    mean_sq = moments[:, 2 * PAIRS : 2 * PAIRS + 1]
    r_row, e_row = rows_from(moments)
    data_gram = assemble(
        tables, r_row, e_row, row_to_col(moments, 0), row_to_col(moments, PAIRS)
    )
    half = jnp.concatenate(
        [total]
        + [pltpu.roll(total, LANES - shift, 1) for shift in (24, 40, 48)]
        + [spread8(border[0:1])],
        axis=0,
    )
    square = jnp.concatenate([half, jnp.zeros((LANES - ROWS, LANES), F32)], axis=0)
    stored = ((lane < 2 * PAIRS) & (lane >= (row & ~7))) | (row >= 2 * PAIRS)
    correction = jnp.where(stored, half, square.T[0:ROWS])
    system = (data_gram - correction) * (1.0 / mean_sq)
    sys_ref[...] = system[0:WIDTH, 0:WIDTH]
    nrm_ref[...] = (mean * jnp.sqrt(mean_sq * (1.0 / ELEM_TOTAL)))[:, 0:WIDTH]

    for buf, count, index in (
        (pieces, NFREQ, 0), (buf_x, NX * NC, 1), (buf_y, NY, 2), (buf_z, NZ, 3), (buf_m, NZY, 4)
    ):
        rest = buf.at[pl.ds(0, count - 1)]
        pltpu.make_async_copy(rest, rest, send_sem.at[index]).wait()


def writer(red, sys, nrm, red_out, sys_out, nrm_out):
    red_out[...] = red[...]
    sys_out[...] = sys[...]
    nrm_out[...] = nrm[...]


def per_device(pole_freq, pole_damp, samples):
    vmem = lambda *shape: pltpu.VMEM(shape, F32)
    in_hbm = lambda v: pltpu.with_memory_space_constraint(v, pltpu.HBM)
    half = lambda *shape: pltpu.VMEM(shape, jnp.bfloat16)
    results = (
        vmem(OWN, WIDTH, WIDTH),
        vmem(WIDTH, WIDTH),
        vmem(1, WIDTH),
    )
    reduced, system, norm_row = pl.pallas_call(
        kernel,
        out_shape=results,
        in_specs=[pl.BlockSpec(memory_space=pltpu.HBM)] * 3,
        out_specs=(pl.BlockSpec(memory_space=pltpu.VMEM),) * 3,
        scratch_shapes=[
            pltpu.SMEM((PAIRS,), F32),
            pltpu.SMEM((PAIRS,), F32),
            vmem(2, FREQ_LOCAL, ELEM_LOCAL),
            half(2 * BASIS, FREQ_LOCAL),
            half(4 * PAIRS, FREQ_LOCAL),
            vmem(ELEM_LOCAL, LANES),
            vmem(NFREQ, 8, LANES),
            vmem(NFREQ, 8, LANES),
            vmem(NZY, 1, LANES),
            vmem(NX * NC, 8, LANES),
            vmem(NY, 8, LANES),
            vmem(NZ, 8, LANES),
            pltpu.SemaphoreType.DMA((2,)),
            pltpu.SemaphoreType.DMA((2, CHUNKS)),
            pltpu.SemaphoreType.DMA((5,)),
            pltpu.SemaphoreType.DMA((5,)),
        ],
        compiler_params=pltpu.CompilerParams(
            collective_id=0, has_side_effects=True, vmem_limit_bytes=40 * 1024 * 1024
        ),
    )(*(in_hbm(v) for v in (pole_freq, pole_damp, samples)))
    in_vmem = lambda v: pltpu.with_memory_space_constraint(v, pltpu.VMEM)
    reduced, system, norm_row = pl.pallas_call(
        writer,
        out_shape=(
            jax.ShapeDtypeStruct((OWN, WIDTH, WIDTH), F32),
            jax.ShapeDtypeStruct((WIDTH, WIDTH), F32),
            jax.ShapeDtypeStruct((1, WIDTH), F32),
        ),
        in_specs=[pl.BlockSpec(memory_space=pltpu.VMEM)] * 3,
        out_specs=(pl.BlockSpec(memory_space=pltpu.VMEM),) * 3,
        compiler_params=pltpu.CompilerParams(vmem_limit_bytes=48 * 1024 * 1024),
    )(in_vmem(reduced), in_vmem(system), in_vmem(norm_row))
    return jnp.transpose(reduced, (1, 2, 0)), system, norm_row.reshape(WIDTH)


def solution(mesh):
    placed = (P(), P(), P(None, "freq", "elem"))
    return jax.shard_map(
        per_device,
        mesh=mesh,
        in_specs=placed,
        out_specs=(P(None, None, ("elem", "freq")), P(), P()),
        check_vma=False,
    )
```

```python
import jax
import jax.numpy as jnp
from jax import lax
from jax.experimental import pallas as pl
from jax.experimental.pallas import tpu as pltpu
from jax.sharding import PartitionSpec as P

HIGH = lax.Precision.HIGHEST
MESH = pl.DeviceIdType.MESH
F32 = jnp.float32

NX, NZH, NZL, NY, NC = 4, 4, 2, 8, 2
NZ = NZH * NZL
NZY = NZL * NY
NFREQ = NZY * NC
QUAD = NZL * NC
PAIRS = 16
WIDTH = 2 * PAIRS + 1
ROWS = 40
BASIS = 48
OWN = 12
GROUP = 3
STRIDE = 40
TILES = OWN // GROUP
CHUNK = 256
CHUNKS = 4
LANES = 128
FREQ_LOCAL = 1024
ELEM_LOCAL = OWN * NFREQ
FREQ_TOTAL = FREQ_LOCAL * NFREQ
ELEM_TOTAL = ELEM_LOCAL * NX * NZH
INV_NF = 1.0 / FREQ_TOTAL


def iota(shape, dim):
    return lax.broadcasted_iota(jnp.int32, shape, dim)


def omega_of(half_position):
    return 0.02 + 0.98 * half_position / FREQ_TOTAL


def inverse_of(value):
    r = pltpu.reciprocal(value, approx=True)
    r = r * (2.0 - value * r)
    return r * (2.0 - value * r)


def split(value):
    high = value.astype(jnp.bfloat16)
    return high, (value - high.astype(F32)).astype(jnp.bfloat16)


def bf_dot(a, b):
    return jnp.dot(a, b, preferred_element_type=F32)


def wrap(value, size):
    return jnp.where(value >= size, value - size, value)


def tree_sum(values):
    values = list(values)
    while len(values) > 1:
        values = [a + b for a, b in zip(values[::2], values[1::2])] + values[len(values) & ~1 :]
    return values[0]


def pick(ref, index, shape):
    out = jnp.zeros(shape, F32)
    for m in range(PAIRS):
        out = jnp.where(index == m, ref[m], out)
    return out


def over_rows(col):
    return jnp.concatenate([col, col, jnp.zeros((8, LANES), F32)], axis=0)


def pair_coefs(ci, di, cj, dj, row_sum, col_sum):
    both = di + dj
    gap = cj - ci
    tot = ci + cj
    sq = both * both
    r1 = inverse_of(sq + gap * gap)
    r2 = inverse_of(sq + tot * tot)
    alpha, beta = both * r1, gap * r1
    gamma, delta = both * r2, -tot * r2
    ap, am = alpha + gamma, alpha - gamma
    bm, bp = beta - delta, beta + delta

    def table(di, bm, bp, row_sum, col_sum):
        ss, bd, bs, da = di * ap, di * bm, di * bp, di * am
        cr = jnp.where(row_sum, jnp.where(col_sum, ss, -bd), jnp.where(col_sum, bs, da))
        ce = jnp.where(row_sum, jnp.where(col_sum, bd, ss), jnp.where(col_sum, -da, bs))
        return cr, ce

    return table(di, bm, bp, row_sum, col_sum) + table(dj, -bp, -bm, col_sum, row_sum)


def coef_tables(c_col, d_col, pf, pd):
    shape = (ROWS, LANES)
    row, col = iota(shape, 0), iota(shape, 1)
    small = iota((8, LANES), 1) & (PAIRS - 1)
    cj, dj = pick(pf, small, (8, LANES)), pick(pd, small, (8, LANES))
    tall = lambda v: jnp.concatenate([v] * (ROWS // 8), axis=0)
    inside = (row < 2 * PAIRS) & (col < 2 * PAIRS)
    cr, ce, crt, cet = pair_coefs(
        over_rows(c_col), over_rows(d_col), tall(cj), tall(dj), row < PAIRS, col < PAIRS
    )
    last_row = row == 2 * PAIRS
    last_col = col == 2 * PAIRS
    one = lambda cond: jnp.where(cond, 1.0, 0.0).astype(F32)
    cr = jnp.where(inside, cr, one(last_row & ((col < PAIRS) | last_col)))
    ce = jnp.where(inside, ce, one(last_row & (col >= PAIRS) & (col < 2 * PAIRS)))
    crt = jnp.where(inside, crt, one(last_col & (row < PAIRS)))
    cet = jnp.where(inside, cet, one(last_col & (row >= PAIRS) & (row < 2 * PAIRS)))
    return cr, ce, crt, cet


def assemble(tables, r_row, e_row, r_col, e_col):
    cr, ce, crt, cet = tables
    return cr * r_row + ce * e_row + crt * over_rows(r_col) + cet * over_rows(e_col)


def row_to_col(row_vec, first):
    row, lane = iota((PAIRS, LANES), 0), iota((PAIRS, LANES), 1)
    kept = jnp.where(lane == row + first, jnp.broadcast_to(row_vec, (PAIRS, LANES)), 0.0)
    return jnp.broadcast_to(jnp.sum(kept, axis=1, keepdims=True), (PAIRS, LANES))


def rows_from(values):
    lane = iota(values.shape, 1)
    j = lane - jnp.where(lane >= 2 * STRIDE, 2 * STRIDE, jnp.where(lane >= STRIDE, STRIDE, 0))
    r_row = jnp.where(
        j < PAIRS,
        values,
        jnp.where(j < 2 * PAIRS, pltpu.roll(values, PAIRS, 1), jnp.where(j == 2 * PAIRS, values, 0.0)),
    )
    e_row = jnp.where(
        j < PAIRS,
        pltpu.roll(values, LANES - PAIRS, 1),
        jnp.where(j < 2 * PAIRS, values, 0.0),
    )
    return r_row, e_row


def eliminate(work):
    parts = [work[8 * b : 8 * b + 8] for b in range(ROWS // 8)]
    sub = iota((8, LANES), 0)
    for first in range(0, WIDTH, 8):
        count = min(8, WIDTH - first)
        b0 = first // 8
        live = range(b0, len(parts))
        cols = [
            [jnp.broadcast_to(parts[b][:, first + t : first + t + 1], (8, LANES)) for b in live]
            for t in range(count)
        ]
        rows = [parts[b0][t : t + 1, :] for t in range(count)]
        for t in range(count):
            inv = inverse_of(cols[t][0][t : t + 1, :])
            factor = [v * inv for v in cols[t]]
            factor[0] = jnp.where(sub > t, factor[0], 0.0)
            for u in range(t + 1, count):
                lead = cols[u][0][t : t + 1, :]
                cols[u] = [v - f * lead for v, f in zip(cols[u], factor)]
                rows[u] = rows[u] - factor[0][u : u + 1, :] * rows[t]
            for n, b in enumerate(live):
                parts[b] = parts[b] - factor[n] * rows[t]
    return jnp.concatenate(parts, axis=0)


def kernel(
    pf_hbm, pd_hbm, s_hbm, red_ref, sys_ref, nrm_ref,
    pf, pd, s_buf, re_buf, im_buf, xt_buf, pieces, recv_b,
    buf_m, buf_x, buf_y, buf_z,
    pole_sem, load_sem, send_sem, recv_sem,
):
    elem, freq = lax.axis_index("elem"), lax.axis_index("freq")
    x, z_hi = elem // NZH, elem % NZH
    zy, core = freq // NC, freq % NC
    z_lo, y = zy // NY, zy % NY
    z = z_hi * NZL + z_lo

    def at_freq(other):
        return {"elem": elem, "freq": other}

    def at_y(other):
        return {"elem": elem, "freq": (z_lo * NY + other) * NC + core}

    z_peers = []
    for dz in range(NZH):
        for low in range(NZL):
            if dz or low:
                hi, lo = wrap(z_hi + dz, NZH), wrap(z_lo + low, NZL)
                z_peers.append({"elem": x * NZH + hi, "freq": (lo * NY + y) * NC + core})
    x_peers = []
    for dx in range(NX):
        for c in range(NC):
            if dx or c:
                to = wrap(x + dx, NX)
                x_peers.append({"elem": to * NZH + z_hi, "freq": zy * NC + wrap(core + c, NC)})
    y_peers = [at_y(wrap(y + dy, NY)) for dy in range(1, NY)]

    pole_loads = [
        pltpu.make_async_copy(pf_hbm, pf, pole_sem.at[0]),
        pltpu.make_async_copy(pd_hbm, pd, pole_sem.at[1]),
    ]
    for load in pole_loads:
        load.start()
    loads = {}
    for k in range(CHUNKS):
        for part in range(2):
            at = pl.ds(k * CHUNK, CHUNK)
            loads[part, k] = pltpu.make_async_copy(
                s_hbm.at[part, at], s_buf.at[part, at], load_sem.at[part, k]
            )
            loads[part, k].start()

    barrier = pltpu.get_barrier_semaphore()

    def greet(device):
        pl.semaphore_signal(barrier, inc=1, device_id=device, device_id_type=MESH)

    for step in range(1, NFREQ):
        greet(at_freq(wrap(freq + step, NFREQ)))
    for device in z_peers[NZL - 1 :] + x_peers[NC - 1 :]:
        greet(device)
    greeted = NFREQ - 1 + len(z_peers) - (NZL - 1) + len(x_peers) - (NC - 1)

    for load in pole_loads:
        load.wait()

    column = iota((PAIRS, LANES), 0)
    c_col = pick(pf, column, (PAIRS, LANES))
    d_col = pick(pd, column, (PAIRS, LANES))
    d_sq = d_col * d_col
    half16 = iota((PAIRS, LANES), 1).astype(F32) + 0.5
    base = (freq * FREQ_LOCAL).astype(F32)
    ones = jnp.where(iota((PAIRS, FREQ_LOCAL), 0) == 0, 1.0, 0.0)
    re_buf[2 * PAIRS : BASIS, :] = ones.astype(jnp.bfloat16)
    re_buf[BASIS + 2 * PAIRS :, :] = jnp.zeros((PAIRS, FREQ_LOCAL), jnp.bfloat16)
    for tile in range(FREQ_LOCAL // LANES):
        at = pl.ds(tile * LANES, LANES)
        w = omega_of(half16 + (base + tile * LANES))
        below, above = w - c_col, w + c_col
        i1 = inverse_of(d_sq + below * below)
        i2 = inverse_of(d_sq + above * above)
        first, second = below * i1, above * i2
        re_buf[0:PAIRS, at], re_buf[BASIS : BASIS + PAIRS, at] = split(d_sq * (i1 + i2))
        re_buf[PAIRS : 2 * PAIRS, at], re_buf[BASIS + PAIRS : BASIS + 2 * PAIRS, at] = split(
            d_col * (first - second)
        )
        im_buf[0:PAIRS, at], im_buf[2 * PAIRS : 3 * PAIRS, at] = split(-d_col * (first + second))
        im_buf[PAIRS : 2 * PAIRS, at], im_buf[3 * PAIRS :, at] = split(d_sq * (i1 - i2))

    quad = z_lo * NC + core
    share = NFREQ // QUAD
    halves = [slice(0, 8), slice(8, 16)]

    def mean_step(step, acc):
        acc = list(acc)
        start = ((quad * share + step) * FREQ_LOCAL).astype(F32)
        for tile in range(FREQ_LOCAL // LANES):
            w = omega_of(half16[0:8] + (start + tile * LANES))
            for h in range(2):
                below, above = w - c_col[halves[h]], w + c_col[halves[h]]
                n1 = d_sq[halves[h]] + below * below
                n2 = d_sq[halves[h]] + above * above
                r = inverse_of(n1 * n2)
                acc[2 * h] = acc[2 * h] + r * (n1 + n2)
                acc[2 * h + 1] = acc[2 * h + 1] + r * (below * n2 - above * n1)
        return tuple(acc)

    acc = lax.fori_loop(0, share, mean_step, (jnp.zeros((8, LANES), F32),) * 4)
    lane16 = iota((PAIRS, LANES), 1)
    sum_r = d_sq * jnp.sum(jnp.concatenate([acc[0], acc[2]], axis=0), axis=1, keepdims=True)
    sum_e = d_col * jnp.sum(jnp.concatenate([acc[1], acc[3]], axis=0), axis=1, keepdims=True)
    sums = jnp.where(lane16 == column, sum_r, jnp.where(lane16 == column + PAIRS, sum_e, 0.0))
    buf_m[quad] = jnp.sum(sums, axis=0, keepdims=True)

    x0 = jnp.zeros((BASIS, ELEM_LOCAL + LANES), F32)
    x1 = jnp.zeros((2 * PAIRS, ELEM_LOCAL), F32)
    for k in range(CHUNKS):
        at = pl.ds(k * CHUNK, CHUNK)
        loads[0, k].wait()
        loads[1, k].wait()
        s0, s1 = s_buf[0, at, :], s_buf[1, at, :]
        squares = s0 * s0 + s1 * s1
        power = tree_sum(squares[:, t * LANES : (t + 1) * LANES] for t in range(ELEM_LOCAL // LANES))
        high, low = split(jnp.concatenate([s0, power], axis=1))
        both = bf_dot(re_buf[:, at], high)
        x0 = x0 + (both[0:BASIS] + both[BASIS:] + bf_dot(re_buf[0:BASIS, at], low))
        high, low = split(s1)
        both = bf_dot(im_buf[:, at], high)
        x1 = x1 + (both[0 : 2 * PAIRS] + both[2 * PAIRS :] + bf_dot(im_buf[0 : 2 * PAIRS, at], low))
    x0, q = x0[:, 0:ELEM_LOCAL], x0[0:ROWS, ELEM_LOCAL:]

    stacked = jnp.concatenate(
        [
            x0,
            jnp.zeros((64 - BASIS, ELEM_LOCAL), F32),
            x1,
            jnp.zeros((LANES - 64 - 2 * PAIRS, ELEM_LOCAL), F32),
        ],
        axis=0,
    )
    for tile in range(ELEM_LOCAL // LANES):
        at = slice(tile * LANES, (tile + 1) * LANES)
        xt_buf[at, :] = stacked[:, at].T
    count = ELEM_LOCAL // GROUP
    thirds = [xt_buf[pl.ds(q, count, stride=GROUP), :] for q in range(GROUP)]
    lane_c = iota((count, LANES), 1)

    def spread(shift):
        rolled = [
            pltpu.roll(thirds[q], (STRIDE * q + shift) % LANES, 1) if (STRIDE * q + shift) % LANES else thirds[q]
            for q in range(GROUP)
        ]
        return jnp.where(
            lane_c < STRIDE, rolled[0], jnp.where(lane_c < 2 * STRIDE, rolled[1], rolled[2])
        )

    part0, part1 = spread(0), spread(64)
    upper = iota((8, LANES), 0) < 4
    for k in range(NZY):
        v0, v1 = part0[8 * k : 8 * k + 8], part1[8 * k : 8 * k + 8]
        pieces[NC * k] = jnp.where(upper, v0, pltpu.roll(v1, 4, 0))
        pieces[NC * k + 1] = jnp.where(upper, pltpu.roll(v0, 4, 0), v1)

    pl.semaphore_wait(barrier, greeted)

    for step in range(1, QUAD):
        lo, c = wrap(z_lo + step // NC, NZL), wrap(core + step % NC, NC)
        pltpu.make_async_remote_copy(
            src_ref=buf_m.at[quad],
            dst_ref=buf_m.at[quad],
            send_sem=send_sem.at[4],
            recv_sem=recv_sem.at[4],
            device_id=at_freq((lo * NY + y) * NC + c),
            device_id_type=MESH,
        ).start()

    for step in range(1, NFREQ):
        other = wrap(freq + step, NFREQ)
        pltpu.make_async_remote_copy(
            src_ref=pieces.at[other],
            dst_ref=recv_b.at[freq],
            send_sem=send_sem.at[0],
            recv_sem=recv_sem.at[0],
            device_id=at_freq(other),
            device_id_type=MESH,
        ).start()
    recv_b[freq] = pieces[freq]

    tables = coef_tables(c_col, d_col, pf, pd)
    rest = buf_m.at[pl.ds(0, QUAD - 1)]
    pltpu.make_async_copy(rest, rest, recv_sem.at[4]).wait()
    mean = tree_sum(buf_m[k] for k in range(QUAD)) * INV_NF
    lane1 = iota((1, LANES), 1)
    mean = jnp.where(lane1 == 2 * PAIRS, 1.0, mean)
    r_row, e_row = rows_from(mean)
    gram = assemble(tables, r_row, e_row, row_to_col(mean, 0), row_to_col(mean, PAIRS))
    row, lane = iota((ROWS, LANES), 0), iota((ROWS, LANES), 1)
    work = gram + jnp.where((lane == row + 64) & (row < WIDTH), 1.0, 0.0)
    work = eliminate(work)
    pivots = jnp.sum(jnp.where((lane == row) & (row < WIDTH), work, 0.0), axis=1, keepdims=True)
    pivots = jnp.where(iota((ROWS, 1), 0) < WIDTH, pivots, 1.0)
    inverse = pltpu.roll(work, 64, 1) * (1.0 / jnp.sqrt(pivots))
    inverse = jnp.where(lane < WIDTH, inverse, 0.0)

    q = jnp.broadcast_to(jnp.sum(q, axis=1, keepdims=True), (ROWS, LANES))
    q_row = jnp.sum(jnp.where(lane == row, q, 0.0), axis=0, keepdims=True)

    triple = [
        v + pltpu.roll(v, STRIDE, 1) + pltpu.roll(v, 2 * STRIDE, 1) for v in tables
    ]

    rest_b = recv_b.at[pl.ds(0, NFREQ - 1)]
    pltpu.make_async_copy(rest_b, rest_b, recv_sem.at[0]).wait()
    owned = tree_sum(recv_b[k] for k in range(NFREQ))
    owned = owned * (-INV_NF)

    other_part = pltpu.roll(owned, 4, 0)
    plus, minus = owned + other_part, owned - other_part
    r_rows, e_rows = rows_from(minus)
    plus_t = jnp.concatenate([plus, jnp.zeros((LANES - 8, LANES), F32)], axis=0).T
    lane16 = iota((PAIRS, LANES), 1)

    def columns(g, first):
        spread_col = [
            jnp.broadcast_to(
                plus_t[STRIDE * q + first : STRIDE * q + first + PAIRS, g : g + 1], (PAIRS, LANES)
            )
            for q in range(GROUP)
        ]
        return jnp.where(
            lane16 < STRIDE, spread_col[0], jnp.where(lane16 < 2 * STRIDE, spread_col[1], spread_col[2])
        )

    coupling = jnp.concatenate(
        [
            assemble(triple, r_rows[g : g + 1, :], e_rows[g : g + 1, :], columns(g, 0), columns(g, PAIRS))
            for g in range(TILES)
        ],
        axis=1,
    )
    reduced = jnp.dot(
        inverse[:, 0:ROWS], coupling, precision=HIGH, preferred_element_type=F32
    )
    parts = [reduced[:, g * LANES : (g + 1) * LANES] for g in range(TILES)]
    tall = jnp.concatenate(parts, axis=0)
    wide = jnp.dot(tall.T, tall, precision=HIGH, preferred_element_type=F32)
    corr = wide[0:ROWS]
    for q in range(1, GROUP):
        at = STRIDE * q
        corr = corr + pltpu.roll(wide[at : at + ROWS], LANES - at, 1)

    sub8, ln8 = iota((8, LANES), 0), iota((8, LANES), 1)
    spread8 = lambda v: jnp.broadcast_to(v, (8, LANES))
    border = jnp.where(
        sub8 == 0, spread8(corr[32:33]), jnp.where(sub8 == 1, spread8(q_row), 0.0)
    )
    packed = pltpu.roll(border, 80, 1)
    for g, first, shift in ((3, 80, 48), (2, 72, 40), (1, 56, 24)):
        packed = jnp.where(ln8 < first, pltpu.roll(corr[8 * g : 8 * g + 8], shift, 1), packed)
    total = jnp.where(ln8 < 32, corr[0:8], packed)

    def send(buf, me, peers, index, value):
        buf[me] = value
        for device in peers:
            pltpu.make_async_remote_copy(
                src_ref=buf.at[me],
                dst_ref=buf.at[me],
                send_sem=send_sem.at[index],
                recv_sem=recv_sem.at[index],
                device_id=device,
                device_id_type=MESH,
            ).start()

    def receive(buf, count, index):
        rest = buf.at[pl.ds(0, count - 1)]
        pltpu.make_async_copy(rest, rest, recv_sem.at[index]).wait()
        return tree_sum(buf[k] for k in range(count))

    send(buf_x, x * NC + core, x_peers, 1, total)

    for g in range(TILES):
        for q in range(GROUP):
            block = pltpu.roll(parts[g], LANES - STRIDE * q, 1) if q else parts[g]
            red_ref[GROUP * g + q] = block[0:WIDTH, 0:WIDTH]

    total = receive(buf_x, NX * NC, 1)
    send(buf_y, y, y_peers, 2, total)
    total = receive(buf_y, NY, 2)
    send(buf_z, z, z_peers, 3, total)
    total = receive(buf_z, NZ, 3)

    border = pltpu.roll(total, LANES - 80, 1)
    moments = jnp.where(lane1 < WIDTH, border[1:2], 0.0) * INV_NF
    mean_sq = moments[:, 2 * PAIRS : 2 * PAIRS + 1]
    r_row, e_row = rows_from(moments)
    data_gram = assemble(
        tables, r_row, e_row, row_to_col(moments, 0), row_to_col(moments, PAIRS)
    )
    half = jnp.concatenate(
        [total]
        + [pltpu.roll(total, LANES - shift, 1) for shift in (24, 40, 48)]
        + [spread8(border[0:1])],
        axis=0,
    )
    square = jnp.concatenate([half, jnp.zeros((LANES - ROWS, LANES), F32)], axis=0)
    stored = ((lane < 2 * PAIRS) & (lane >= (row & ~7))) | (row >= 2 * PAIRS)
    correction = jnp.where(stored, half, square.T[0:ROWS])
    system = (data_gram - correction) * (1.0 / mean_sq)
    sys_ref[...] = system[0:WIDTH, 0:WIDTH]
    nrm_ref[...] = (mean * jnp.sqrt(mean_sq * (1.0 / ELEM_TOTAL)))[:, 0:WIDTH]

    for buf, count, index in (
        (pieces, NFREQ, 0), (buf_x, NX * NC, 1), (buf_y, NY, 2), (buf_z, NZ, 3), (buf_m, QUAD, 4)
    ):
        rest = buf.at[pl.ds(0, count - 1)]
        pltpu.make_async_copy(rest, rest, send_sem.at[index]).wait()


def writer(red, sys, nrm, red_out, sys_out, nrm_out):
    red_out[...] = red[...]
    sys_out[...] = sys[...]
    nrm_out[...] = nrm[...]


def per_device(pole_freq, pole_damp, samples):
    vmem = lambda *shape: pltpu.VMEM(shape, F32)
    in_hbm = lambda v: pltpu.with_memory_space_constraint(v, pltpu.HBM)
    half = lambda *shape: pltpu.VMEM(shape, jnp.bfloat16)
    results = (
        vmem(OWN, WIDTH, WIDTH),
        vmem(WIDTH, WIDTH),
        vmem(1, WIDTH),
    )
    reduced, system, norm_row = pl.pallas_call(
        kernel,
        out_shape=results,
        in_specs=[pl.BlockSpec(memory_space=pltpu.HBM)] * 3,
        out_specs=(pl.BlockSpec(memory_space=pltpu.VMEM),) * 3,
        scratch_shapes=[
            pltpu.SMEM((PAIRS,), F32),
            pltpu.SMEM((PAIRS,), F32),
            vmem(2, FREQ_LOCAL, ELEM_LOCAL),
            half(2 * BASIS, FREQ_LOCAL),
            half(4 * PAIRS, FREQ_LOCAL),
            vmem(ELEM_LOCAL, LANES),
            vmem(NFREQ, 8, LANES),
            vmem(NFREQ, 8, LANES),
            vmem(QUAD, 1, LANES),
            vmem(NX * NC, 8, LANES),
            vmem(NY, 8, LANES),
            vmem(NZ, 8, LANES),
            pltpu.SemaphoreType.DMA((2,)),
            pltpu.SemaphoreType.DMA((2, CHUNKS)),
            pltpu.SemaphoreType.DMA((5,)),
            pltpu.SemaphoreType.DMA((5,)),
        ],
        compiler_params=pltpu.CompilerParams(
            collective_id=0, has_side_effects=True, vmem_limit_bytes=40 * 1024 * 1024
        ),
    )(*(in_hbm(v) for v in (pole_freq, pole_damp, samples)))
    in_vmem = lambda v: pltpu.with_memory_space_constraint(v, pltpu.VMEM)
    reduced, system, norm_row = pl.pallas_call(
        writer,
        out_shape=(
            jax.ShapeDtypeStruct((OWN, WIDTH, WIDTH), F32),
            jax.ShapeDtypeStruct((WIDTH, WIDTH), F32),
            jax.ShapeDtypeStruct((1, WIDTH), F32),
        ),
        in_specs=[pl.BlockSpec(memory_space=pltpu.VMEM)] * 3,
        out_specs=(pl.BlockSpec(memory_space=pltpu.VMEM),) * 3,
        compiler_params=pltpu.CompilerParams(vmem_limit_bytes=48 * 1024 * 1024),
    )(in_vmem(reduced), in_vmem(system), in_vmem(norm_row))
    return jnp.transpose(reduced, (1, 2, 0)), system, norm_row.reshape(WIDTH)


def solution(mesh):
    placed = (P(), P(), P(None, "freq", "elem"))
    return jax.shard_map(
        per_device,
        mesh=mesh,
        in_specs=placed,
        out_specs=(P(None, None, ("elem", "freq")), P(), P()),
        check_vma=False,
    )
```

```python
import jax
import jax.numpy as jnp
from jax import lax
from jax.experimental import pallas as pl
from jax.experimental.pallas import tpu as pltpu
from jax.sharding import PartitionSpec as P

HIGH = lax.Precision.HIGHEST
MESH = pl.DeviceIdType.MESH
F32 = jnp.float32

NX, NZH, NZL, NY, NC = 4, 4, 2, 8, 2
NZ = NZH * NZL
NZY = NZL * NY
NFREQ = NZY * NC
QUAD = NZL * NC
PAIRS = 16
WIDTH = 2 * PAIRS + 1
ROWS = 40
BASIS = 48
OWN = 12
GROUP = 3
STRIDE = 40
TILES = OWN // GROUP
CHUNK = 256
CHUNKS = 4
LANES = 128
FREQ_LOCAL = 1024
ELEM_LOCAL = OWN * NFREQ
FREQ_TOTAL = FREQ_LOCAL * NFREQ
ELEM_TOTAL = ELEM_LOCAL * NX * NZH
INV_NF = 1.0 / FREQ_TOTAL


def iota(shape, dim):
    return lax.broadcasted_iota(jnp.int32, shape, dim)


def omega_of(half_position):
    return 0.02 + 0.98 * half_position / FREQ_TOTAL


def inverse_of(value):
    r = pltpu.reciprocal(value, approx=True)
    r = r * (2.0 - value * r)
    return r * (2.0 - value * r)


def split(value):
    high = value.astype(jnp.bfloat16)
    return high, (value - high.astype(F32)).astype(jnp.bfloat16)


def bf_dot(a, b):
    return jnp.dot(a, b, preferred_element_type=F32)


def wrap(value, size):
    return jnp.where(value >= size, value - size, value)


def tree_sum(values):
    values = list(values)
    while len(values) > 1:
        values = [a + b for a, b in zip(values[::2], values[1::2])] + values[len(values) & ~1 :]
    return values[0]


def pick(ref, index, shape):
    out = jnp.zeros(shape, F32)
    for m in range(PAIRS):
        out = jnp.where(index == m, ref[m], out)
    return out


def over_rows(col):
    return jnp.concatenate([col, col, jnp.zeros((8, LANES), F32)], axis=0)


def pair_coefs(ci, di, cj, dj, row_sum, col_sum):
    both = di + dj
    gap = cj - ci
    tot = ci + cj
    sq = both * both
    r1 = inverse_of(sq + gap * gap)
    r2 = inverse_of(sq + tot * tot)
    alpha, beta = both * r1, gap * r1
    gamma, delta = both * r2, -tot * r2
    ap, am = alpha + gamma, alpha - gamma
    bm, bp = beta - delta, beta + delta

    def table(di, bm, bp, row_sum, col_sum):
        ss, bd, bs, da = di * ap, di * bm, di * bp, di * am
        cr = jnp.where(row_sum, jnp.where(col_sum, ss, -bd), jnp.where(col_sum, bs, da))
        ce = jnp.where(row_sum, jnp.where(col_sum, bd, ss), jnp.where(col_sum, -da, bs))
        return cr, ce

    return table(di, bm, bp, row_sum, col_sum) + table(dj, -bp, -bm, col_sum, row_sum)


def coef_tables(c_col, d_col, pf, pd):
    shape = (ROWS, LANES)
    row, col = iota(shape, 0), iota(shape, 1)
    small = iota((8, LANES), 1) & (PAIRS - 1)
    cj, dj = pick(pf, small, (8, LANES)), pick(pd, small, (8, LANES))
    tall = lambda v: jnp.concatenate([v] * (ROWS // 8), axis=0)
    inside = (row < 2 * PAIRS) & (col < 2 * PAIRS)
    cr, ce, crt, cet = pair_coefs(
        over_rows(c_col), over_rows(d_col), tall(cj), tall(dj), row < PAIRS, col < PAIRS
    )
    last_row = row == 2 * PAIRS
    last_col = col == 2 * PAIRS
    one = lambda cond: jnp.where(cond, 1.0, 0.0).astype(F32)
    cr = jnp.where(inside, cr, one(last_row & ((col < PAIRS) | last_col)))
    ce = jnp.where(inside, ce, one(last_row & (col >= PAIRS) & (col < 2 * PAIRS)))
    crt = jnp.where(inside, crt, one(last_col & (row < PAIRS)))
    cet = jnp.where(inside, cet, one(last_col & (row >= PAIRS) & (row < 2 * PAIRS)))
    return cr, ce, crt, cet


def assemble(tables, r_row, e_row, r_col, e_col):
    cr, ce, crt, cet = tables
    return cr * r_row + ce * e_row + crt * over_rows(r_col) + cet * over_rows(e_col)


def row_to_col(row_vec, first):
    row, lane = iota((PAIRS, LANES), 0), iota((PAIRS, LANES), 1)
    kept = jnp.where(lane == row + first, jnp.broadcast_to(row_vec, (PAIRS, LANES)), 0.0)
    return jnp.broadcast_to(jnp.sum(kept, axis=1, keepdims=True), (PAIRS, LANES))


def rows_from(values):
    lane = iota(values.shape, 1)
    j = lane - jnp.where(lane >= 2 * STRIDE, 2 * STRIDE, jnp.where(lane >= STRIDE, STRIDE, 0))
    r_row = jnp.where(
        j < PAIRS,
        values,
        jnp.where(j < 2 * PAIRS, pltpu.roll(values, PAIRS, 1), jnp.where(j == 2 * PAIRS, values, 0.0)),
    )
    e_row = jnp.where(
        j < PAIRS,
        pltpu.roll(values, LANES - PAIRS, 1),
        jnp.where(j < 2 * PAIRS, values, 0.0),
    )
    return r_row, e_row


def eliminate(work):
    parts = [work[8 * b : 8 * b + 8] for b in range(ROWS // 8)]
    sub = iota((8, LANES), 0)
    for first in range(0, WIDTH, 8):
        count = min(8, WIDTH - first)
        b0 = first // 8
        live = range(b0, len(parts))
        cols = [
            [jnp.broadcast_to(parts[b][:, first + t : first + t + 1], (8, LANES)) for b in live]
            for t in range(count)
        ]
        rows = [parts[b0][t : t + 1, :] for t in range(count)]
        for t in range(count):
            inv = inverse_of(cols[t][0][t : t + 1, :])
            factor = [v * inv for v in cols[t]]
            factor[0] = jnp.where(sub > t, factor[0], 0.0)
            for u in range(t + 1, count):
                lead = cols[u][0][t : t + 1, :]
                cols[u] = [v - f * lead for v, f in zip(cols[u], factor)]
                rows[u] = rows[u] - factor[0][u : u + 1, :] * rows[t]
            for n, b in enumerate(live):
                parts[b] = parts[b] - factor[n] * rows[t]
    return jnp.concatenate(parts, axis=0)


def kernel(
    pf_hbm, pd_hbm, s_hbm, red_ref, sys_ref, nrm_ref,
    pf, pd, s_buf, re_buf, im_buf, xt_buf, pieces, recv_a, sum_a, recv_b,
    buf_m, buf_x, buf_y, buf_z,
    pole_sem, load_sem, send_sem, recv_sem,
):
    elem, freq = lax.axis_index("elem"), lax.axis_index("freq")
    x, z_hi = elem // NZH, elem % NZH
    zy, core = freq // NC, freq % NC
    z_lo, y = zy // NY, zy % NY
    z = z_hi * NZL + z_lo

    def at_freq(other):
        return {"elem": elem, "freq": other}

    def at_y(other):
        return {"elem": elem, "freq": (z_lo * NY + other) * NC + core}

    def far_first(size):
        return sorted(range(size), key=lambda d: -min(d, size - d))

    sibling = at_freq(zy * NC + (1 - core))
    zy_peers = [
        wrap(z_lo + dz, NZL) * NY + wrap(y + dy, NY)
        for dy in far_first(NY)
        for dz in (1, 0)
        if dy or dz
    ]
    y_peers = [at_y(wrap(y + dy, NY)) for dy in far_first(NY) if dy]
    z_peers = []
    for dz in far_first(NZ):
        if dz:
            to = wrap(z + dz, NZ)
            hi = to // NZL
            z_peers.append({"elem": x * NZH + hi, "freq": ((to - hi * NZL) * NY + y) * NC + core})
    x_peers = []
    for dx in far_first(NX):
        for c in (1, 0):
            if dx or c:
                to = wrap(x + dx, NX)
                x_peers.append({"elem": to * NZH + z_hi, "freq": zy * NC + wrap(core + c, NC)})
    corner = at_freq((wrap(z_lo + 1, NZL) * NY + y) * NC + (1 - core))

    pole_loads = [
        pltpu.make_async_copy(pf_hbm, pf, pole_sem.at[0]),
        pltpu.make_async_copy(pd_hbm, pd, pole_sem.at[1]),
    ]
    for load in pole_loads:
        load.start()
    loads = {}
    for k in range(CHUNKS):
        for part in range(2):
            at = pl.ds(k * CHUNK, CHUNK)
            loads[part, k] = pltpu.make_async_copy(
                s_hbm.at[part, at], s_buf.at[part, at], load_sem.at[part, k]
            )
            loads[part, k].start()

    barrier = pltpu.get_barrier_semaphore()

    def greet(device):
        pl.semaphore_signal(barrier, inc=1, device_id=device, device_id_type=MESH)

    z_rest = []
    for hi_step in range(1, NZH):
        hi = wrap(z_hi + hi_step, NZH)
        z_rest += [{"elem": x * NZH + hi, "freq": (lo * NY + y) * NC + core} for lo in range(NZL)]
    greets = [at_freq(zy_peer * NC + core) for zy_peer in zy_peers]
    greets += [corner] + z_rest + x_peers
    for device in greets:
        greet(device)
    greeted = len(greets)

    for load in pole_loads:
        load.wait()

    column = iota((PAIRS, LANES), 0)
    c_col = pick(pf, column, (PAIRS, LANES))
    d_col = pick(pd, column, (PAIRS, LANES))
    d_sq = d_col * d_col
    half16 = iota((PAIRS, LANES), 1).astype(F32) + 0.5
    base = (freq * FREQ_LOCAL).astype(F32)
    ones = jnp.where(iota((PAIRS, FREQ_LOCAL), 0) == 0, 1.0, 0.0)
    re_buf[2 * PAIRS : BASIS, :] = ones.astype(jnp.bfloat16)
    re_buf[BASIS + 2 * PAIRS :, :] = jnp.zeros((PAIRS, FREQ_LOCAL), jnp.bfloat16)
    for tile in range(FREQ_LOCAL // LANES):
        at = pl.ds(tile * LANES, LANES)
        w = omega_of(half16 + (base + tile * LANES))
        below, above = w - c_col, w + c_col
        i1 = inverse_of(d_sq + below * below)
        i2 = inverse_of(d_sq + above * above)
        first, second = below * i1, above * i2
        re_buf[0:PAIRS, at], re_buf[BASIS : BASIS + PAIRS, at] = split(d_sq * (i1 + i2))
        re_buf[PAIRS : 2 * PAIRS, at], re_buf[BASIS + PAIRS : BASIS + 2 * PAIRS, at] = split(
            d_col * (first - second)
        )
        im_buf[0:PAIRS, at], im_buf[2 * PAIRS : 3 * PAIRS, at] = split(-d_col * (first + second))
        im_buf[PAIRS : 2 * PAIRS, at], im_buf[3 * PAIRS :, at] = split(d_sq * (i1 - i2))

    quad = z_lo * NC + core
    share = NFREQ // QUAD
    halves = [slice(0, 8), slice(8, 16)]

    def mean_step(step, acc):
        acc = list(acc)
        start = ((quad * share + step) * FREQ_LOCAL).astype(F32)
        for tile in range(FREQ_LOCAL // LANES):
            w = omega_of(half16[0:8] + (start + tile * LANES))
            for h in range(2):
                below, above = w - c_col[halves[h]], w + c_col[halves[h]]
                n1 = d_sq[halves[h]] + below * below
                n2 = d_sq[halves[h]] + above * above
                r = inverse_of(n1 * n2)
                acc[2 * h] = acc[2 * h] + r * (n1 + n2)
                acc[2 * h + 1] = acc[2 * h + 1] + r * (below * n2 - above * n1)
        return tuple(acc)

    acc = lax.fori_loop(0, share, mean_step, (jnp.zeros((8, LANES), F32),) * 4)
    lane16 = iota((PAIRS, LANES), 1)
    sum_r = d_sq * jnp.sum(jnp.concatenate([acc[0], acc[2]], axis=0), axis=1, keepdims=True)
    sum_e = d_col * jnp.sum(jnp.concatenate([acc[1], acc[3]], axis=0), axis=1, keepdims=True)
    sums = jnp.where(lane16 == column, sum_r, jnp.where(lane16 == column + PAIRS, sum_e, 0.0))
    buf_m[quad] = jnp.sum(sums, axis=0, keepdims=True)

    x0 = jnp.zeros((BASIS, ELEM_LOCAL + LANES), F32)
    x1 = jnp.zeros((2 * PAIRS, ELEM_LOCAL), F32)
    for k in range(CHUNKS):
        at = pl.ds(k * CHUNK, CHUNK)
        loads[0, k].wait()
        loads[1, k].wait()
        s0, s1 = s_buf[0, at, :], s_buf[1, at, :]
        squares = s0 * s0 + s1 * s1
        power = tree_sum(squares[:, t * LANES : (t + 1) * LANES] for t in range(ELEM_LOCAL // LANES))
        high, low = split(jnp.concatenate([s0, power], axis=1))
        both = bf_dot(re_buf[:, at], high)
        x0 = x0 + (both[0:BASIS] + both[BASIS:] + bf_dot(re_buf[0:BASIS, at], low))
        high, low = split(s1)
        both = bf_dot(im_buf[:, at], high)
        x1 = x1 + (both[0 : 2 * PAIRS] + both[2 * PAIRS :] + bf_dot(im_buf[0 : 2 * PAIRS, at], low))
    x0, q = x0[:, 0:ELEM_LOCAL], x0[0:ROWS, ELEM_LOCAL:]

    stacked = jnp.concatenate(
        [
            x0,
            jnp.zeros((64 - BASIS, ELEM_LOCAL), F32),
            x1,
            jnp.zeros((LANES - 64 - 2 * PAIRS, ELEM_LOCAL), F32),
        ],
        axis=0,
    )
    for tile in range(ELEM_LOCAL // LANES):
        at = slice(tile * LANES, (tile + 1) * LANES)
        xt_buf[at, :] = stacked[:, at].T
    count = ELEM_LOCAL // GROUP
    thirds = [xt_buf[pl.ds(q, count, stride=GROUP), :] for q in range(GROUP)]
    lane_c = iota((count, LANES), 1)

    def spread(shift):
        rolled = [
            pltpu.roll(thirds[q], (STRIDE * q + shift) % LANES, 1) if (STRIDE * q + shift) % LANES else thirds[q]
            for q in range(GROUP)
        ]
        return jnp.where(
            lane_c < STRIDE, rolled[0], jnp.where(lane_c < 2 * STRIDE, rolled[1], rolled[2])
        )

    part0, part1 = spread(0), spread(64)
    upper = iota((8, LANES), 0) < 4
    for k in range(NZY):
        v0, v1 = part0[8 * k : 8 * k + 8], part1[8 * k : 8 * k + 8]
        pieces[0, k] = jnp.where(upper, v0, pltpu.roll(v1, 4, 0))
        pieces[1, k] = jnp.where(upper, pltpu.roll(v0, 4, 0), v1)

    pl.semaphore_wait(barrier, greeted)

    copy_a = pltpu.make_async_remote_copy(
        src_ref=pieces.at[1 - core],
        dst_ref=recv_a,
        send_sem=send_sem.at[5],
        recv_sem=recv_sem.at[5],
        device_id=sibling,
        device_id_type=MESH,
    )
    copy_a.start()
    for step in range(1, QUAD):
        lo, c = wrap(z_lo + step // NC, NZL), wrap(core + step % NC, NC)
        pltpu.make_async_remote_copy(
            src_ref=buf_m.at[quad],
            dst_ref=buf_m.at[quad],
            send_sem=send_sem.at[4],
            recv_sem=recv_sem.at[4],
            device_id=at_freq((lo * NY + y) * NC + c),
            device_id_type=MESH,
        ).start()

    tables = coef_tables(c_col, d_col, pf, pd)
    copy_a.wait_recv()
    for k in range(NZY):
        sum_a[k] = pieces[core, k] + recv_a[k]
    for other in zy_peers:
        pltpu.make_async_remote_copy(
            src_ref=sum_a.at[other],
            dst_ref=recv_b.at[zy],
            send_sem=send_sem.at[0],
            recv_sem=recv_sem.at[0],
            device_id=at_freq(other * NC + core),
            device_id_type=MESH,
        ).start()
    recv_b[zy] = sum_a[zy]

    rest = buf_m.at[pl.ds(0, QUAD - 1)]
    pltpu.make_async_copy(rest, rest, recv_sem.at[4]).wait()
    mean = tree_sum(buf_m[k] for k in range(QUAD)) * INV_NF
    lane1 = iota((1, LANES), 1)
    mean = jnp.where(lane1 == 2 * PAIRS, 1.0, mean)
    r_row, e_row = rows_from(mean)
    gram = assemble(tables, r_row, e_row, row_to_col(mean, 0), row_to_col(mean, PAIRS))
    row, lane = iota((ROWS, LANES), 0), iota((ROWS, LANES), 1)
    work = gram + jnp.where((lane == row + 64) & (row < WIDTH), 1.0, 0.0)
    work = eliminate(work)
    pivots = jnp.sum(jnp.where((lane == row) & (row < WIDTH), work, 0.0), axis=1, keepdims=True)
    pivots = jnp.where(iota((ROWS, 1), 0) < WIDTH, pivots, 1.0)
    inverse = pltpu.roll(work, 64, 1) * (1.0 / jnp.sqrt(pivots))
    inverse = jnp.where(lane < WIDTH, inverse, 0.0)

    q = jnp.broadcast_to(jnp.sum(q, axis=1, keepdims=True), (ROWS, LANES))
    q_row = jnp.sum(jnp.where(lane == row, q, 0.0), axis=0, keepdims=True)

    triple = [
        v + pltpu.roll(v, STRIDE, 1) + pltpu.roll(v, 2 * STRIDE, 1) for v in tables
    ]

    rest_b = recv_b.at[pl.ds(0, NZY - 1)]
    pltpu.make_async_copy(rest_b, rest_b, recv_sem.at[0]).wait()
    owned = tree_sum(recv_b[k] for k in range(NZY))
    owned = owned * (-INV_NF)

    other_part = pltpu.roll(owned, 4, 0)
    plus, minus = owned + other_part, owned - other_part
    r_rows, e_rows = rows_from(minus)
    plus_t = jnp.concatenate([plus, jnp.zeros((LANES - 8, LANES), F32)], axis=0).T
    lane16 = iota((PAIRS, LANES), 1)

    def columns(g, first):
        spread_col = [
            jnp.broadcast_to(
                plus_t[STRIDE * q + first : STRIDE * q + first + PAIRS, g : g + 1], (PAIRS, LANES)
            )
            for q in range(GROUP)
        ]
        return jnp.where(
            lane16 < STRIDE, spread_col[0], jnp.where(lane16 < 2 * STRIDE, spread_col[1], spread_col[2])
        )

    coupling = jnp.concatenate(
        [
            assemble(triple, r_rows[g : g + 1, :], e_rows[g : g + 1, :], columns(g, 0), columns(g, PAIRS))
            for g in range(TILES)
        ],
        axis=1,
    )
    reduced = jnp.dot(
        inverse[:, 0:ROWS], coupling, precision=HIGH, preferred_element_type=F32
    )
    parts = [reduced[:, g * LANES : (g + 1) * LANES] for g in range(TILES)]
    tall = jnp.concatenate(parts, axis=0)
    wide = jnp.dot(tall.T, tall, precision=HIGH, preferred_element_type=F32)
    corr = wide[0:ROWS]
    for q in range(1, GROUP):
        at = STRIDE * q
        corr = corr + pltpu.roll(wide[at : at + ROWS], LANES - at, 1)

    sub8, ln8 = iota((8, LANES), 0), iota((8, LANES), 1)
    spread8 = lambda v: jnp.broadcast_to(v, (8, LANES))
    border = jnp.where(
        sub8 == 0, spread8(corr[32:33]), jnp.where(sub8 == 1, spread8(q_row), 0.0)
    )
    packed = pltpu.roll(border, 80, 1)
    for g, first, shift in ((3, 80, 48), (2, 72, 40), (1, 56, 24)):
        packed = jnp.where(ln8 < first, pltpu.roll(corr[8 * g : 8 * g + 8], shift, 1), packed)
    total = jnp.where(ln8 < 32, corr[0:8], packed)

    def send(buf, me, peers, index, value):
        buf[me] = value
        for device in peers:
            pltpu.make_async_remote_copy(
                src_ref=buf.at[me],
                dst_ref=buf.at[me],
                send_sem=send_sem.at[index],
                recv_sem=recv_sem.at[index],
                device_id=device,
                device_id_type=MESH,
            ).start()

    def receive(buf, count, index):
        rest = buf.at[pl.ds(0, count - 1)]
        pltpu.make_async_copy(rest, rest, recv_sem.at[index]).wait()
        return tree_sum(buf[k] for k in range(count))

    send(buf_x, x * NC + core, x_peers, 1, total)

    for g in range(TILES):
        for q in range(GROUP):
            block = pltpu.roll(parts[g], LANES - STRIDE * q, 1) if q else parts[g]
            red_ref[GROUP * g + q] = block[0:WIDTH, 0:WIDTH]

    total = receive(buf_x, NX * NC, 1)
    send(buf_y, y, y_peers, 2, total)
    total = receive(buf_y, NY, 2)
    send(buf_z, z, z_peers, 3, total)
    total = receive(buf_z, NZ, 3)

    border = pltpu.roll(total, LANES - 80, 1)
    moments = jnp.where(lane1 < WIDTH, border[1:2], 0.0) * INV_NF
    mean_sq = moments[:, 2 * PAIRS : 2 * PAIRS + 1]
    r_row, e_row = rows_from(moments)
    data_gram = assemble(
        tables, r_row, e_row, row_to_col(moments, 0), row_to_col(moments, PAIRS)
    )
    half = jnp.concatenate(
        [total]
        + [pltpu.roll(total, LANES - shift, 1) for shift in (24, 40, 48)]
        + [spread8(border[0:1])],
        axis=0,
    )
    square = jnp.concatenate([half, jnp.zeros((LANES - ROWS, LANES), F32)], axis=0)
    stored = ((lane < 2 * PAIRS) & (lane >= (row & ~7))) | (row >= 2 * PAIRS)
    correction = jnp.where(stored, half, square.T[0:ROWS])
    system = (data_gram - correction) * (1.0 / mean_sq)
    sys_ref[...] = system[0:WIDTH, 0:WIDTH]
    nrm_ref[...] = (mean * jnp.sqrt(mean_sq * (1.0 / ELEM_TOTAL)))[:, 0:WIDTH]

    copy_a.wait_send()
    for buf, count, index in (
        (sum_a, NZY, 0), (buf_x, NX * NC, 1), (buf_y, NY, 2), (buf_z, NZ, 3), (buf_m, QUAD, 4)
    ):
        rest = buf.at[pl.ds(0, count - 1)]
        pltpu.make_async_copy(rest, rest, send_sem.at[index]).wait()


def writer(red, sys, nrm, red_out, sys_out, nrm_out):
    red_out[...] = red[...]
    sys_out[...] = sys[...]
    nrm_out[...] = nrm[...]


def per_device(pole_freq, pole_damp, samples):
    vmem = lambda *shape: pltpu.VMEM(shape, F32)
    in_hbm = lambda v: pltpu.with_memory_space_constraint(v, pltpu.HBM)
    half = lambda *shape: pltpu.VMEM(shape, jnp.bfloat16)
    results = (
        vmem(OWN, WIDTH, WIDTH),
        vmem(WIDTH, WIDTH),
        vmem(1, WIDTH),
    )
    reduced, system, norm_row = pl.pallas_call(
        kernel,
        out_shape=results,
        in_specs=[pl.BlockSpec(memory_space=pltpu.HBM)] * 3,
        out_specs=(pl.BlockSpec(memory_space=pltpu.VMEM),) * 3,
        scratch_shapes=[
            pltpu.SMEM((PAIRS,), F32),
            pltpu.SMEM((PAIRS,), F32),
            vmem(2, FREQ_LOCAL, ELEM_LOCAL),
            half(2 * BASIS, FREQ_LOCAL),
            half(4 * PAIRS, FREQ_LOCAL),
            vmem(ELEM_LOCAL, LANES),
            vmem(NC, NZY, 8, LANES),
            vmem(NZY, 8, LANES),
            vmem(NZY, 8, LANES),
            vmem(NZY, 8, LANES),
            vmem(QUAD, 1, LANES),
            vmem(NX * NC, 8, LANES),
            vmem(NY, 8, LANES),
            vmem(NZ, 8, LANES),
            pltpu.SemaphoreType.DMA((2,)),
            pltpu.SemaphoreType.DMA((2, CHUNKS)),
            pltpu.SemaphoreType.DMA((6,)),
            pltpu.SemaphoreType.DMA((6,)),
        ],
        compiler_params=pltpu.CompilerParams(
            collective_id=0, has_side_effects=True, vmem_limit_bytes=40 * 1024 * 1024
        ),
    )(*(in_hbm(v) for v in (pole_freq, pole_damp, samples)))
    in_vmem = lambda v: pltpu.with_memory_space_constraint(v, pltpu.VMEM)
    reduced, system, norm_row = pl.pallas_call(
        writer,
        out_shape=(
            jax.ShapeDtypeStruct((OWN, WIDTH, WIDTH), F32),
            jax.ShapeDtypeStruct((WIDTH, WIDTH), F32),
            jax.ShapeDtypeStruct((1, WIDTH), F32),
        ),
        in_specs=[pl.BlockSpec(memory_space=pltpu.VMEM)] * 3,
        out_specs=(pl.BlockSpec(memory_space=pltpu.VMEM),) * 3,
        compiler_params=pltpu.CompilerParams(vmem_limit_bytes=48 * 1024 * 1024),
    )(in_vmem(reduced), in_vmem(system), in_vmem(norm_row))
    return jnp.transpose(reduced, (1, 2, 0)), system, norm_row.reshape(WIDTH)


def solution(mesh):
    placed = (P(), P(), P(None, "freq", "elem"))
    return jax.shard_map(
        per_device,
        mesh=mesh,
        in_specs=placed,
        out_specs=(P(None, None, ("elem", "freq")), P(), P()),
        check_vma=False,
    )
```

```python
import jax
import jax.numpy as jnp
from jax import lax
from jax.experimental import pallas as pl
from jax.experimental.pallas import tpu as pltpu
from jax.sharding import PartitionSpec as P

HIGH = lax.Precision.HIGHEST
MESH = pl.DeviceIdType.MESH
F32 = jnp.float32

NX, NZH, NZL, NY, NC = 4, 4, 2, 8, 2
NZ = NZH * NZL
NZY = NZL * NY
NFREQ = NZY * NC
PAIRS = 16
WIDTH = 2 * PAIRS + 1
ROWS = 40
BASIS = 48
OWN = 12
GROUP = 3
STRIDE = 40
TILES = OWN // GROUP
CHUNK = 256
CHUNKS = 4
LANES = 128
FREQ_LOCAL = 1024
ELEM_LOCAL = OWN * NFREQ
FREQ_TOTAL = FREQ_LOCAL * NFREQ
ELEM_TOTAL = ELEM_LOCAL * NX * NZH
INV_NF = 1.0 / FREQ_TOTAL


def iota(shape, dim):
    return lax.broadcasted_iota(jnp.int32, shape, dim)


def omega_of(half_position):
    return 0.02 + 0.98 * half_position / FREQ_TOTAL


def inverse_of(value):
    r = pltpu.reciprocal(value, approx=True)
    r = r * (2.0 - value * r)
    return r * (2.0 - value * r)


def split(value):
    high = value.astype(jnp.bfloat16)
    return high, (value - high.astype(F32)).astype(jnp.bfloat16)


def bf_dot(a, b):
    return jnp.dot(a, b, preferred_element_type=F32)


def wrap(value, size):
    return jnp.where(value >= size, value - size, value)


def tree_sum(values):
    values = list(values)
    while len(values) > 1:
        values = [a + b for a, b in zip(values[::2], values[1::2])] + values[len(values) & ~1 :]
    return values[0]


def pick(ref, index, shape):
    out = jnp.zeros(shape, F32)
    for m in range(PAIRS):
        out = jnp.where(index == m, ref[m], out)
    return out


def over_rows(col):
    return jnp.concatenate([col, col, jnp.zeros((8, LANES), F32)], axis=0)


def pair_coefs(ci, di, cj, dj, row_sum, col_sum):
    both = di + dj
    gap = cj - ci
    tot = ci + cj
    sq = both * both
    r1 = inverse_of(sq + gap * gap)
    r2 = inverse_of(sq + tot * tot)
    alpha, beta = both * r1, gap * r1
    gamma, delta = both * r2, -tot * r2
    ap, am = alpha + gamma, alpha - gamma
    bm, bp = beta - delta, beta + delta

    def table(di, bm, bp, row_sum, col_sum):
        ss, bd, bs, da = di * ap, di * bm, di * bp, di * am
        cr = jnp.where(row_sum, jnp.where(col_sum, ss, -bd), jnp.where(col_sum, bs, da))
        ce = jnp.where(row_sum, jnp.where(col_sum, bd, ss), jnp.where(col_sum, -da, bs))
        return cr, ce

    return table(di, bm, bp, row_sum, col_sum) + table(dj, -bp, -bm, col_sum, row_sum)


def coef_tables(c_col, d_col, pf, pd):
    shape = (ROWS, LANES)
    row, col = iota(shape, 0), iota(shape, 1)
    small = iota((8, LANES), 1) & (PAIRS - 1)
    cj, dj = pick(pf, small, (8, LANES)), pick(pd, small, (8, LANES))
    tall = lambda v: jnp.concatenate([v] * (ROWS // 8), axis=0)
    inside = (row < 2 * PAIRS) & (col < 2 * PAIRS)
    cr, ce, crt, cet = pair_coefs(
        over_rows(c_col), over_rows(d_col), tall(cj), tall(dj), row < PAIRS, col < PAIRS
    )
    last_row = row == 2 * PAIRS
    last_col = col == 2 * PAIRS
    one = lambda cond: jnp.where(cond, 1.0, 0.0).astype(F32)
    cr = jnp.where(inside, cr, one(last_row & ((col < PAIRS) | last_col)))
    ce = jnp.where(inside, ce, one(last_row & (col >= PAIRS) & (col < 2 * PAIRS)))
    crt = jnp.where(inside, crt, one(last_col & (row < PAIRS)))
    cet = jnp.where(inside, cet, one(last_col & (row >= PAIRS) & (row < 2 * PAIRS)))
    return cr, ce, crt, cet


def assemble(tables, r_row, e_row, r_col, e_col):
    cr, ce, crt, cet = tables
    return cr * r_row + ce * e_row + crt * over_rows(r_col) + cet * over_rows(e_col)


def row_to_col(row_vec, first):
    row, lane = iota((PAIRS, LANES), 0), iota((PAIRS, LANES), 1)
    kept = jnp.where(lane == row + first, jnp.broadcast_to(row_vec, (PAIRS, LANES)), 0.0)
    return jnp.broadcast_to(jnp.sum(kept, axis=1, keepdims=True), (PAIRS, LANES))


def rows_from(values):
    lane = iota(values.shape, 1)
    j = lane - jnp.where(lane >= 2 * STRIDE, 2 * STRIDE, jnp.where(lane >= STRIDE, STRIDE, 0))
    r_row = jnp.where(
        j < PAIRS,
        values,
        jnp.where(j < 2 * PAIRS, pltpu.roll(values, PAIRS, 1), jnp.where(j == 2 * PAIRS, values, 0.0)),
    )
    e_row = jnp.where(
        j < PAIRS,
        pltpu.roll(values, LANES - PAIRS, 1),
        jnp.where(j < 2 * PAIRS, values, 0.0),
    )
    return r_row, e_row


def eliminate(work):
    parts = [work[8 * b : 8 * b + 8] for b in range(ROWS // 8)]
    sub = iota((8, LANES), 0)
    for first in range(0, WIDTH, 8):
        count = min(8, WIDTH - first)
        b0 = first // 8
        live = range(b0, len(parts))
        cols = [
            [jnp.broadcast_to(parts[b][:, first + t : first + t + 1], (8, LANES)) for b in live]
            for t in range(count)
        ]
        rows = [parts[b0][t : t + 1, :] for t in range(count)]
        for t in range(count):
            inv = inverse_of(cols[t][0][t : t + 1, :])
            factor = [v * inv for v in cols[t]]
            factor[0] = jnp.where(sub > t, factor[0], 0.0)
            for u in range(t + 1, count):
                lead = cols[u][0][t : t + 1, :]
                cols[u] = [v - f * lead for v, f in zip(cols[u], factor)]
                rows[u] = rows[u] - factor[0][u : u + 1, :] * rows[t]
            for n, b in enumerate(live):
                parts[b] = parts[b] - factor[n] * rows[t]
    return jnp.concatenate(parts, axis=0)


def kernel(
    pf_hbm, pd_hbm, s_hbm, red_ref, sys_ref, nrm_ref,
    pf, pd, s_buf, re_buf, im_buf, xt_buf, pieces, recv_a, sum_a, recv_b,
    buf_x, buf_y, buf_z,
    pole_sem, load_sem, send_sem, recv_sem,
):
    elem, freq = lax.axis_index("elem"), lax.axis_index("freq")
    x, z_hi = elem // NZH, elem % NZH
    zy, core = freq // NC, freq % NC
    z_lo, y = zy // NY, zy % NY
    z = z_hi * NZL + z_lo

    def at_freq(other):
        return {"elem": elem, "freq": other}

    def at_y(other):
        return {"elem": elem, "freq": (z_lo * NY + other) * NC + core}

    def far_first(size):
        return sorted(range(size), key=lambda d: -min(d, size - d))

    sibling = at_freq(zy * NC + (1 - core))
    zy_peers = [
        wrap(z_lo + dz, NZL) * NY + wrap(y + dy, NY)
        for dy in far_first(NY)
        for dz in (1, 0)
        if dy or dz
    ]
    y_peers = [at_y(wrap(y + dy, NY)) for dy in far_first(NY) if dy]
    z_peers = []
    for dz in far_first(NZ):
        if dz:
            to = wrap(z + dz, NZ)
            hi = to // NZL
            z_peers.append({"elem": x * NZH + hi, "freq": ((to - hi * NZL) * NY + y) * NC + core})
    x_peers = []
    for dx in far_first(NX):
        for c in (1, 0):
            if dx or c:
                to = wrap(x + dx, NX)
                x_peers.append({"elem": to * NZH + z_hi, "freq": zy * NC + wrap(core + c, NC)})

    pole_loads = [
        pltpu.make_async_copy(pf_hbm, pf, pole_sem.at[0]),
        pltpu.make_async_copy(pd_hbm, pd, pole_sem.at[1]),
    ]
    for load in pole_loads:
        load.start()
    loads = []
    for k in range(CHUNKS):
        at = pl.ds(k * CHUNK, CHUNK)
        load = pltpu.make_async_copy(s_hbm.at[:, at], s_buf.at[:, at], load_sem.at[k])
        load.start()
        loads.append(load)

    barrier = pltpu.get_barrier_semaphore()

    def greet(device):
        pl.semaphore_signal(barrier, inc=1, device_id=device, device_id_type=MESH)

    z_rest = []
    for hi_step in range(1, NZH):
        hi = wrap(z_hi + hi_step, NZH)
        z_rest += [{"elem": x * NZH + hi, "freq": (lo * NY + y) * NC + core} for lo in range(NZL)]
    greets = [at_freq(zy_peer * NC + core) for zy_peer in zy_peers]
    greets += z_rest + x_peers
    for device in greets:
        greet(device)
    greeted = len(greets)

    for load in pole_loads:
        load.wait()

    column = iota((PAIRS, LANES), 0)
    c_col = pick(pf, column, (PAIRS, LANES))
    d_col = pick(pd, column, (PAIRS, LANES))
    d_sq = d_col * d_col
    half16 = iota((PAIRS, LANES), 1).astype(F32) + 0.5
    base = (freq * FREQ_LOCAL).astype(F32)
    ones = jnp.where(iota((PAIRS, FREQ_LOCAL), 0) == 0, 1.0, 0.0)
    re_buf[2 * PAIRS : BASIS, :] = ones.astype(jnp.bfloat16)
    re_buf[BASIS + 2 * PAIRS :, :] = jnp.zeros((PAIRS, FREQ_LOCAL), jnp.bfloat16)
    for tile in range(FREQ_LOCAL // LANES):
        at = pl.ds(tile * LANES, LANES)
        w = omega_of(half16 + (base + tile * LANES))
        below, above = w - c_col, w + c_col
        i1 = inverse_of(d_sq + below * below)
        i2 = inverse_of(d_sq + above * above)
        first, second = below * i1, above * i2
        re_buf[0:PAIRS, at], re_buf[BASIS : BASIS + PAIRS, at] = split(d_sq * (i1 + i2))
        re_buf[PAIRS : 2 * PAIRS, at], re_buf[BASIS + PAIRS : BASIS + 2 * PAIRS, at] = split(
            d_col * (first - second)
        )
        im_buf[0:PAIRS, at], im_buf[2 * PAIRS : 3 * PAIRS, at] = split(-d_col * (first + second))
        im_buf[PAIRS : 2 * PAIRS, at], im_buf[3 * PAIRS :, at] = split(d_sq * (i1 - i2))

    share = NFREQ // NC
    halves = [slice(0, 8), slice(8, 16)]

    def mean_step(step, acc):
        acc = list(acc)
        start = ((core * share + step) * FREQ_LOCAL).astype(F32)
        for tile in range(FREQ_LOCAL // LANES):
            w = omega_of(half16[0:8] + (start + tile * LANES))
            for h in range(2):
                below, above = w - c_col[halves[h]], w + c_col[halves[h]]
                n1 = d_sq[halves[h]] + below * below
                n2 = d_sq[halves[h]] + above * above
                r = inverse_of(n1 * n2)
                acc[2 * h] = acc[2 * h] + r * (n1 + n2)
                acc[2 * h + 1] = acc[2 * h + 1] + r * (below * n2 - above * n1)
        return tuple(acc)

    acc = lax.fori_loop(0, share, mean_step, (jnp.zeros((8, LANES), F32),) * 4)
    lane16 = iota((PAIRS, LANES), 1)
    sum_r = d_sq * jnp.sum(jnp.concatenate([acc[0], acc[2]], axis=0), axis=1, keepdims=True)
    sum_e = d_col * jnp.sum(jnp.concatenate([acc[1], acc[3]], axis=0), axis=1, keepdims=True)
    sums = jnp.where(lane16 == column, sum_r, jnp.where(lane16 == column + PAIRS, sum_e, 0.0))
    mean = jnp.sum(sums, axis=0, keepdims=True)
    pieces[1 - core, NZY] = jnp.broadcast_to(mean, (8, LANES))

    x0 = jnp.zeros((BASIS, ELEM_LOCAL + LANES), F32)
    x1 = jnp.zeros((2 * PAIRS, ELEM_LOCAL), F32)
    for k in range(CHUNKS):
        at = pl.ds(k * CHUNK, CHUNK)
        loads[k].wait()
        s0, s1 = s_buf[0, at, :], s_buf[1, at, :]
        squares = s0 * s0 + s1 * s1
        power = tree_sum(squares[:, t * LANES : (t + 1) * LANES] for t in range(ELEM_LOCAL // LANES))
        high, low = split(jnp.concatenate([s0, power], axis=1))
        both = bf_dot(re_buf[:, at], high)
        x0 = x0 + (both[0:BASIS] + both[BASIS:] + bf_dot(re_buf[0:BASIS, at], low))
        high, low = split(s1)
        both = bf_dot(im_buf[:, at], high)
        x1 = x1 + (both[0 : 2 * PAIRS] + both[2 * PAIRS :] + bf_dot(im_buf[0 : 2 * PAIRS, at], low))
    x0, q = x0[:, 0:ELEM_LOCAL], x0[0:ROWS, ELEM_LOCAL:]

    stacked = jnp.concatenate(
        [
            x0,
            jnp.zeros((64 - BASIS, ELEM_LOCAL), F32),
            x1,
            jnp.zeros((LANES - 64 - 2 * PAIRS, ELEM_LOCAL), F32),
        ],
        axis=0,
    )
    for tile in range(ELEM_LOCAL // LANES):
        at = slice(tile * LANES, (tile + 1) * LANES)
        xt_buf[at, :] = stacked[:, at].T
    count = ELEM_LOCAL // GROUP
    thirds = [xt_buf[pl.ds(q, count, stride=GROUP), :] for q in range(GROUP)]
    lane_c = iota((count, LANES), 1)

    def spread(shift):
        rolled = [
            pltpu.roll(thirds[q], (STRIDE * q + shift) % LANES, 1) if (STRIDE * q + shift) % LANES else thirds[q]
            for q in range(GROUP)
        ]
        return jnp.where(
            lane_c < STRIDE, rolled[0], jnp.where(lane_c < 2 * STRIDE, rolled[1], rolled[2])
        )

    part0, part1 = spread(0), spread(64)
    upper = iota((8, LANES), 0) < 4
    for k in range(NZY):
        v0, v1 = part0[8 * k : 8 * k + 8], part1[8 * k : 8 * k + 8]
        pieces[0, k] = jnp.where(upper, v0, pltpu.roll(v1, 4, 0))
        pieces[1, k] = jnp.where(upper, pltpu.roll(v0, 4, 0), v1)

    pl.semaphore_wait(barrier, greeted)

    copy_a = pltpu.make_async_remote_copy(
        src_ref=pieces.at[1 - core],
        dst_ref=recv_a,
        send_sem=send_sem.at[4],
        recv_sem=recv_sem.at[4],
        device_id=sibling,
        device_id_type=MESH,
    )
    copy_a.start()
    tables = coef_tables(c_col, d_col, pf, pd)
    copy_a.wait_recv()
    for k in range(NZY):
        sum_a[k] = pieces[core, k] + recv_a[k]
    for other in zy_peers:
        pltpu.make_async_remote_copy(
            src_ref=sum_a.at[other],
            dst_ref=recv_b.at[zy],
            send_sem=send_sem.at[0],
            recv_sem=recv_sem.at[0],
            device_id=at_freq(other * NC + core),
            device_id_type=MESH,
        ).start()
    recv_b[zy] = sum_a[zy]

    mean = (mean + recv_a[NZY, 0:1, :]) * INV_NF
    lane1 = iota((1, LANES), 1)
    mean = jnp.where(lane1 == 2 * PAIRS, 1.0, mean)
    r_row, e_row = rows_from(mean)
    gram = assemble(tables, r_row, e_row, row_to_col(mean, 0), row_to_col(mean, PAIRS))
    row, lane = iota((ROWS, LANES), 0), iota((ROWS, LANES), 1)
    work = gram + jnp.where((lane == row + 64) & (row < WIDTH), 1.0, 0.0)
    work = eliminate(work)
    pivots = jnp.sum(jnp.where((lane == row) & (row < WIDTH), work, 0.0), axis=1, keepdims=True)
    pivots = jnp.where(iota((ROWS, 1), 0) < WIDTH, pivots, 1.0)
    inverse = pltpu.roll(work, 64, 1) * (1.0 / jnp.sqrt(pivots))
    inverse = jnp.where(lane < WIDTH, inverse, 0.0)

    q = jnp.broadcast_to(jnp.sum(q, axis=1, keepdims=True), (ROWS, LANES))
    q_row = jnp.sum(jnp.where(lane == row, q, 0.0), axis=0, keepdims=True)

    triple = [
        v + pltpu.roll(v, STRIDE, 1) + pltpu.roll(v, 2 * STRIDE, 1) for v in tables
    ]

    rest_b = recv_b.at[pl.ds(0, NZY - 1)]
    pltpu.make_async_copy(rest_b, rest_b, recv_sem.at[0]).wait()
    owned = tree_sum(recv_b[k] for k in range(NZY))
    owned = owned * (-INV_NF)

    other_part = pltpu.roll(owned, 4, 0)
    plus, minus = owned + other_part, owned - other_part
    r_rows, e_rows = rows_from(minus)
    plus_t = plus.T
    lane16 = iota((PAIRS, LANES), 1)

    def columns(g, first):
        spread_col = [
            jnp.broadcast_to(
                plus_t[STRIDE * q + first : STRIDE * q + first + PAIRS, g : g + 1], (PAIRS, LANES)
            )
            for q in range(GROUP)
        ]
        return jnp.where(
            lane16 < STRIDE, spread_col[0], jnp.where(lane16 < 2 * STRIDE, spread_col[1], spread_col[2])
        )

    coupling = jnp.concatenate(
        [
            assemble(triple, r_rows[g : g + 1, :], e_rows[g : g + 1, :], columns(g, 0), columns(g, PAIRS))
            for g in range(TILES)
        ],
        axis=1,
    )
    reduced = jnp.dot(
        inverse[:, 0:ROWS], coupling, precision=HIGH, preferred_element_type=F32
    )
    parts = [reduced[:, g * LANES : (g + 1) * LANES] for g in range(TILES)]
    tall = jnp.concatenate(parts, axis=0)
    wide = jnp.dot(tall.T, tall, precision=HIGH, preferred_element_type=F32)
    corr = wide[0:ROWS]
    for q in range(1, GROUP):
        at = STRIDE * q
        corr = corr + pltpu.roll(wide[at : at + ROWS], LANES - at, 1)

    sub8, ln8 = iota((8, LANES), 0), iota((8, LANES), 1)
    spread8 = lambda v: jnp.broadcast_to(v, (8, LANES))
    border = jnp.where(
        sub8 == 0, spread8(corr[32:33]), jnp.where(sub8 == 1, spread8(q_row), 0.0)
    )
    packed = pltpu.roll(border, 80, 1)
    for g, first, shift in ((3, 80, 48), (2, 72, 40), (1, 56, 24)):
        packed = jnp.where(ln8 < first, pltpu.roll(corr[8 * g : 8 * g + 8], shift, 1), packed)
    total = jnp.where(ln8 < 32, corr[0:8], packed)

    def send(buf, me, peers, index, value):
        buf[me] = value
        for device in peers:
            pltpu.make_async_remote_copy(
                src_ref=buf.at[me],
                dst_ref=buf.at[me],
                send_sem=send_sem.at[index],
                recv_sem=recv_sem.at[index],
                device_id=device,
                device_id_type=MESH,
            ).start()

    def receive(buf, count, index):
        rest = buf.at[pl.ds(0, count - 1)]
        pltpu.make_async_copy(rest, rest, recv_sem.at[index]).wait()
        return tree_sum(buf[k] for k in range(count))

    send(buf_x, x * NC + core, x_peers, 1, total)

    for g in range(TILES):
        for q in range(GROUP):
            block = pltpu.roll(parts[g], LANES - STRIDE * q, 1) if q else parts[g]
            red_ref[GROUP * g + q] = block[0:WIDTH, 0:WIDTH]

    total = receive(buf_x, NX * NC, 1)
    send(buf_y, y, y_peers, 2, total)
    total = receive(buf_y, NY, 2)
    send(buf_z, z, z_peers, 3, total)
    total = receive(buf_z, NZ, 3)

    border = pltpu.roll(total, LANES - 80, 1)
    moments = jnp.where(lane1 < WIDTH, border[1:2], 0.0) * INV_NF
    mean_sq = moments[:, 2 * PAIRS : 2 * PAIRS + 1]
    r_row, e_row = rows_from(moments)
    data_gram = assemble(
        tables, r_row, e_row, row_to_col(moments, 0), row_to_col(moments, PAIRS)
    )
    half = jnp.concatenate(
        [total]
        + [pltpu.roll(total, LANES - shift, 1) for shift in (24, 40, 48)]
        + [spread8(border[0:1])],
        axis=0,
    )
    square = jnp.concatenate([half, jnp.zeros((LANES - ROWS, LANES), F32)], axis=0)
    stored = ((lane < 2 * PAIRS) & (lane >= (row & ~7))) | (row >= 2 * PAIRS)
    correction = jnp.where(stored, half, square.T[0:ROWS])
    system = (data_gram - correction) * (1.0 / mean_sq)
    sys_ref[...] = system[0:WIDTH, 0:WIDTH]
    nrm_ref[...] = (mean * jnp.sqrt(mean_sq * (1.0 / ELEM_TOTAL)))[:, 0:WIDTH]

    copy_a.wait_send()
    for buf, count, index in (
        (sum_a, NZY, 0), (buf_x, NX * NC, 1), (buf_y, NY, 2), (buf_z, NZ, 3)
    ):
        rest = buf.at[pl.ds(0, count - 1)]
        pltpu.make_async_copy(rest, rest, send_sem.at[index]).wait()


def writer(red, sys, nrm, red_out, sys_out, nrm_out):
    red_out[...] = red[...]
    sys_out[...] = sys[...]
    nrm_out[...] = nrm[...]


def per_device(pole_freq, pole_damp, samples):
    vmem = lambda *shape: pltpu.VMEM(shape, F32)
    in_hbm = lambda v: pltpu.with_memory_space_constraint(v, pltpu.HBM)
    half = lambda *shape: pltpu.VMEM(shape, jnp.bfloat16)
    results = (
        vmem(OWN, WIDTH, WIDTH),
        vmem(WIDTH, WIDTH),
        vmem(1, WIDTH),
    )
    reduced, system, norm_row = pl.pallas_call(
        kernel,
        out_shape=results,
        in_specs=[pl.BlockSpec(memory_space=pltpu.HBM)] * 3,
        out_specs=(pl.BlockSpec(memory_space=pltpu.VMEM),) * 3,
        scratch_shapes=[
            pltpu.SMEM((PAIRS,), F32),
            pltpu.SMEM((PAIRS,), F32),
            vmem(2, FREQ_LOCAL, ELEM_LOCAL),
            half(2 * BASIS, FREQ_LOCAL),
            half(4 * PAIRS, FREQ_LOCAL),
            vmem(ELEM_LOCAL, LANES),
            vmem(NC, NZY + 1, 8, LANES),
            vmem(NZY + 1, 8, LANES),
            vmem(NZY, 8, LANES),
            vmem(NZY, 8, LANES),
            vmem(NX * NC, 8, LANES),
            vmem(NY, 8, LANES),
            vmem(NZ, 8, LANES),
            pltpu.SemaphoreType.DMA((2,)),
            pltpu.SemaphoreType.DMA((CHUNKS,)),
            pltpu.SemaphoreType.DMA((5,)),
            pltpu.SemaphoreType.DMA((5,)),
        ],
        compiler_params=pltpu.CompilerParams(
            collective_id=0, has_side_effects=True, vmem_limit_bytes=40 * 1024 * 1024
        ),
    )(*(in_hbm(v) for v in (pole_freq, pole_damp, samples)))
    in_vmem = lambda v: pltpu.with_memory_space_constraint(v, pltpu.VMEM)
    reduced, system, norm_row = pl.pallas_call(
        writer,
        out_shape=(
            jax.ShapeDtypeStruct((OWN, WIDTH, WIDTH), F32),
            jax.ShapeDtypeStruct((WIDTH, WIDTH), F32),
            jax.ShapeDtypeStruct((1, WIDTH), F32),
        ),
        in_specs=[pl.BlockSpec(memory_space=pltpu.VMEM)] * 3,
        out_specs=(pl.BlockSpec(memory_space=pltpu.VMEM),) * 3,
        compiler_params=pltpu.CompilerParams(vmem_limit_bytes=48 * 1024 * 1024),
    )(in_vmem(reduced), in_vmem(system), in_vmem(norm_row))
    return jnp.transpose(reduced, (1, 2, 0)), system, norm_row.reshape(WIDTH)


def solution(mesh):
    placed = (P(), P(), P(None, "freq", "elem"))
    return jax.shard_map(
        per_device,
        mesh=mesh,
        in_specs=placed,
        out_specs=(P(None, None, ("elem", "freq")), P(), P()),
        check_vma=False,
    )
```

```python
import jax
import jax.numpy as jnp
from jax import lax
from jax.experimental import pallas as pl
from jax.experimental.pallas import tpu as pltpu
from jax.sharding import PartitionSpec as P

HIGH = lax.Precision.HIGHEST
MESH = pl.DeviceIdType.MESH
F32 = jnp.float32

NX, NZH, NZL, NY, NC = 4, 4, 2, 8, 2
NZ = NZH * NZL
NZY = NZL * NY
NFREQ = NZY * NC
QUAD = NZL * NC
PAIRS = 16
WIDTH = 2 * PAIRS + 1
ROWS = 40
BASIS = 48
OWN = 12
GROUP = 3
STRIDE = 40
TILES = OWN // GROUP
CHUNK = 256
CHUNKS = 4
LANES = 128
FREQ_LOCAL = 1024
ELEM_LOCAL = OWN * NFREQ
FREQ_TOTAL = FREQ_LOCAL * NFREQ
ELEM_TOTAL = ELEM_LOCAL * NX * NZH
INV_NF = 1.0 / FREQ_TOTAL


def iota(shape, dim):
    return lax.broadcasted_iota(jnp.int32, shape, dim)


def omega_of(half_position):
    return 0.02 + 0.98 * half_position / FREQ_TOTAL


def inverse_of(value):
    r = pltpu.reciprocal(value, approx=True)
    r = r * (2.0 - value * r)
    return r * (2.0 - value * r)


def split(value):
    high = value.astype(jnp.bfloat16)
    return high, (value - high.astype(F32)).astype(jnp.bfloat16)


def bf_dot(a, b):
    return jnp.dot(a, b, preferred_element_type=F32)


def wrap(value, size):
    return jnp.where(value >= size, value - size, value)


def tree_sum(values):
    values = list(values)
    while len(values) > 1:
        values = [a + b for a, b in zip(values[::2], values[1::2])] + values[len(values) & ~1 :]
    return values[0]


def pick(ref, index, shape):
    out = jnp.zeros(shape, F32)
    for m in range(PAIRS):
        out = jnp.where(index == m, ref[m], out)
    return out


def over_rows(col):
    return jnp.concatenate([col, col, jnp.zeros((8, LANES), F32)], axis=0)


def pair_coefs(ci, di, cj, dj, row_sum, col_sum):
    both = di + dj
    gap = cj - ci
    tot = ci + cj
    sq = both * both
    r1 = inverse_of(sq + gap * gap)
    r2 = inverse_of(sq + tot * tot)
    alpha, beta = both * r1, gap * r1
    gamma, delta = both * r2, -tot * r2
    ap, am = alpha + gamma, alpha - gamma
    bm, bp = beta - delta, beta + delta

    def table(di, bm, bp, row_sum, col_sum):
        ss, bd, bs, da = di * ap, di * bm, di * bp, di * am
        cr = jnp.where(row_sum, jnp.where(col_sum, ss, -bd), jnp.where(col_sum, bs, da))
        ce = jnp.where(row_sum, jnp.where(col_sum, bd, ss), jnp.where(col_sum, -da, bs))
        return cr, ce

    return table(di, bm, bp, row_sum, col_sum) + table(dj, -bp, -bm, col_sum, row_sum)


def coef_tables(c_col, d_col, pf, pd):
    shape = (ROWS, LANES)
    row, col = iota(shape, 0), iota(shape, 1)
    small = iota((8, LANES), 1) & (PAIRS - 1)
    cj, dj = pick(pf, small, (8, LANES)), pick(pd, small, (8, LANES))
    tall = lambda v: jnp.concatenate([v] * (ROWS // 8), axis=0)
    inside = (row < 2 * PAIRS) & (col < 2 * PAIRS)
    cr, ce, crt, cet = pair_coefs(
        over_rows(c_col), over_rows(d_col), tall(cj), tall(dj), row < PAIRS, col < PAIRS
    )
    last_row = row == 2 * PAIRS
    last_col = col == 2 * PAIRS
    one = lambda cond: jnp.where(cond, 1.0, 0.0).astype(F32)
    cr = jnp.where(inside, cr, one(last_row & ((col < PAIRS) | last_col)))
    ce = jnp.where(inside, ce, one(last_row & (col >= PAIRS) & (col < 2 * PAIRS)))
    crt = jnp.where(inside, crt, one(last_col & (row < PAIRS)))
    cet = jnp.where(inside, cet, one(last_col & (row >= PAIRS) & (row < 2 * PAIRS)))
    return cr, ce, crt, cet


def assemble(tables, r_row, e_row, r_col, e_col):
    cr, ce, crt, cet = tables
    return cr * r_row + ce * e_row + crt * over_rows(r_col) + cet * over_rows(e_col)


def row_to_col(row_vec, first):
    row, lane = iota((PAIRS, LANES), 0), iota((PAIRS, LANES), 1)
    kept = jnp.where(lane == row + first, jnp.broadcast_to(row_vec, (PAIRS, LANES)), 0.0)
    return jnp.broadcast_to(jnp.sum(kept, axis=1, keepdims=True), (PAIRS, LANES))


def rows_from(values):
    lane = iota(values.shape, 1)
    j = lane - jnp.where(lane >= 2 * STRIDE, 2 * STRIDE, jnp.where(lane >= STRIDE, STRIDE, 0))
    r_row = jnp.where(
        j < PAIRS,
        values,
        jnp.where(j < 2 * PAIRS, pltpu.roll(values, PAIRS, 1), jnp.where(j == 2 * PAIRS, values, 0.0)),
    )
    e_row = jnp.where(
        j < PAIRS,
        pltpu.roll(values, LANES - PAIRS, 1),
        jnp.where(j < 2 * PAIRS, values, 0.0),
    )
    return r_row, e_row


def eliminate(work):
    parts = [work[8 * b : 8 * b + 8] for b in range(ROWS // 8)]
    sub = iota((8, LANES), 0)
    for first in range(0, WIDTH, 8):
        count = min(8, WIDTH - first)
        b0 = first // 8
        live = range(b0, len(parts))
        cols = [
            [jnp.broadcast_to(parts[b][:, first + t : first + t + 1], (8, LANES)) for b in live]
            for t in range(count)
        ]
        rows = [parts[b0][t : t + 1, :] for t in range(count)]
        for t in range(count):
            inv = inverse_of(cols[t][0][t : t + 1, :])
            factor = [v * inv for v in cols[t]]
            factor[0] = jnp.where(sub > t, factor[0], 0.0)
            for u in range(t + 1, count):
                lead = cols[u][0][t : t + 1, :]
                cols[u] = [v - f * lead for v, f in zip(cols[u], factor)]
                rows[u] = rows[u] - factor[0][u : u + 1, :] * rows[t]
            for n, b in enumerate(live):
                parts[b] = parts[b] - factor[n] * rows[t]
    return jnp.concatenate(parts, axis=0)


def kernel(
    pf_hbm, pd_hbm, s_hbm, red_ref, sys_ref, nrm_ref,
    pf, pd, s_buf, re_buf, im_buf, xt_buf, pieces, recv_a, sum_a, recv_b,
    buf_m, buf_x, buf_y, buf_z,
    pole_sem, load_sem, send_sem, recv_sem,
):
    elem, freq = lax.axis_index("elem"), lax.axis_index("freq")
    x, z_hi = elem // NZH, elem % NZH
    zy, core = freq // NC, freq % NC
    z_lo, y = zy // NY, zy % NY
    z = z_hi * NZL + z_lo

    def at_freq(other):
        return {"elem": elem, "freq": other}

    def at_y(other):
        return {"elem": elem, "freq": (z_lo * NY + other) * NC + core}

    def far_first(size):
        return sorted(range(size), key=lambda d: -min(d, size - d))

    sibling = at_freq(zy * NC + (1 - core))
    zy_peers = [
        wrap(z_lo + dz, NZL) * NY + wrap(y + dy, NY)
        for dy in far_first(NY)
        for dz in (1, 0)
        if dy or dz
    ]
    y_peers = [at_y(wrap(y + dy, NY)) for dy in far_first(NY) if dy]
    z_peers = []
    for dz in far_first(NZ):
        if dz:
            to = wrap(z + dz, NZ)
            hi = to // NZL
            z_peers.append({"elem": x * NZH + hi, "freq": ((to - hi * NZL) * NY + y) * NC + core})
    x_peers = []
    for dx in far_first(NX):
        for c in (1, 0):
            if dx or c:
                to = wrap(x + dx, NX)
                x_peers.append({"elem": to * NZH + z_hi, "freq": zy * NC + wrap(core + c, NC)})
    corner = at_freq((wrap(z_lo + 1, NZL) * NY + y) * NC + (1 - core))

    pole_loads = [
        pltpu.make_async_copy(pf_hbm, pf, pole_sem.at[0]),
        pltpu.make_async_copy(pd_hbm, pd, pole_sem.at[1]),
    ]
    for load in pole_loads:
        load.start()
    loads = []
    for k in range(CHUNKS):
        at = pl.ds(k * CHUNK, CHUNK)
        load = pltpu.make_async_copy(s_hbm.at[:, at], s_buf.at[:, at], load_sem.at[k])
        load.start()
        loads.append(load)

    barrier = pltpu.get_barrier_semaphore()

    def greet(device):
        pl.semaphore_signal(barrier, inc=1, device_id=device, device_id_type=MESH)

    z_rest = []
    for hi_step in range(1, NZH):
        hi = wrap(z_hi + hi_step, NZH)
        z_rest += [{"elem": x * NZH + hi, "freq": (lo * NY + y) * NC + core} for lo in range(NZL)]
    greets = [at_freq(zy_peer * NC + core) for zy_peer in zy_peers]
    greets += [corner] + z_rest + x_peers
    for device in greets:
        greet(device)
    greeted = len(greets)

    for load in pole_loads:
        load.wait()

    column = iota((PAIRS, LANES), 0)
    c_col = pick(pf, column, (PAIRS, LANES))
    d_col = pick(pd, column, (PAIRS, LANES))
    d_sq = d_col * d_col
    half16 = iota((PAIRS, LANES), 1).astype(F32) + 0.5
    base = (freq * FREQ_LOCAL).astype(F32)
    ones = jnp.where(iota((PAIRS, FREQ_LOCAL), 0) == 0, 1.0, 0.0)
    re_buf[2 * PAIRS : BASIS, :] = ones.astype(jnp.bfloat16)
    re_buf[BASIS + 2 * PAIRS :, :] = jnp.zeros((PAIRS, FREQ_LOCAL), jnp.bfloat16)
    for tile in range(FREQ_LOCAL // LANES):
        at = pl.ds(tile * LANES, LANES)
        w = omega_of(half16 + (base + tile * LANES))
        below, above = w - c_col, w + c_col
        i1 = inverse_of(d_sq + below * below)
        i2 = inverse_of(d_sq + above * above)
        first, second = below * i1, above * i2
        re_buf[0:PAIRS, at], re_buf[BASIS : BASIS + PAIRS, at] = split(d_sq * (i1 + i2))
        re_buf[PAIRS : 2 * PAIRS, at], re_buf[BASIS + PAIRS : BASIS + 2 * PAIRS, at] = split(
            d_col * (first - second)
        )
        im_buf[0:PAIRS, at], im_buf[2 * PAIRS : 3 * PAIRS, at] = split(-d_col * (first + second))
        im_buf[PAIRS : 2 * PAIRS, at], im_buf[3 * PAIRS :, at] = split(d_sq * (i1 - i2))

    x0 = jnp.zeros((BASIS, ELEM_LOCAL + LANES), F32)
    x1 = jnp.zeros((2 * PAIRS, ELEM_LOCAL), F32)
    for k in range(CHUNKS):
        at = pl.ds(k * CHUNK, CHUNK)
        loads[k].wait()
        s0, s1 = s_buf[0, at, :], s_buf[1, at, :]
        squares = s0 * s0 + s1 * s1
        power = tree_sum(squares[:, t * LANES : (t + 1) * LANES] for t in range(ELEM_LOCAL // LANES))
        high, low = split(jnp.concatenate([s0, power], axis=1))
        both = bf_dot(re_buf[:, at], high)
        x0 = x0 + (both[0:BASIS] + both[BASIS:] + bf_dot(re_buf[0:BASIS, at], low))
        high, low = split(s1)
        both = bf_dot(im_buf[:, at], high)
        x1 = x1 + (both[0 : 2 * PAIRS] + both[2 * PAIRS :] + bf_dot(im_buf[0 : 2 * PAIRS, at], low))
    x0, q = x0[:, 0:ELEM_LOCAL], x0[0:ROWS, ELEM_LOCAL:]

    stacked = jnp.concatenate(
        [
            x0,
            jnp.zeros((64 - BASIS, ELEM_LOCAL), F32),
            x1,
            jnp.zeros((LANES - 64 - 2 * PAIRS, ELEM_LOCAL), F32),
        ],
        axis=0,
    )
    for tile in range(ELEM_LOCAL // LANES):
        at = slice(tile * LANES, (tile + 1) * LANES)
        xt_buf[at, :] = stacked[:, at].T
    count = ELEM_LOCAL // GROUP
    thirds = [xt_buf[pl.ds(q, count, stride=GROUP), :] for q in range(GROUP)]
    lane_c = iota((count, LANES), 1)

    def spread(shift):
        rolled = [
            pltpu.roll(thirds[q], (STRIDE * q + shift) % LANES, 1) if (STRIDE * q + shift) % LANES else thirds[q]
            for q in range(GROUP)
        ]
        return jnp.where(
            lane_c < STRIDE, rolled[0], jnp.where(lane_c < 2 * STRIDE, rolled[1], rolled[2])
        )

    part0, part1 = spread(0), spread(64)
    upper = iota((8, LANES), 0) < 4
    for k in range(NZY):
        v0, v1 = part0[8 * k : 8 * k + 8], part1[8 * k : 8 * k + 8]
        pieces[0, k] = jnp.where(upper, v0, pltpu.roll(v1, 4, 0))
        pieces[1, k] = jnp.where(upper, pltpu.roll(v0, 4, 0), v1)

    pl.semaphore_wait(barrier, greeted)

    copy_a = pltpu.make_async_remote_copy(
        src_ref=pieces.at[1 - core],
        dst_ref=recv_a,
        send_sem=send_sem.at[5],
        recv_sem=recv_sem.at[5],
        device_id=sibling,
        device_id_type=MESH,
    )
    copy_a.start()

    quad = z_lo * NC + core
    share = NFREQ // QUAD
    halves = [slice(0, 8), slice(8, 16)]

    def mean_step(step, acc):
        acc = list(acc)
        start = ((quad * share + step) * FREQ_LOCAL).astype(F32)
        for tile in range(FREQ_LOCAL // LANES):
            w = omega_of(half16[0:8] + (start + tile * LANES))
            for h in range(2):
                below, above = w - c_col[halves[h]], w + c_col[halves[h]]
                n1 = d_sq[halves[h]] + below * below
                n2 = d_sq[halves[h]] + above * above
                r = inverse_of(n1 * n2)
                acc[2 * h] = acc[2 * h] + r * (n1 + n2)
                acc[2 * h + 1] = acc[2 * h + 1] + r * (below * n2 - above * n1)
        return tuple(acc)

    acc = lax.fori_loop(0, share, mean_step, (jnp.zeros((8, LANES), F32),) * 4)
    lane16 = iota((PAIRS, LANES), 1)
    sum_r = d_sq * jnp.sum(jnp.concatenate([acc[0], acc[2]], axis=0), axis=1, keepdims=True)
    sum_e = d_col * jnp.sum(jnp.concatenate([acc[1], acc[3]], axis=0), axis=1, keepdims=True)
    sums = jnp.where(lane16 == column, sum_r, jnp.where(lane16 == column + PAIRS, sum_e, 0.0))
    buf_m[quad] = jnp.sum(sums, axis=0, keepdims=True)

    for step in range(1, QUAD):
        lo, c = wrap(z_lo + step // NC, NZL), wrap(core + step % NC, NC)
        pltpu.make_async_remote_copy(
            src_ref=buf_m.at[quad],
            dst_ref=buf_m.at[quad],
            send_sem=send_sem.at[4],
            recv_sem=recv_sem.at[4],
            device_id=at_freq((lo * NY + y) * NC + c),
            device_id_type=MESH,
        ).start()

    copy_a.wait_recv()
    for k in range(NZY):
        sum_a[k] = pieces[core, k] + recv_a[k]
    for other in zy_peers:
        pltpu.make_async_remote_copy(
            src_ref=sum_a.at[other],
            dst_ref=recv_b.at[zy],
            send_sem=send_sem.at[0],
            recv_sem=recv_sem.at[0],
            device_id=at_freq(other * NC + core),
            device_id_type=MESH,
        ).start()
    recv_b[zy] = sum_a[zy]

    tables = coef_tables(c_col, d_col, pf, pd)
    rest = buf_m.at[pl.ds(0, QUAD - 1)]
    pltpu.make_async_copy(rest, rest, recv_sem.at[4]).wait()
    mean = tree_sum(buf_m[k] for k in range(QUAD)) * INV_NF
    lane1 = iota((1, LANES), 1)
    mean = jnp.where(lane1 == 2 * PAIRS, 1.0, mean)
    r_row, e_row = rows_from(mean)
    gram = assemble(tables, r_row, e_row, row_to_col(mean, 0), row_to_col(mean, PAIRS))
    row, lane = iota((ROWS, LANES), 0), iota((ROWS, LANES), 1)
    work = gram + jnp.where((lane == row + 64) & (row < WIDTH), 1.0, 0.0)
    work = eliminate(work)
    pivots = jnp.sum(jnp.where((lane == row) & (row < WIDTH), work, 0.0), axis=1, keepdims=True)
    pivots = jnp.where(iota((ROWS, 1), 0) < WIDTH, pivots, 1.0)
    inverse = pltpu.roll(work, 64, 1) * (1.0 / jnp.sqrt(pivots))
    inverse = jnp.where(lane < WIDTH, inverse, 0.0)

    q = jnp.broadcast_to(jnp.sum(q, axis=1, keepdims=True), (ROWS, LANES))
    q_row = jnp.sum(jnp.where(lane == row, q, 0.0), axis=0, keepdims=True)

    triple = [
        v + pltpu.roll(v, STRIDE, 1) + pltpu.roll(v, 2 * STRIDE, 1) for v in tables
    ]

    rest_b = recv_b.at[pl.ds(0, NZY - 1)]
    pltpu.make_async_copy(rest_b, rest_b, recv_sem.at[0]).wait()
    owned = tree_sum(recv_b[k] for k in range(NZY))
    owned = owned * (-INV_NF)

    other_part = pltpu.roll(owned, 4, 0)
    plus, minus = owned + other_part, owned - other_part
    r_rows, e_rows = rows_from(minus)
    plus_t = plus.T
    lane16 = iota((PAIRS, LANES), 1)

    def columns(g, first):
        spread_col = [
            jnp.broadcast_to(
                plus_t[STRIDE * q + first : STRIDE * q + first + PAIRS, g : g + 1], (PAIRS, LANES)
            )
            for q in range(GROUP)
        ]
        return jnp.where(
            lane16 < STRIDE, spread_col[0], jnp.where(lane16 < 2 * STRIDE, spread_col[1], spread_col[2])
        )

    coupling = jnp.concatenate(
        [
            assemble(triple, r_rows[g : g + 1, :], e_rows[g : g + 1, :], columns(g, 0), columns(g, PAIRS))
            for g in range(TILES)
        ],
        axis=1,
    )
    reduced = jnp.dot(
        inverse[:, 0:ROWS], coupling, precision=HIGH, preferred_element_type=F32
    )
    parts = [reduced[:, g * LANES : (g + 1) * LANES] for g in range(TILES)]
    tall = jnp.concatenate(parts, axis=0)
    wide = jnp.dot(tall.T, tall, precision=HIGH, preferred_element_type=F32)
    corr = wide[0:ROWS]
    for q in range(1, GROUP):
        at = STRIDE * q
        corr = corr + pltpu.roll(wide[at : at + ROWS], LANES - at, 1)

    sub8, ln8 = iota((8, LANES), 0), iota((8, LANES), 1)
    spread8 = lambda v: jnp.broadcast_to(v, (8, LANES))
    border = jnp.where(
        sub8 == 0, spread8(corr[32:33]), jnp.where(sub8 == 1, spread8(q_row), 0.0)
    )
    packed = pltpu.roll(border, 80, 1)
    for g, first, shift in ((3, 80, 48), (2, 72, 40), (1, 56, 24)):
        packed = jnp.where(ln8 < first, pltpu.roll(corr[8 * g : 8 * g + 8], shift, 1), packed)
    total = jnp.where(ln8 < 32, corr[0:8], packed)

    def send(buf, me, peers, index, value):
        buf[me] = value
        for device in peers:
            pltpu.make_async_remote_copy(
                src_ref=buf.at[me],
                dst_ref=buf.at[me],
                send_sem=send_sem.at[index],
                recv_sem=recv_sem.at[index],
                device_id=device,
                device_id_type=MESH,
            ).start()

    def receive(buf, count, index):
        rest = buf.at[pl.ds(0, count - 1)]
        pltpu.make_async_copy(rest, rest, recv_sem.at[index]).wait()
        return tree_sum(buf[k] for k in range(count))

    send(buf_x, x * NC + core, x_peers, 1, total)

    for g in range(TILES):
        for q in range(GROUP):
            block = pltpu.roll(parts[g], LANES - STRIDE * q, 1) if q else parts[g]
            red_ref[GROUP * g + q] = block[0:WIDTH, 0:WIDTH]

    total = receive(buf_x, NX * NC, 1)
    send(buf_y, y, y_peers, 2, total)
    total = receive(buf_y, NY, 2)
    send(buf_z, z, z_peers, 3, total)
    total = receive(buf_z, NZ, 3)

    border = pltpu.roll(total, LANES - 80, 1)
    moments = jnp.where(lane1 < WIDTH, border[1:2], 0.0) * INV_NF
    mean_sq = moments[:, 2 * PAIRS : 2 * PAIRS + 1]
    r_row, e_row = rows_from(moments)
    data_gram = assemble(
        tables, r_row, e_row, row_to_col(moments, 0), row_to_col(moments, PAIRS)
    )
    half = jnp.concatenate(
        [total]
        + [pltpu.roll(total, LANES - shift, 1) for shift in (24, 40, 48)]
        + [spread8(border[0:1])],
        axis=0,
    )
    square = jnp.concatenate([half, jnp.zeros((LANES - ROWS, LANES), F32)], axis=0)
    stored = ((lane < 2 * PAIRS) & (lane >= (row & ~7))) | (row >= 2 * PAIRS)
    correction = jnp.where(stored, half, square.T[0:ROWS])
    system = (data_gram - correction) * (1.0 / mean_sq)
    sys_ref[...] = system[0:WIDTH, 0:WIDTH]
    nrm_ref[...] = (mean * jnp.sqrt(mean_sq * (1.0 / ELEM_TOTAL)))[:, 0:WIDTH]

    copy_a.wait_send()
    for buf, count, index in (
        (sum_a, NZY, 0), (buf_x, NX * NC, 1), (buf_y, NY, 2), (buf_z, NZ, 3), (buf_m, QUAD, 4)
    ):
        rest = buf.at[pl.ds(0, count - 1)]
        pltpu.make_async_copy(rest, rest, send_sem.at[index]).wait()


def writer(red, sys, nrm, red_out, sys_out, nrm_out):
    red_out[...] = red[...]
    sys_out[...] = sys[...]
    nrm_out[...] = nrm[...]


def per_device(pole_freq, pole_damp, samples):
    vmem = lambda *shape: pltpu.VMEM(shape, F32)
    in_hbm = lambda v: pltpu.with_memory_space_constraint(v, pltpu.HBM)
    half = lambda *shape: pltpu.VMEM(shape, jnp.bfloat16)
    results = (
        vmem(OWN, WIDTH, WIDTH),
        vmem(WIDTH, WIDTH),
        vmem(1, WIDTH),
    )
    reduced, system, norm_row = pl.pallas_call(
        kernel,
        out_shape=results,
        in_specs=[pl.BlockSpec(memory_space=pltpu.HBM)] * 3,
        out_specs=(pl.BlockSpec(memory_space=pltpu.VMEM),) * 3,
        scratch_shapes=[
            pltpu.SMEM((PAIRS,), F32),
            pltpu.SMEM((PAIRS,), F32),
            vmem(2, FREQ_LOCAL, ELEM_LOCAL),
            half(2 * BASIS, FREQ_LOCAL),
            half(4 * PAIRS, FREQ_LOCAL),
            vmem(ELEM_LOCAL, LANES),
            vmem(NC, NZY, 8, LANES),
            vmem(NZY, 8, LANES),
            vmem(NZY, 8, LANES),
            vmem(NZY, 8, LANES),
            vmem(QUAD, 1, LANES),
            vmem(NX * NC, 8, LANES),
            vmem(NY, 8, LANES),
            vmem(NZ, 8, LANES),
            pltpu.SemaphoreType.DMA((2,)),
            pltpu.SemaphoreType.DMA((CHUNKS,)),
            pltpu.SemaphoreType.DMA((6,)),
            pltpu.SemaphoreType.DMA((6,)),
        ],
        compiler_params=pltpu.CompilerParams(
            collective_id=0, has_side_effects=True, vmem_limit_bytes=40 * 1024 * 1024
        ),
    )(*(in_hbm(v) for v in (pole_freq, pole_damp, samples)))
    in_vmem = lambda v: pltpu.with_memory_space_constraint(v, pltpu.VMEM)
    reduced, system, norm_row = pl.pallas_call(
        writer,
        out_shape=(
            jax.ShapeDtypeStruct((OWN, WIDTH, WIDTH), F32),
            jax.ShapeDtypeStruct((WIDTH, WIDTH), F32),
            jax.ShapeDtypeStruct((1, WIDTH), F32),
        ),
        in_specs=[pl.BlockSpec(memory_space=pltpu.VMEM)] * 3,
        out_specs=(pl.BlockSpec(memory_space=pltpu.VMEM),) * 3,
        compiler_params=pltpu.CompilerParams(vmem_limit_bytes=48 * 1024 * 1024),
    )(in_vmem(reduced), in_vmem(system), in_vmem(norm_row))
    return jnp.transpose(reduced, (1, 2, 0)), system, norm_row.reshape(WIDTH)


def solution(mesh):
    placed = (P(), P(), P(None, "freq", "elem"))
    return jax.shard_map(
        per_device,
        mesh=mesh,
        in_specs=placed,
        out_specs=(P(None, None, ("elem", "freq")), P(), P()),
        check_vma=False,
    )
```

```python
import jax
import jax.numpy as jnp
from jax import lax
from jax.experimental import pallas as pl
from jax.experimental.pallas import tpu as pltpu
from jax.sharding import PartitionSpec as P

HIGH = lax.Precision.HIGHEST
MESH = pl.DeviceIdType.MESH
F32 = jnp.float32

NX, NZH, NZL, NY, NC = 4, 4, 2, 8, 2
NZ = NZH * NZL
NZY = NZL * NY
NFREQ = NZY * NC
QUAD = NY // 2
PAIRS = 16
WIDTH = 2 * PAIRS + 1
ROWS = 40
BASIS = 48
OWN = 12
GROUP = 3
STRIDE = 40
TILES = OWN // GROUP
CHUNK = 256
CHUNKS = 4
LANES = 128
FREQ_LOCAL = 1024
ELEM_LOCAL = OWN * NFREQ
FREQ_TOTAL = FREQ_LOCAL * NFREQ
ELEM_TOTAL = ELEM_LOCAL * NX * NZH
INV_NF = 1.0 / FREQ_TOTAL


def iota(shape, dim):
    return lax.broadcasted_iota(jnp.int32, shape, dim)


def omega_of(half_position):
    return 0.02 + 0.98 * half_position / FREQ_TOTAL


def inverse_of(value):
    r = pltpu.reciprocal(value, approx=True)
    r = r * (2.0 - value * r)
    return r * (2.0 - value * r)


def split(value):
    high = value.astype(jnp.bfloat16)
    return high, (value - high.astype(F32)).astype(jnp.bfloat16)


def bf_dot(a, b):
    return jnp.dot(a, b, preferred_element_type=F32)


def wrap(value, size):
    return jnp.where(value >= size, value - size, value)


def tree_sum(values):
    values = list(values)
    while len(values) > 1:
        values = [a + b for a, b in zip(values[::2], values[1::2])] + values[len(values) & ~1 :]
    return values[0]


def pick(ref, index, shape):
    out = jnp.zeros(shape, F32)
    for m in range(PAIRS):
        out = jnp.where(index == m, ref[m], out)
    return out


def over_rows(col):
    return jnp.concatenate([col, col, jnp.zeros((8, LANES), F32)], axis=0)


def pair_coefs(ci, di, cj, dj, row_sum, col_sum):
    both = di + dj
    gap = cj - ci
    tot = ci + cj
    sq = both * both
    r1 = inverse_of(sq + gap * gap)
    r2 = inverse_of(sq + tot * tot)
    alpha, beta = both * r1, gap * r1
    gamma, delta = both * r2, -tot * r2
    ap, am = alpha + gamma, alpha - gamma
    bm, bp = beta - delta, beta + delta

    def table(di, bm, bp, row_sum, col_sum):
        ss, bd, bs, da = di * ap, di * bm, di * bp, di * am
        cr = jnp.where(row_sum, jnp.where(col_sum, ss, -bd), jnp.where(col_sum, bs, da))
        ce = jnp.where(row_sum, jnp.where(col_sum, bd, ss), jnp.where(col_sum, -da, bs))
        return cr, ce

    return table(di, bm, bp, row_sum, col_sum) + table(dj, -bp, -bm, col_sum, row_sum)


def coef_tables(c_col, d_col, pf, pd):
    shape = (ROWS, LANES)
    row, col = iota(shape, 0), iota(shape, 1)
    small = iota((8, LANES), 1) & (PAIRS - 1)
    cj, dj = pick(pf, small, (8, LANES)), pick(pd, small, (8, LANES))
    tall = lambda v: jnp.concatenate([v] * (ROWS // 8), axis=0)
    inside = (row < 2 * PAIRS) & (col < 2 * PAIRS)
    cr, ce, crt, cet = pair_coefs(
        over_rows(c_col), over_rows(d_col), tall(cj), tall(dj), row < PAIRS, col < PAIRS
    )
    last_row = row == 2 * PAIRS
    last_col = col == 2 * PAIRS
    one = lambda cond: jnp.where(cond, 1.0, 0.0).astype(F32)
    cr = jnp.where(inside, cr, one(last_row & ((col < PAIRS) | last_col)))
    ce = jnp.where(inside, ce, one(last_row & (col >= PAIRS) & (col < 2 * PAIRS)))
    crt = jnp.where(inside, crt, one(last_col & (row < PAIRS)))
    cet = jnp.where(inside, cet, one(last_col & (row >= PAIRS) & (row < 2 * PAIRS)))
    return cr, ce, crt, cet


def assemble(tables, r_row, e_row, r_col, e_col):
    cr, ce, crt, cet = tables
    return cr * r_row + ce * e_row + crt * over_rows(r_col) + cet * over_rows(e_col)


def row_to_col(row_vec, first):
    row, lane = iota((PAIRS, LANES), 0), iota((PAIRS, LANES), 1)
    kept = jnp.where(lane == row + first, jnp.broadcast_to(row_vec, (PAIRS, LANES)), 0.0)
    return jnp.broadcast_to(jnp.sum(kept, axis=1, keepdims=True), (PAIRS, LANES))


def rows_from(values):
    lane = iota(values.shape, 1)
    j = lane - jnp.where(lane >= 2 * STRIDE, 2 * STRIDE, jnp.where(lane >= STRIDE, STRIDE, 0))
    r_row = jnp.where(
        j < PAIRS,
        values,
        jnp.where(j < 2 * PAIRS, pltpu.roll(values, PAIRS, 1), jnp.where(j == 2 * PAIRS, values, 0.0)),
    )
    e_row = jnp.where(
        j < PAIRS,
        pltpu.roll(values, LANES - PAIRS, 1),
        jnp.where(j < 2 * PAIRS, values, 0.0),
    )
    return r_row, e_row


def eliminate(work):
    parts = [work[8 * b : 8 * b + 8] for b in range(ROWS // 8)]
    sub = iota((8, LANES), 0)
    for first in range(0, WIDTH, 8):
        count = min(8, WIDTH - first)
        b0 = first // 8
        live = range(b0, len(parts))
        cols = [
            [jnp.broadcast_to(parts[b][:, first + t : first + t + 1], (8, LANES)) for b in live]
            for t in range(count)
        ]
        rows = [parts[b0][t : t + 1, :] for t in range(count)]
        for t in range(count):
            inv = inverse_of(cols[t][0][t : t + 1, :])
            factor = [v * inv for v in cols[t]]
            factor[0] = jnp.where(sub > t, factor[0], 0.0)
            for u in range(t + 1, count):
                lead = cols[u][0][t : t + 1, :]
                cols[u] = [v - f * lead for v, f in zip(cols[u], factor)]
                rows[u] = rows[u] - factor[0][u : u + 1, :] * rows[t]
            for n, b in enumerate(live):
                parts[b] = parts[b] - factor[n] * rows[t]
    return jnp.concatenate(parts, axis=0)


def kernel(
    pf_hbm, pd_hbm, s_hbm, red_ref, sys_ref, nrm_ref,
    pf, pd, s_buf, re_buf, im_buf, xt_buf, pieces, recv_a, sum_a, recv_z, sum_z, recv_b,
    buf_m, buf_x, buf_y, buf_z,
    pole_sem, load_sem, send_sem, recv_sem,
):
    elem, freq = lax.axis_index("elem"), lax.axis_index("freq")
    x, z_hi = elem // NZH, elem % NZH
    zy, core = freq // NC, freq % NC
    z_lo, y = zy // NY, zy % NY
    z = z_hi * NZL + z_lo

    def at_freq(other):
        return {"elem": elem, "freq": other}

    def at_y(other):
        return {"elem": elem, "freq": (z_lo * NY + other) * NC + core}

    def far_first(size):
        return sorted(range(size), key=lambda d: -min(d, size - d))

    sibling = at_freq(zy * NC + (1 - core))
    y_peers = [at_y(wrap(y + dy, NY)) for dy in far_first(NY) if dy]
    z_peers = []
    for dz in far_first(NZ):
        if dz:
            to = wrap(z + dz, NZ)
            hi = to // NZL
            z_peers.append({"elem": x * NZH + hi, "freq": ((to - hi * NZL) * NY + y) * NC + core})
    x_peers = []
    for dx in far_first(NX):
        for c in (1, 0):
            if dx or c:
                to = wrap(x + dx, NX)
                x_peers.append({"elem": to * NZH + z_hi, "freq": zy * NC + wrap(core + c, NC)})
    z_neighbour = at_freq(((1 - z_lo) * NY + y) * NC + core)

    pole_loads = [
        pltpu.make_async_copy(pf_hbm, pf, pole_sem.at[0]),
        pltpu.make_async_copy(pd_hbm, pd, pole_sem.at[1]),
    ]
    for load in pole_loads:
        load.start()
    loads = {}
    for k in range(CHUNKS):
        for part in range(2):
            at = pl.ds(k * CHUNK, CHUNK)
            loads[part, k] = pltpu.make_async_copy(
                s_hbm.at[part, at], s_buf.at[part, at], load_sem.at[part, k]
            )
            loads[part, k].start()

    barrier = pltpu.get_barrier_semaphore()

    def greet(device):
        pl.semaphore_signal(barrier, inc=1, device_id=device, device_id_type=MESH)

    greets = y_peers + z_peers + x_peers
    for device in greets:
        greet(device)
    greeted = len(greets)

    for load in pole_loads:
        load.wait()

    column = iota((PAIRS, LANES), 0)
    c_col = pick(pf, column, (PAIRS, LANES))
    d_col = pick(pd, column, (PAIRS, LANES))
    d_sq = d_col * d_col
    half16 = iota((PAIRS, LANES), 1).astype(F32) + 0.5
    base = (freq * FREQ_LOCAL).astype(F32)
    ones = jnp.where(iota((PAIRS, FREQ_LOCAL), 0) == 0, 1.0, 0.0)
    re_buf[2 * PAIRS : BASIS, :] = ones.astype(jnp.bfloat16)
    re_buf[BASIS + 2 * PAIRS :, :] = jnp.zeros((PAIRS, FREQ_LOCAL), jnp.bfloat16)
    for tile in range(FREQ_LOCAL // LANES):
        at = pl.ds(tile * LANES, LANES)
        w = omega_of(half16 + (base + tile * LANES))
        below, above = w - c_col, w + c_col
        i1 = inverse_of(d_sq + below * below)
        i2 = inverse_of(d_sq + above * above)
        first, second = below * i1, above * i2
        re_buf[0:PAIRS, at], re_buf[BASIS : BASIS + PAIRS, at] = split(d_sq * (i1 + i2))
        re_buf[PAIRS : 2 * PAIRS, at], re_buf[BASIS + PAIRS : BASIS + 2 * PAIRS, at] = split(
            d_col * (first - second)
        )
        im_buf[0:PAIRS, at], im_buf[2 * PAIRS : 3 * PAIRS, at] = split(-d_col * (first + second))
        im_buf[PAIRS : 2 * PAIRS, at], im_buf[3 * PAIRS :, at] = split(d_sq * (i1 - i2))

    quad = y % QUAD
    share = NFREQ // QUAD
    halves = [slice(0, 8), slice(8, 16)]

    def mean_step(step, acc):
        acc = list(acc)
        start = ((quad * share + step) * FREQ_LOCAL).astype(F32)
        for tile in range(FREQ_LOCAL // LANES):
            w = omega_of(half16[0:8] + (start + tile * LANES))
            for h in range(2):
                below, above = w - c_col[halves[h]], w + c_col[halves[h]]
                n1 = d_sq[halves[h]] + below * below
                n2 = d_sq[halves[h]] + above * above
                r = inverse_of(n1 * n2)
                acc[2 * h] = acc[2 * h] + r * (n1 + n2)
                acc[2 * h + 1] = acc[2 * h + 1] + r * (below * n2 - above * n1)
        return tuple(acc)

    acc = lax.fori_loop(0, share, mean_step, (jnp.zeros((8, LANES), F32),) * 4)
    lane16 = iota((PAIRS, LANES), 1)
    sum_r = d_sq * jnp.sum(jnp.concatenate([acc[0], acc[2]], axis=0), axis=1, keepdims=True)
    sum_e = d_col * jnp.sum(jnp.concatenate([acc[1], acc[3]], axis=0), axis=1, keepdims=True)
    sums = jnp.where(lane16 == column, sum_r, jnp.where(lane16 == column + PAIRS, sum_e, 0.0))
    buf_m[quad] = jnp.sum(sums, axis=0, keepdims=True)

    x0 = jnp.zeros((BASIS, ELEM_LOCAL + LANES), F32)
    x1 = jnp.zeros((2 * PAIRS, ELEM_LOCAL), F32)
    for k in range(CHUNKS):
        at = pl.ds(k * CHUNK, CHUNK)
        loads[0, k].wait()
        loads[1, k].wait()
        s0, s1 = s_buf[0, at, :], s_buf[1, at, :]
        squares = s0 * s0 + s1 * s1
        power = tree_sum(squares[:, t * LANES : (t + 1) * LANES] for t in range(ELEM_LOCAL // LANES))
        high, low = split(jnp.concatenate([s0, power], axis=1))
        both = bf_dot(re_buf[:, at], high)
        x0 = x0 + (both[0:BASIS] + both[BASIS:] + bf_dot(re_buf[0:BASIS, at], low))
        high, low = split(s1)
        both = bf_dot(im_buf[:, at], high)
        x1 = x1 + (both[0 : 2 * PAIRS] + both[2 * PAIRS :] + bf_dot(im_buf[0 : 2 * PAIRS, at], low))
    x0, q = x0[:, 0:ELEM_LOCAL], x0[0:ROWS, ELEM_LOCAL:]

    stacked = jnp.concatenate(
        [
            x0,
            jnp.zeros((64 - BASIS, ELEM_LOCAL), F32),
            x1,
            jnp.zeros((LANES - 64 - 2 * PAIRS, ELEM_LOCAL), F32),
        ],
        axis=0,
    )
    for tile in range(ELEM_LOCAL // LANES):
        at = slice(tile * LANES, (tile + 1) * LANES)
        xt_buf[at, :] = stacked[:, at].T
    count = ELEM_LOCAL // GROUP
    thirds = [xt_buf[pl.ds(q, count, stride=GROUP), :] for q in range(GROUP)]
    lane_c = iota((count, LANES), 1)

    def spread(shift):
        rolled = [
            pltpu.roll(thirds[q], (STRIDE * q + shift) % LANES, 1) if (STRIDE * q + shift) % LANES else thirds[q]
            for q in range(GROUP)
        ]
        return jnp.where(
            lane_c < STRIDE, rolled[0], jnp.where(lane_c < 2 * STRIDE, rolled[1], rolled[2])
        )

    part0, part1 = spread(0), spread(64)
    upper = iota((8, LANES), 0) < 4
    for k in range(NZY):
        v0, v1 = part0[8 * k : 8 * k + 8], part1[8 * k : 8 * k + 8]
        pieces[0, k] = jnp.where(upper, v0, pltpu.roll(v1, 4, 0))
        pieces[1, k] = jnp.where(upper, pltpu.roll(v0, 4, 0), v1)

    pl.semaphore_wait(barrier, greeted)

    copy_a = pltpu.make_async_remote_copy(
        src_ref=pieces.at[1 - core],
        dst_ref=recv_a,
        send_sem=send_sem.at[5],
        recv_sem=recv_sem.at[5],
        device_id=sibling,
        device_id_type=MESH,
    )
    copy_a.start()
    for step in range(1, QUAD):
        other = y - quad + wrap(quad + step, QUAD)
        pltpu.make_async_remote_copy(
            src_ref=buf_m.at[quad],
            dst_ref=buf_m.at[quad],
            send_sem=send_sem.at[4],
            recv_sem=recv_sem.at[4],
            device_id=at_y(other),
            device_id_type=MESH,
        ).start()

    copy_a.wait_recv()
    for k in range(NZY):
        sum_a[k] = pieces[core, k] + recv_a[k]
    copy_z = pltpu.make_async_remote_copy(
        src_ref=sum_a.at[pl.ds((1 - z_lo) * NY, NY)],
        dst_ref=recv_z,
        send_sem=send_sem.at[6],
        recv_sem=recv_sem.at[6],
        device_id=z_neighbour,
        device_id_type=MESH,
    )
    copy_z.start()
    tables = coef_tables(c_col, d_col, pf, pd)
    copy_z.wait_recv()
    for k in range(NY):
        sum_z[k] = sum_a[z_lo * NY + k] + recv_z[k]
    for dy in far_first(NY):
        if dy:
            other = wrap(y + dy, NY)
            pltpu.make_async_remote_copy(
                src_ref=sum_z.at[other],
                dst_ref=recv_b.at[y],
                send_sem=send_sem.at[0],
                recv_sem=recv_sem.at[0],
                device_id=at_y(other),
                device_id_type=MESH,
            ).start()
    recv_b[y] = sum_z[y]

    rest = buf_m.at[pl.ds(0, QUAD - 1)]
    pltpu.make_async_copy(rest, rest, recv_sem.at[4]).wait()
    mean = tree_sum(buf_m[k] for k in range(QUAD)) * INV_NF
    lane1 = iota((1, LANES), 1)
    mean = jnp.where(lane1 == 2 * PAIRS, 1.0, mean)
    r_row, e_row = rows_from(mean)
    gram = assemble(tables, r_row, e_row, row_to_col(mean, 0), row_to_col(mean, PAIRS))
    row, lane = iota((ROWS, LANES), 0), iota((ROWS, LANES), 1)
    work = gram + jnp.where((lane == row + 64) & (row < WIDTH), 1.0, 0.0)
    work = eliminate(work)
    pivots = jnp.sum(jnp.where((lane == row) & (row < WIDTH), work, 0.0), axis=1, keepdims=True)
    pivots = jnp.where(iota((ROWS, 1), 0) < WIDTH, pivots, 1.0)
    inverse = pltpu.roll(work, 64, 1) * (1.0 / jnp.sqrt(pivots))
    inverse = jnp.where(lane < WIDTH, inverse, 0.0)

    q = jnp.broadcast_to(jnp.sum(q, axis=1, keepdims=True), (ROWS, LANES))
    q_row = jnp.sum(jnp.where(lane == row, q, 0.0), axis=0, keepdims=True)

    triple = [
        v + pltpu.roll(v, STRIDE, 1) + pltpu.roll(v, 2 * STRIDE, 1) for v in tables
    ]

    rest_b = recv_b.at[pl.ds(0, NY - 1)]
    pltpu.make_async_copy(rest_b, rest_b, recv_sem.at[0]).wait()
    owned = tree_sum(recv_b[k] for k in range(NY))
    owned = owned * (-INV_NF)

    other_part = pltpu.roll(owned, 4, 0)
    plus, minus = owned + other_part, owned - other_part
    r_rows, e_rows = rows_from(minus)
    plus_t = jnp.concatenate([plus, jnp.zeros((LANES - 8, LANES), F32)], axis=0).T
    lane16 = iota((PAIRS, LANES), 1)

    def columns(g, first):
        spread_col = [
            jnp.broadcast_to(
                plus_t[STRIDE * q + first : STRIDE * q + first + PAIRS, g : g + 1], (PAIRS, LANES)
            )
            for q in range(GROUP)
        ]
        return jnp.where(
            lane16 < STRIDE, spread_col[0], jnp.where(lane16 < 2 * STRIDE, spread_col[1], spread_col[2])
        )

    coupling = jnp.concatenate(
        [
            assemble(triple, r_rows[g : g + 1, :], e_rows[g : g + 1, :], columns(g, 0), columns(g, PAIRS))
            for g in range(TILES)
        ],
        axis=1,
    )
    reduced = jnp.dot(
        inverse[:, 0:ROWS], coupling, precision=HIGH, preferred_element_type=F32
    )
    parts = [reduced[:, g * LANES : (g + 1) * LANES] for g in range(TILES)]
    tall = jnp.concatenate(parts, axis=0)
    wide = jnp.dot(tall.T, tall, precision=HIGH, preferred_element_type=F32)
    corr = wide[0:ROWS]
    for q in range(1, GROUP):
        at = STRIDE * q
        corr = corr + pltpu.roll(wide[at : at + ROWS], LANES - at, 1)

    sub8, ln8 = iota((8, LANES), 0), iota((8, LANES), 1)
    spread8 = lambda v: jnp.broadcast_to(v, (8, LANES))
    border = jnp.where(
        sub8 == 0, spread8(corr[32:33]), jnp.where(sub8 == 1, spread8(q_row), 0.0)
    )
    packed = pltpu.roll(border, 80, 1)
    for g, first, shift in ((3, 80, 48), (2, 72, 40), (1, 56, 24)):
        packed = jnp.where(ln8 < first, pltpu.roll(corr[8 * g : 8 * g + 8], shift, 1), packed)
    total = jnp.where(ln8 < 32, corr[0:8], packed)

    def send(buf, me, peers, index, value):
        buf[me] = value
        for device in peers:
            pltpu.make_async_remote_copy(
                src_ref=buf.at[me],
                dst_ref=buf.at[me],
                send_sem=send_sem.at[index],
                recv_sem=recv_sem.at[index],
                device_id=device,
                device_id_type=MESH,
            ).start()

    def receive(buf, count, index):
        rest = buf.at[pl.ds(0, count - 1)]
        pltpu.make_async_copy(rest, rest, recv_sem.at[index]).wait()
        return tree_sum(buf[k] for k in range(count))

    send(buf_x, x * NC + core, x_peers, 1, total)

    for g in range(TILES):
        for q in range(GROUP):
            block = pltpu.roll(parts[g], LANES - STRIDE * q, 1) if q else parts[g]
            red_ref[GROUP * g + q] = block[0:WIDTH, 0:WIDTH]

    total = receive(buf_x, NX * NC, 1)
    send(buf_y, y, y_peers, 2, total)
    total = receive(buf_y, NY, 2)
    send(buf_z, z, z_peers, 3, total)
    total = receive(buf_z, NZ, 3)

    border = pltpu.roll(total, LANES - 80, 1)
    moments = jnp.where(lane1 < WIDTH, border[1:2], 0.0) * INV_NF
    mean_sq = moments[:, 2 * PAIRS : 2 * PAIRS + 1]
    r_row, e_row = rows_from(moments)
    data_gram = assemble(
        tables, r_row, e_row, row_to_col(moments, 0), row_to_col(moments, PAIRS)
    )
    half = jnp.concatenate(
        [total]
        + [pltpu.roll(total, LANES - shift, 1) for shift in (24, 40, 48)]
        + [spread8(border[0:1])],
        axis=0,
    )
    square = jnp.concatenate([half, jnp.zeros((LANES - ROWS, LANES), F32)], axis=0)
    stored = ((lane < 2 * PAIRS) & (lane >= (row & ~7))) | (row >= 2 * PAIRS)
    correction = jnp.where(stored, half, square.T[0:ROWS])
    system = (data_gram - correction) * (1.0 / mean_sq)
    sys_ref[...] = system[0:WIDTH, 0:WIDTH]
    nrm_ref[...] = (mean * jnp.sqrt(mean_sq * (1.0 / ELEM_TOTAL)))[:, 0:WIDTH]

    copy_a.wait_send()
    copy_z.wait_send()
    for buf, count, index in (
        (sum_z, NY, 0), (buf_x, NX * NC, 1), (buf_y, NY, 2), (buf_z, NZ, 3), (buf_m, QUAD, 4)
    ):
        rest = buf.at[pl.ds(0, count - 1)]
        pltpu.make_async_copy(rest, rest, send_sem.at[index]).wait()


def writer(red, sys, nrm, red_out, sys_out, nrm_out):
    red_out[...] = red[...]
    sys_out[...] = sys[...]
    nrm_out[...] = nrm[...]


def per_device(pole_freq, pole_damp, samples):
    vmem = lambda *shape: pltpu.VMEM(shape, F32)
    in_hbm = lambda v: pltpu.with_memory_space_constraint(v, pltpu.HBM)
    half = lambda *shape: pltpu.VMEM(shape, jnp.bfloat16)
    results = (
        vmem(OWN, WIDTH, WIDTH),
        vmem(WIDTH, WIDTH),
        vmem(1, WIDTH),
    )
    reduced, system, norm_row = pl.pallas_call(
        kernel,
        out_shape=results,
        in_specs=[pl.BlockSpec(memory_space=pltpu.HBM)] * 3,
        out_specs=(pl.BlockSpec(memory_space=pltpu.VMEM),) * 3,
        scratch_shapes=[
            pltpu.SMEM((PAIRS,), F32),
            pltpu.SMEM((PAIRS,), F32),
            vmem(2, FREQ_LOCAL, ELEM_LOCAL),
            half(2 * BASIS, FREQ_LOCAL),
            half(4 * PAIRS, FREQ_LOCAL),
            vmem(ELEM_LOCAL, LANES),
            vmem(NC, NZY, 8, LANES),
            vmem(NZY, 8, LANES),
            vmem(NZY, 8, LANES),
            vmem(NY, 8, LANES),
            vmem(NY, 8, LANES),
            vmem(NY, 8, LANES),
            vmem(QUAD, 1, LANES),
            vmem(NX * NC, 8, LANES),
            vmem(NY, 8, LANES),
            vmem(NZ, 8, LANES),
            pltpu.SemaphoreType.DMA((2,)),
            pltpu.SemaphoreType.DMA((2, CHUNKS)),
            pltpu.SemaphoreType.DMA((7,)),
            pltpu.SemaphoreType.DMA((7,)),
        ],
        compiler_params=pltpu.CompilerParams(
            collective_id=0, has_side_effects=True, vmem_limit_bytes=40 * 1024 * 1024
        ),
    )(*(in_hbm(v) for v in (pole_freq, pole_damp, samples)))
    in_vmem = lambda v: pltpu.with_memory_space_constraint(v, pltpu.VMEM)
    reduced, system, norm_row = pl.pallas_call(
        writer,
        out_shape=(
            jax.ShapeDtypeStruct((OWN, WIDTH, WIDTH), F32),
            jax.ShapeDtypeStruct((WIDTH, WIDTH), F32),
            jax.ShapeDtypeStruct((1, WIDTH), F32),
        ),
        in_specs=[pl.BlockSpec(memory_space=pltpu.VMEM)] * 3,
        out_specs=(pl.BlockSpec(memory_space=pltpu.VMEM),) * 3,
        compiler_params=pltpu.CompilerParams(vmem_limit_bytes=48 * 1024 * 1024),
    )(in_vmem(reduced), in_vmem(system), in_vmem(norm_row))
    return jnp.transpose(reduced, (1, 2, 0)), system, norm_row.reshape(WIDTH)


def solution(mesh):
    placed = (P(), P(), P(None, "freq", "elem"))
    return jax.shard_map(
        per_device,
        mesh=mesh,
        in_specs=placed,
        out_specs=(P(None, None, ("elem", "freq")), P(), P()),
        check_vma=False,
    )
```

```python
import jax
import jax.numpy as jnp
from jax import lax
from jax.experimental import pallas as pl
from jax.experimental.pallas import tpu as pltpu
from jax.sharding import PartitionSpec as P

HIGH = lax.Precision.HIGHEST
MESH = pl.DeviceIdType.MESH
F32 = jnp.float32

NX, NZH, NZL, NY, NC = 4, 4, 2, 8, 2
NZ = NZH * NZL
NZY = NZL * NY
NFREQ = NZY * NC
QUAD = NZL * NC
PAIRS = 16
WIDTH = 2 * PAIRS + 1
ROWS = 40
BASIS = 48
OWN = 12
GROUP = 3
STRIDE = 40
TILES = OWN // GROUP
SUMS = 6
CHUNK = 256
CHUNKS = 4
LANES = 128
FREQ_LOCAL = 1024
ELEM_LOCAL = OWN * NFREQ
FREQ_TOTAL = FREQ_LOCAL * NFREQ
ELEM_TOTAL = ELEM_LOCAL * NX * NZH
INV_NF = 1.0 / FREQ_TOTAL


def iota(shape, dim):
    return lax.broadcasted_iota(jnp.int32, shape, dim)


def omega_of(half_position):
    return 0.02 + 0.98 * half_position / FREQ_TOTAL


def inverse_of(value):
    r = pltpu.reciprocal(value, approx=True)
    r = r * (2.0 - value * r)
    return r * (2.0 - value * r)


def split(value):
    high = value.astype(jnp.bfloat16)
    return high, (value - high.astype(F32)).astype(jnp.bfloat16)


def bf_dot(a, b):
    return jnp.dot(a, b, preferred_element_type=F32)


def wrap(value, size):
    return jnp.where(value >= size, value - size, value)


def tree_sum(values):
    values = list(values)
    while len(values) > 1:
        values = [a + b for a, b in zip(values[::2], values[1::2])] + values[len(values) & ~1 :]
    return values[0]


def pick(ref, index, shape):
    out = jnp.zeros(shape, F32)
    for m in range(PAIRS):
        out = jnp.where(index == m, ref[m], out)
    return out


def over_rows(col):
    return jnp.concatenate([col, col, jnp.zeros((8, LANES), F32)], axis=0)


def pair_coefs(ci, di, cj, dj, row_sum, col_sum):
    both = di + dj
    gap = cj - ci
    tot = ci + cj
    sq = both * both
    r1 = inverse_of(sq + gap * gap)
    r2 = inverse_of(sq + tot * tot)
    alpha, beta = both * r1, gap * r1
    gamma, delta = both * r2, -tot * r2
    ap, am = alpha + gamma, alpha - gamma
    bm, bp = beta - delta, beta + delta

    def table(di, bm, bp, row_sum, col_sum):
        ss, bd, bs, da = di * ap, di * bm, di * bp, di * am
        cr = jnp.where(row_sum, jnp.where(col_sum, ss, -bd), jnp.where(col_sum, bs, da))
        ce = jnp.where(row_sum, jnp.where(col_sum, bd, ss), jnp.where(col_sum, -da, bs))
        return cr, ce

    return table(di, bm, bp, row_sum, col_sum) + table(dj, -bp, -bm, col_sum, row_sum)


def coef_tables(c_col, d_col, pf, pd):
    shape = (ROWS, LANES)
    row, col = iota(shape, 0), iota(shape, 1)
    small = iota((8, LANES), 1) & (PAIRS - 1)
    cj, dj = pick(pf, small, (8, LANES)), pick(pd, small, (8, LANES))
    tall = lambda v: jnp.concatenate([v] * (ROWS // 8), axis=0)
    inside = (row < 2 * PAIRS) & (col < 2 * PAIRS)
    cr, ce, crt, cet = pair_coefs(
        over_rows(c_col), over_rows(d_col), tall(cj), tall(dj), row < PAIRS, col < PAIRS
    )
    last_row = row == 2 * PAIRS
    last_col = col == 2 * PAIRS
    one = lambda cond: jnp.where(cond, 1.0, 0.0).astype(F32)
    cr = jnp.where(inside, cr, one(last_row & ((col < PAIRS) | last_col)))
    ce = jnp.where(inside, ce, one(last_row & (col >= PAIRS) & (col < 2 * PAIRS)))
    crt = jnp.where(inside, crt, one(last_col & (row < PAIRS)))
    cet = jnp.where(inside, cet, one(last_col & (row >= PAIRS) & (row < 2 * PAIRS)))
    return cr, ce, crt, cet


def assemble(tables, r_row, e_row, r_col, e_col):
    cr, ce, crt, cet = tables
    return cr * r_row + ce * e_row + crt * over_rows(r_col) + cet * over_rows(e_col)


def row_to_col(row_vec, first):
    row, lane = iota((PAIRS, LANES), 0), iota((PAIRS, LANES), 1)
    kept = jnp.where(lane == row + first, jnp.broadcast_to(row_vec, (PAIRS, LANES)), 0.0)
    return jnp.broadcast_to(jnp.sum(kept, axis=1, keepdims=True), (PAIRS, LANES))


def rows_from(values):
    lane = iota(values.shape, 1)
    j = lane - jnp.where(lane >= 2 * STRIDE, 2 * STRIDE, jnp.where(lane >= STRIDE, STRIDE, 0))
    r_row = jnp.where(
        j < PAIRS,
        values,
        jnp.where(j < 2 * PAIRS, pltpu.roll(values, PAIRS, 1), jnp.where(j == 2 * PAIRS, values, 0.0)),
    )
    e_row = jnp.where(
        j < PAIRS,
        pltpu.roll(values, LANES - PAIRS, 1),
        jnp.where(j < 2 * PAIRS, values, 0.0),
    )
    return r_row, e_row


def eliminate(work):
    parts = [work[8 * b : 8 * b + 8] for b in range(ROWS // 8)]
    sub = iota((8, LANES), 0)
    for first in range(0, WIDTH, 8):
        count = min(8, WIDTH - first)
        b0 = first // 8
        live = range(b0, len(parts))
        cols = [
            [jnp.broadcast_to(parts[b][:, first + t : first + t + 1], (8, LANES)) for b in live]
            for t in range(count)
        ]
        rows = [parts[b0][t : t + 1, :] for t in range(count)]
        for t in range(count):
            inv = inverse_of(cols[t][0][t : t + 1, :])
            factor = [v * inv for v in cols[t]]
            factor[0] = jnp.where(sub > t, factor[0], 0.0)
            for u in range(t + 1, count):
                lead = cols[u][0][t : t + 1, :]
                cols[u] = [v - f * lead for v, f in zip(cols[u], factor)]
                rows[u] = rows[u] - factor[0][u : u + 1, :] * rows[t]
            for n, b in enumerate(live):
                parts[b] = parts[b] - factor[n] * rows[t]
    return jnp.concatenate(parts, axis=0)


def kernel(
    pf_hbm, pd_hbm, s_hbm, red_ref, sys_ref, nrm_ref,
    pf, pd, s_buf, re_buf, im_buf, xt_buf, pieces, recv_a, sum_a, recv_b,
    buf_m, buf_x, buf_y, buf_z,
    pole_sem, load_sem, send_sem, recv_sem,
):
    elem, freq = lax.axis_index("elem"), lax.axis_index("freq")
    x, z_hi = elem // NZH, elem % NZH
    zy, core = freq // NC, freq % NC
    z_lo, y = zy // NY, zy % NY
    z = z_hi * NZL + z_lo

    def at_freq(other):
        return {"elem": elem, "freq": other}

    def at_y(other):
        return {"elem": elem, "freq": (z_lo * NY + other) * NC + core}

    def far_first(size):
        return sorted(range(size), key=lambda d: -min(d, size - d))

    sibling = at_freq(zy * NC + (1 - core))
    zy_peers = [
        wrap(z_lo + dz, NZL) * NY + wrap(y + dy, NY)
        for dy in far_first(NY)
        for dz in (1, 0)
        if dy or dz
    ]
    y_peers = [at_y(wrap(y + dy, NY)) for dy in far_first(NY) if dy]
    z_peers = []
    for dz in far_first(NZ):
        if dz:
            to = wrap(z + dz, NZ)
            hi = to // NZL
            z_peers.append({"elem": x * NZH + hi, "freq": ((to - hi * NZL) * NY + y) * NC + core})
    x_peers = []
    for dx in far_first(NX):
        for c in (1, 0):
            if dx or c:
                to = wrap(x + dx, NX)
                x_peers.append({"elem": to * NZH + z_hi, "freq": zy * NC + wrap(core + c, NC)})
    corner = at_freq((wrap(z_lo + 1, NZL) * NY + y) * NC + (1 - core))

    pole_loads = [
        pltpu.make_async_copy(pf_hbm, pf, pole_sem.at[0]),
        pltpu.make_async_copy(pd_hbm, pd, pole_sem.at[1]),
    ]
    for load in pole_loads:
        load.start()
    loads = {}
    for k in range(CHUNKS):
        for part in range(2):
            at = pl.ds(k * CHUNK, CHUNK)
            loads[part, k] = pltpu.make_async_copy(
                s_hbm.at[part, at], s_buf.at[part, at], load_sem.at[part, k]
            )
            loads[part, k].start()

    barrier = pltpu.get_barrier_semaphore()

    def greet(device):
        pl.semaphore_signal(barrier, inc=1, device_id=device, device_id_type=MESH)

    z_rest = []
    for hi_step in range(1, NZH):
        hi = wrap(z_hi + hi_step, NZH)
        z_rest += [{"elem": x * NZH + hi, "freq": (lo * NY + y) * NC + core} for lo in range(NZL)]
    greets = [at_freq(zy_peer * NC + core) for zy_peer in zy_peers]
    greets += [corner] + z_rest + x_peers
    for device in greets:
        greet(device)
    greeted = len(greets)

    for load in pole_loads:
        load.wait()

    column = iota((PAIRS, LANES), 0)
    c_col = pick(pf, column, (PAIRS, LANES))
    d_col = pick(pd, column, (PAIRS, LANES))
    d_sq = d_col * d_col
    half16 = iota((PAIRS, LANES), 1).astype(F32) + 0.5
    base = (freq * FREQ_LOCAL).astype(F32)
    ones = jnp.where(iota((PAIRS, FREQ_LOCAL), 0) == 0, 1.0, 0.0)
    re_buf[2 * PAIRS : BASIS, :] = ones.astype(jnp.bfloat16)
    re_buf[BASIS + 2 * PAIRS :, :] = jnp.zeros((PAIRS, FREQ_LOCAL), jnp.bfloat16)
    for tile in range(FREQ_LOCAL // LANES):
        at = pl.ds(tile * LANES, LANES)
        w = omega_of(half16 + (base + tile * LANES))
        below, above = w - c_col, w + c_col
        i1 = inverse_of(d_sq + below * below)
        i2 = inverse_of(d_sq + above * above)
        first, second = below * i1, above * i2
        re_buf[0:PAIRS, at], re_buf[BASIS : BASIS + PAIRS, at] = split(d_sq * (i1 + i2))
        re_buf[PAIRS : 2 * PAIRS, at], re_buf[BASIS + PAIRS : BASIS + 2 * PAIRS, at] = split(
            d_col * (first - second)
        )
        im_buf[0:PAIRS, at], im_buf[2 * PAIRS : 3 * PAIRS, at] = split(-d_col * (first + second))
        im_buf[PAIRS : 2 * PAIRS, at], im_buf[3 * PAIRS :, at] = split(d_sq * (i1 - i2))

    quad = z_lo * NC + core
    share = NFREQ // QUAD
    halves = [slice(0, 8), slice(8, 16)]

    def mean_step(step, acc):
        acc = list(acc)
        start = ((quad * share + step) * FREQ_LOCAL).astype(F32)
        for tile in range(FREQ_LOCAL // LANES):
            w = omega_of(half16[0:8] + (start + tile * LANES))
            for h in range(2):
                below, above = w - c_col[halves[h]], w + c_col[halves[h]]
                n1 = d_sq[halves[h]] + below * below
                n2 = d_sq[halves[h]] + above * above
                r = inverse_of(n1 * n2)
                acc[2 * h] = acc[2 * h] + r * (n1 + n2)
                acc[2 * h + 1] = acc[2 * h + 1] + r * (below * n2 - above * n1)
        return tuple(acc)

    acc = lax.fori_loop(0, share, mean_step, (jnp.zeros((8, LANES), F32),) * 4)
    lane16 = iota((PAIRS, LANES), 1)
    sum_r = d_sq * jnp.sum(jnp.concatenate([acc[0], acc[2]], axis=0), axis=1, keepdims=True)
    sum_e = d_col * jnp.sum(jnp.concatenate([acc[1], acc[3]], axis=0), axis=1, keepdims=True)
    sums = jnp.where(lane16 == column, sum_r, jnp.where(lane16 == column + PAIRS, sum_e, 0.0))
    buf_m[quad] = jnp.sum(sums, axis=0, keepdims=True)

    x0 = jnp.zeros((BASIS, ELEM_LOCAL + LANES), F32)
    x1 = jnp.zeros((2 * PAIRS, ELEM_LOCAL), F32)
    for k in range(CHUNKS):
        at = pl.ds(k * CHUNK, CHUNK)
        loads[0, k].wait()
        loads[1, k].wait()
        s0, s1 = s_buf[0, at, :], s_buf[1, at, :]
        squares = s0 * s0 + s1 * s1
        power = tree_sum(squares[:, t * LANES : (t + 1) * LANES] for t in range(ELEM_LOCAL // LANES))
        high, low = split(jnp.concatenate([s0, power], axis=1))
        both = bf_dot(re_buf[:, at], high)
        x0 = x0 + (both[0:BASIS] + both[BASIS:] + bf_dot(re_buf[0:BASIS, at], low))
        high, low = split(s1)
        both = bf_dot(im_buf[:, at], high)
        x1 = x1 + (both[0 : 2 * PAIRS] + both[2 * PAIRS :] + bf_dot(im_buf[0 : 2 * PAIRS, at], low))
    x0, q = x0[:, 0:ELEM_LOCAL], x0[0:ROWS, ELEM_LOCAL:]

    stacked = jnp.concatenate(
        [
            x0,
            jnp.zeros((64 - BASIS, ELEM_LOCAL), F32),
            x1,
            jnp.zeros((LANES - 64 - 2 * PAIRS, ELEM_LOCAL), F32),
        ],
        axis=0,
    )
    for tile in range(ELEM_LOCAL // LANES):
        at = slice(tile * LANES, (tile + 1) * LANES)
        xt_buf[at, :] = stacked[:, at].T
    count = ELEM_LOCAL // GROUP
    thirds = [xt_buf[pl.ds(q, count, stride=GROUP), :] for q in range(GROUP)]
    lane_c = iota((count, LANES), 1)

    def spread(shift):
        rolled = [
            pltpu.roll(thirds[q], (STRIDE * q + shift) % LANES, 1) if (STRIDE * q + shift) % LANES else thirds[q]
            for q in range(GROUP)
        ]
        return jnp.where(
            lane_c < STRIDE, rolled[0], jnp.where(lane_c < 2 * STRIDE, rolled[1], rolled[2])
        )

    part0, part1 = spread(0), spread(64)
    upper = iota((8, LANES), 0) < 4
    for k in range(NZY):
        v0, v1 = part0[8 * k : 8 * k + 8], part1[8 * k : 8 * k + 8]
        pieces[0, k] = jnp.where(upper, v0, pltpu.roll(v1, 4, 0))
        pieces[1, k] = jnp.where(upper, pltpu.roll(v0, 4, 0), v1)

    pl.semaphore_wait(barrier, greeted)

    copy_a = pltpu.make_async_remote_copy(
        src_ref=pieces.at[1 - core],
        dst_ref=recv_a,
        send_sem=send_sem.at[5],
        recv_sem=recv_sem.at[5],
        device_id=sibling,
        device_id_type=MESH,
    )
    copy_a.start()
    for step in range(1, QUAD):
        lo, c = wrap(z_lo + step // NC, NZL), wrap(core + step % NC, NC)
        pltpu.make_async_remote_copy(
            src_ref=buf_m.at[quad],
            dst_ref=buf_m.at[quad],
            send_sem=send_sem.at[4],
            recv_sem=recv_sem.at[4],
            device_id=at_freq((lo * NY + y) * NC + c),
            device_id_type=MESH,
        ).start()

    tables = coef_tables(c_col, d_col, pf, pd)
    copy_a.wait_recv()
    for k in range(NZY):
        sum_a[k] = pieces[core, k] + recv_a[k]
    for other in zy_peers:
        pltpu.make_async_remote_copy(
            src_ref=sum_a.at[other],
            dst_ref=recv_b.at[zy],
            send_sem=send_sem.at[0],
            recv_sem=recv_sem.at[0],
            device_id=at_freq(other * NC + core),
            device_id_type=MESH,
        ).start()
    recv_b[zy] = sum_a[zy]

    rest = buf_m.at[pl.ds(0, QUAD - 1)]
    pltpu.make_async_copy(rest, rest, recv_sem.at[4]).wait()
    mean = tree_sum(buf_m[k] for k in range(QUAD)) * INV_NF
    lane1 = iota((1, LANES), 1)
    mean = jnp.where(lane1 == 2 * PAIRS, 1.0, mean)
    r_row, e_row = rows_from(mean)
    gram = assemble(tables, r_row, e_row, row_to_col(mean, 0), row_to_col(mean, PAIRS))
    row, lane = iota((ROWS, LANES), 0), iota((ROWS, LANES), 1)
    work = gram + jnp.where((lane == row + 64) & (row < WIDTH), 1.0, 0.0)
    work = eliminate(work)
    pivots = jnp.sum(jnp.where((lane == row) & (row < WIDTH), work, 0.0), axis=1, keepdims=True)
    pivots = jnp.where(iota((ROWS, 1), 0) < WIDTH, pivots, 1.0)
    inverse = pltpu.roll(work, 64, 1) * (1.0 / jnp.sqrt(pivots))
    inverse = jnp.where(lane < WIDTH, inverse, 0.0)

    q = jnp.broadcast_to(jnp.sum(q, axis=1, keepdims=True), (ROWS, LANES))
    q_row = jnp.sum(jnp.where(lane == row, q, 0.0), axis=0, keepdims=True)

    triple = [
        v + pltpu.roll(v, STRIDE, 1) + pltpu.roll(v, 2 * STRIDE, 1) for v in tables
    ]

    rest_b = recv_b.at[pl.ds(0, NZY - 1)]
    pltpu.make_async_copy(rest_b, rest_b, recv_sem.at[0]).wait()
    owned = tree_sum(recv_b[k] for k in range(NZY))
    owned = owned * (-INV_NF)

    other_part = pltpu.roll(owned, 4, 0)
    plus, minus = owned + other_part, owned - other_part
    r_rows, e_rows = rows_from(minus)
    plus_t = jnp.concatenate([plus, jnp.zeros((LANES - 8, LANES), F32)], axis=0).T
    lane16 = iota((PAIRS, LANES), 1)

    def columns(g, first):
        spread_col = [
            jnp.broadcast_to(
                plus_t[STRIDE * q + first : STRIDE * q + first + PAIRS, g : g + 1], (PAIRS, LANES)
            )
            for q in range(GROUP)
        ]
        return jnp.where(
            lane16 < STRIDE, spread_col[0], jnp.where(lane16 < 2 * STRIDE, spread_col[1], spread_col[2])
        )

    coupling = jnp.concatenate(
        [
            assemble(triple, r_rows[g : g + 1, :], e_rows[g : g + 1, :], columns(g, 0), columns(g, PAIRS))
            for g in range(TILES)
        ],
        axis=1,
    )
    reduced = jnp.dot(
        inverse[:, 0:ROWS], coupling, precision=HIGH, preferred_element_type=F32
    )
    parts = [reduced[:, g * LANES : (g + 1) * LANES] for g in range(TILES)]
    tall = jnp.concatenate(parts, axis=0)
    wide = jnp.dot(tall.T, tall, precision=HIGH, preferred_element_type=F32)
    corr = wide[0:ROWS]
    for q in range(1, GROUP):
        at = STRIDE * q
        corr = corr + pltpu.roll(wide[at : at + ROWS], LANES - at, 1)

    sub8, ln8 = iota((8, LANES), 0), iota((8, LANES), 1)
    spread8 = lambda v: jnp.broadcast_to(v, (8, LANES))
    packed = pltpu.roll(corr[24:32], 48, 1)
    for g, first, shift in ((2, 72, 40), (1, 56, 24)):
        packed = jnp.where(ln8 < first, pltpu.roll(corr[8 * g : 8 * g + 8], shift, 1), packed)
    packed = jnp.where(ln8 < 32, corr[0:8], packed)
    behind = jnp.where(
        sub8 < 2,
        spread8(packed[6:7]),
        jnp.where(
            sub8 < 4,
            spread8(packed[7:8]),
            jnp.where(sub8 == 4, spread8(corr[32:33]), spread8(q_row)),
        ),
    )
    second = (sub8 == 1) | (sub8 == 3)
    behind = jnp.where(second, pltpu.roll(behind, 32, 1), pltpu.roll(behind, 80, 1))
    total = jnp.where(ln8 < 80, packed, behind)[0:SUMS]

    def send(buf, me, peers, index, value):
        buf[me] = value
        for device in peers:
            pltpu.make_async_remote_copy(
                src_ref=buf.at[me],
                dst_ref=buf.at[me],
                send_sem=send_sem.at[index],
                recv_sem=recv_sem.at[index],
                device_id=device,
                device_id_type=MESH,
            ).start()

    def receive(buf, count, index):
        rest = buf.at[pl.ds(0, count - 1)]
        pltpu.make_async_copy(rest, rest, recv_sem.at[index]).wait()
        return tree_sum(buf[k] for k in range(count))

    send(buf_x, x * NC + core, x_peers, 1, total)

    for g in range(TILES):
        for q in range(GROUP):
            block = pltpu.roll(parts[g], LANES - STRIDE * q, 1) if q else parts[g]
            red_ref[GROUP * g + q] = block[0:WIDTH, 0:WIDTH]

    total = receive(buf_x, NX * NC, 1)
    send(buf_y, y, y_peers, 2, total)
    total = receive(buf_y, NY, 2)
    send(buf_z, z, z_peers, 3, total)
    total = receive(buf_z, NZ, 3)

    total = jnp.concatenate([total, jnp.zeros((8 - SUMS, LANES), F32)], axis=0)
    by_80, by_32 = pltpu.roll(total, LANES - 80, 1), pltpu.roll(total, LANES - 32, 1)
    row_6 = jnp.where(lane1 < 48, by_80[0:1], by_32[1:2])
    row_7 = jnp.where(lane1 < 48, by_80[2:3], by_32[3:4])
    total = jnp.where(sub8 == 6, spread8(row_6), jnp.where(sub8 == 7, spread8(row_7), total))
    border = by_80[4:5]
    moments = jnp.where(lane1 < WIDTH, by_80[5:6], 0.0) * INV_NF
    mean_sq = moments[:, 2 * PAIRS : 2 * PAIRS + 1]
    r_row, e_row = rows_from(moments)
    data_gram = assemble(
        tables, r_row, e_row, row_to_col(moments, 0), row_to_col(moments, PAIRS)
    )
    half = jnp.concatenate(
        [total]
        + [pltpu.roll(total, LANES - shift, 1) for shift in (24, 40, 48)]
        + [spread8(border)],
        axis=0,
    )
    square = jnp.concatenate([half, jnp.zeros((LANES - ROWS, LANES), F32)], axis=0)
    stored = ((lane < 2 * PAIRS) & (lane >= (row & ~7))) | (row >= 2 * PAIRS)
    correction = jnp.where(stored, half, square.T[0:ROWS])
    system = (data_gram - correction) * (1.0 / mean_sq)
    sys_ref[...] = system[0:WIDTH, 0:WIDTH]
    nrm_ref[...] = (mean * jnp.sqrt(mean_sq * (1.0 / ELEM_TOTAL)))[:, 0:WIDTH]

    copy_a.wait_send()
    for buf, count, index in (
        (sum_a, NZY, 0), (buf_x, NX * NC, 1), (buf_y, NY, 2), (buf_z, NZ, 3), (buf_m, QUAD, 4)
    ):
        rest = buf.at[pl.ds(0, count - 1)]
        pltpu.make_async_copy(rest, rest, send_sem.at[index]).wait()


def writer(red, sys, nrm, red_out, sys_out, nrm_out):
    red_out[...] = red[...]
    sys_out[...] = sys[...]
    nrm_out[...] = nrm[...]


def per_device(pole_freq, pole_damp, samples):
    vmem = lambda *shape: pltpu.VMEM(shape, F32)
    in_hbm = lambda v: pltpu.with_memory_space_constraint(v, pltpu.HBM)
    half = lambda *shape: pltpu.VMEM(shape, jnp.bfloat16)
    results = (
        vmem(OWN, WIDTH, WIDTH),
        vmem(WIDTH, WIDTH),
        vmem(1, WIDTH),
    )
    reduced, system, norm_row = pl.pallas_call(
        kernel,
        out_shape=results,
        in_specs=[pl.BlockSpec(memory_space=pltpu.HBM)] * 3,
        out_specs=(pl.BlockSpec(memory_space=pltpu.VMEM),) * 3,
        scratch_shapes=[
            pltpu.SMEM((PAIRS,), F32),
            pltpu.SMEM((PAIRS,), F32),
            vmem(2, FREQ_LOCAL, ELEM_LOCAL),
            half(2 * BASIS, FREQ_LOCAL),
            half(4 * PAIRS, FREQ_LOCAL),
            vmem(ELEM_LOCAL, LANES),
            vmem(NC, NZY, 8, LANES),
            vmem(NZY, 8, LANES),
            vmem(NZY, 8, LANES),
            vmem(NZY, 8, LANES),
            vmem(QUAD, 1, LANES),
            vmem(NX * NC, SUMS, LANES),
            vmem(NY, SUMS, LANES),
            vmem(NZ, SUMS, LANES),
            pltpu.SemaphoreType.DMA((2,)),
            pltpu.SemaphoreType.DMA((2, CHUNKS)),
            pltpu.SemaphoreType.DMA((6,)),
            pltpu.SemaphoreType.DMA((6,)),
        ],
        compiler_params=pltpu.CompilerParams(
            collective_id=0, has_side_effects=True, vmem_limit_bytes=40 * 1024 * 1024
        ),
    )(*(in_hbm(v) for v in (pole_freq, pole_damp, samples)))
    in_vmem = lambda v: pltpu.with_memory_space_constraint(v, pltpu.VMEM)
    reduced, system, norm_row = pl.pallas_call(
        writer,
        out_shape=(
            jax.ShapeDtypeStruct((OWN, WIDTH, WIDTH), F32),
            jax.ShapeDtypeStruct((WIDTH, WIDTH), F32),
            jax.ShapeDtypeStruct((1, WIDTH), F32),
        ),
        in_specs=[pl.BlockSpec(memory_space=pltpu.VMEM)] * 3,
        out_specs=(pl.BlockSpec(memory_space=pltpu.VMEM),) * 3,
        compiler_params=pltpu.CompilerParams(vmem_limit_bytes=48 * 1024 * 1024),
    )(in_vmem(reduced), in_vmem(system), in_vmem(norm_row))
    return jnp.transpose(reduced, (1, 2, 0)), system, norm_row.reshape(WIDTH)


def solution(mesh):
    placed = (P(), P(), P(None, "freq", "elem"))
    return jax.shard_map(
        per_device,
        mesh=mesh,
        in_specs=placed,
        out_specs=(P(None, None, ("elem", "freq")), P(), P()),
        check_vma=False,
    )
```

```python
import jax
import jax.numpy as jnp
from jax import lax
from jax.experimental import pallas as pl
from jax.experimental.pallas import tpu as pltpu
from jax.sharding import PartitionSpec as P

HIGH = lax.Precision.HIGHEST
MESH = pl.DeviceIdType.MESH
F32 = jnp.float32

NX, NZH, NZL, NY, NC = 4, 4, 2, 8, 2
NZ = NZH * NZL
NZY = NZL * NY
NFREQ = NZY * NC
QUAD = NZL * NC
PAIRS = 16
WIDTH = 2 * PAIRS + 1
ROWS = 40
BASIS = 48
OWN = 12
GROUP = 3
STRIDE = 40
TILES = OWN // GROUP
SUMS = 6
CHUNK = 256
CHUNKS = 4
LANES = 128
FREQ_LOCAL = 1024
ELEM_LOCAL = OWN * NFREQ
FREQ_TOTAL = FREQ_LOCAL * NFREQ
ELEM_TOTAL = ELEM_LOCAL * NX * NZH
INV_NF = 1.0 / FREQ_TOTAL


def iota(shape, dim):
    return lax.broadcasted_iota(jnp.int32, shape, dim)


def omega_of(half_position):
    return 0.02 + 0.98 * half_position / FREQ_TOTAL


def inverse_of(value):
    r = pltpu.reciprocal(value, approx=True)
    r = r * (2.0 - value * r)
    return r * (2.0 - value * r)


def split(value):
    high = value.astype(jnp.bfloat16)
    return high, (value - high.astype(F32)).astype(jnp.bfloat16)


def bf_dot(a, b):
    return jnp.dot(a, b, preferred_element_type=F32)


def wrap(value, size):
    return jnp.where(value >= size, value - size, value)


def tree_sum(values):
    values = list(values)
    while len(values) > 1:
        values = [a + b for a, b in zip(values[::2], values[1::2])] + values[len(values) & ~1 :]
    return values[0]


def pick(ref, index, shape):
    out = jnp.zeros(shape, F32)
    for m in range(PAIRS):
        out = jnp.where(index == m, ref[m], out)
    return out


def over_rows(col):
    return jnp.concatenate([col, col, jnp.zeros((8, LANES), F32)], axis=0)


def pair_coefs(ci, di, cj, dj, row_sum, col_sum):
    both = di + dj
    gap = cj - ci
    tot = ci + cj
    sq = both * both
    r1 = inverse_of(sq + gap * gap)
    r2 = inverse_of(sq + tot * tot)
    alpha, beta = both * r1, gap * r1
    gamma, delta = both * r2, -tot * r2
    ap, am = alpha + gamma, alpha - gamma
    bm, bp = beta - delta, beta + delta

    def table(di, bm, bp, row_sum, col_sum):
        ss, bd, bs, da = di * ap, di * bm, di * bp, di * am
        cr = jnp.where(row_sum, jnp.where(col_sum, ss, -bd), jnp.where(col_sum, bs, da))
        ce = jnp.where(row_sum, jnp.where(col_sum, bd, ss), jnp.where(col_sum, -da, bs))
        return cr, ce

    return table(di, bm, bp, row_sum, col_sum) + table(dj, -bp, -bm, col_sum, row_sum)


def coef_tables(c_col, d_col, pf, pd):
    shape = (ROWS, LANES)
    row, col = iota(shape, 0), iota(shape, 1)
    small = iota((8, LANES), 1) & (PAIRS - 1)
    cj, dj = pick(pf, small, (8, LANES)), pick(pd, small, (8, LANES))
    tall = lambda v: jnp.concatenate([v] * (ROWS // 8), axis=0)
    inside = (row < 2 * PAIRS) & (col < 2 * PAIRS)
    cr, ce, crt, cet = pair_coefs(
        over_rows(c_col), over_rows(d_col), tall(cj), tall(dj), row < PAIRS, col < PAIRS
    )
    last_row = row == 2 * PAIRS
    last_col = col == 2 * PAIRS
    one = lambda cond: jnp.where(cond, 1.0, 0.0).astype(F32)
    cr = jnp.where(inside, cr, one(last_row & ((col < PAIRS) | last_col)))
    ce = jnp.where(inside, ce, one(last_row & (col >= PAIRS) & (col < 2 * PAIRS)))
    crt = jnp.where(inside, crt, one(last_col & (row < PAIRS)))
    cet = jnp.where(inside, cet, one(last_col & (row >= PAIRS) & (row < 2 * PAIRS)))
    return cr, ce, crt, cet


def assemble(tables, r_row, e_row, r_col, e_col):
    cr, ce, crt, cet = tables
    return cr * r_row + ce * e_row + crt * over_rows(r_col) + cet * over_rows(e_col)


def row_to_col(row_vec, first):
    row, lane = iota((PAIRS, LANES), 0), iota((PAIRS, LANES), 1)
    kept = jnp.where(lane == row + first, jnp.broadcast_to(row_vec, (PAIRS, LANES)), 0.0)
    return jnp.broadcast_to(jnp.sum(kept, axis=1, keepdims=True), (PAIRS, LANES))


def rows_from(values):
    lane = iota(values.shape, 1)
    j = lane - jnp.where(lane >= 2 * STRIDE, 2 * STRIDE, jnp.where(lane >= STRIDE, STRIDE, 0))
    r_row = jnp.where(
        j < PAIRS,
        values,
        jnp.where(j < 2 * PAIRS, pltpu.roll(values, PAIRS, 1), jnp.where(j == 2 * PAIRS, values, 0.0)),
    )
    e_row = jnp.where(
        j < PAIRS,
        pltpu.roll(values, LANES - PAIRS, 1),
        jnp.where(j < 2 * PAIRS, values, 0.0),
    )
    return r_row, e_row


def eliminate(work):
    parts = [work[8 * b : 8 * b + 8] for b in range(ROWS // 8)]
    sub = iota((8, LANES), 0)
    for first in range(0, WIDTH, 8):
        count = min(8, WIDTH - first)
        b0 = first // 8
        live = range(b0, len(parts))
        cols = [
            [jnp.broadcast_to(parts[b][:, first + t : first + t + 1], (8, LANES)) for b in live]
            for t in range(count)
        ]
        rows = [parts[b0][t : t + 1, :] for t in range(count)]
        for t in range(count):
            inv = inverse_of(cols[t][0][t : t + 1, :])
            factor = [v * inv for v in cols[t]]
            factor[0] = jnp.where(sub > t, factor[0], 0.0)
            for u in range(t + 1, count):
                lead = cols[u][0][t : t + 1, :]
                cols[u] = [v - f * lead for v, f in zip(cols[u], factor)]
                rows[u] = rows[u] - factor[0][u : u + 1, :] * rows[t]
            for n, b in enumerate(live):
                parts[b] = parts[b] - factor[n] * rows[t]
    return jnp.concatenate(parts, axis=0)


def kernel(
    pf_hbm, pd_hbm, s_hbm, red_ref, sys_ref, nrm_ref,
    pf, pd, s_buf, re_buf, im_buf, xt_buf, pieces, recv_a, sum_a, recv_b,
    buf_m, buf_y, buf_xz, mine, recv_c,
    pole_sem, load_sem, send_sem, recv_sem,
):
    elem, freq = lax.axis_index("elem"), lax.axis_index("freq")
    x, z_hi = elem // NZH, elem % NZH
    zy, core = freq // NC, freq % NC
    z_lo, y = zy // NY, zy % NY
    z = z_hi * NZL + z_lo

    def at_freq(other):
        return {"elem": elem, "freq": other}

    def at_y(other):
        return {"elem": elem, "freq": (z_lo * NY + other) * NC + core}

    def far_first(size):
        return sorted(range(size), key=lambda d: -min(d, size - d))

    sibling = at_freq(zy * NC + (1 - core))
    zy_peers = [
        wrap(z_lo + dz, NZL) * NY + wrap(y + dy, NY)
        for dy in far_first(NY)
        for dz in (1, 0)
        if dy or dz
    ]
    y_peers = [
        at_freq((z_lo * NY + wrap(y + dy, NY)) * NC + wrap(core + c, NC))
        for dy in far_first(NY)
        for c in (1, 0)
        if dy or c
    ]
    freq_across = (wrap(z_lo + core, NZL) * NY + y) * NC + core
    across = {"elem": elem, "freq": freq_across}
    xz_peers = [
        {"elem": wrap(x + dx, NX) * NZH + wrap(z_hi + dz, NZH), "freq": freq_across}
        for dz in far_first(NZH)
        for dx in far_first(NX)
        if dx or dz
    ]
    corner = at_freq((wrap(z_lo + 1, NZL) * NY + y) * NC + (1 - core))

    pole_loads = [
        pltpu.make_async_copy(pf_hbm, pf, pole_sem.at[0]),
        pltpu.make_async_copy(pd_hbm, pd, pole_sem.at[1]),
    ]
    for load in pole_loads:
        load.start()
    loads = {}
    for k in range(CHUNKS):
        for part in range(2):
            at = pl.ds(k * CHUNK, CHUNK)
            loads[part, k] = pltpu.make_async_copy(
                s_hbm.at[part, at], s_buf.at[part, at], load_sem.at[part, k]
            )
            loads[part, k].start()

    barrier = pltpu.get_barrier_semaphore()

    def greet(device):
        pl.semaphore_signal(barrier, inc=1, device_id=device, device_id_type=MESH)

    greets = [at_freq(zy_peer * NC + core) for zy_peer in zy_peers]
    greets += [
        at_freq((z_lo * NY + wrap(y + dy, NY)) * NC + (1 - core)) for dy in far_first(NY)
    ]
    greets += [corner] + xz_peers
    for device in greets:
        greet(device)
    greeted = len(greets)

    for load in pole_loads:
        load.wait()

    column = iota((PAIRS, LANES), 0)
    c_col = pick(pf, column, (PAIRS, LANES))
    d_col = pick(pd, column, (PAIRS, LANES))
    d_sq = d_col * d_col
    half16 = iota((PAIRS, LANES), 1).astype(F32) + 0.5
    base = (freq * FREQ_LOCAL).astype(F32)
    ones = jnp.where(iota((PAIRS, FREQ_LOCAL), 0) == 0, 1.0, 0.0)
    re_buf[2 * PAIRS : BASIS, :] = ones.astype(jnp.bfloat16)
    re_buf[BASIS + 2 * PAIRS :, :] = jnp.zeros((PAIRS, FREQ_LOCAL), jnp.bfloat16)
    for tile in range(FREQ_LOCAL // LANES):
        at = pl.ds(tile * LANES, LANES)
        w = omega_of(half16 + (base + tile * LANES))
        below, above = w - c_col, w + c_col
        i1 = inverse_of(d_sq + below * below)
        i2 = inverse_of(d_sq + above * above)
        first, second = below * i1, above * i2
        re_buf[0:PAIRS, at], re_buf[BASIS : BASIS + PAIRS, at] = split(d_sq * (i1 + i2))
        re_buf[PAIRS : 2 * PAIRS, at], re_buf[BASIS + PAIRS : BASIS + 2 * PAIRS, at] = split(
            d_col * (first - second)
        )
        im_buf[0:PAIRS, at], im_buf[2 * PAIRS : 3 * PAIRS, at] = split(-d_col * (first + second))
        im_buf[PAIRS : 2 * PAIRS, at], im_buf[3 * PAIRS :, at] = split(d_sq * (i1 - i2))

    quad = z_lo * NC + core
    share = NFREQ // QUAD
    halves = [slice(0, 8), slice(8, 16)]

    def mean_step(step, acc):
        acc = list(acc)
        start = ((quad * share + step) * FREQ_LOCAL).astype(F32)
        for tile in range(FREQ_LOCAL // LANES):
            w = omega_of(half16[0:8] + (start + tile * LANES))
            for h in range(2):
                below, above = w - c_col[halves[h]], w + c_col[halves[h]]
                n1 = d_sq[halves[h]] + below * below
                n2 = d_sq[halves[h]] + above * above
                r = inverse_of(n1 * n2)
                acc[2 * h] = acc[2 * h] + r * (n1 + n2)
                acc[2 * h + 1] = acc[2 * h + 1] + r * (below * n2 - above * n1)
        return tuple(acc)

    acc = lax.fori_loop(0, share, mean_step, (jnp.zeros((8, LANES), F32),) * 4)
    lane16 = iota((PAIRS, LANES), 1)
    sum_r = d_sq * jnp.sum(jnp.concatenate([acc[0], acc[2]], axis=0), axis=1, keepdims=True)
    sum_e = d_col * jnp.sum(jnp.concatenate([acc[1], acc[3]], axis=0), axis=1, keepdims=True)
    sums = jnp.where(lane16 == column, sum_r, jnp.where(lane16 == column + PAIRS, sum_e, 0.0))
    buf_m[quad] = jnp.sum(sums, axis=0, keepdims=True)

    x0 = jnp.zeros((BASIS, ELEM_LOCAL + LANES), F32)
    x1 = jnp.zeros((2 * PAIRS, ELEM_LOCAL), F32)
    for k in range(CHUNKS):
        at = pl.ds(k * CHUNK, CHUNK)
        loads[0, k].wait()
        loads[1, k].wait()
        s0, s1 = s_buf[0, at, :], s_buf[1, at, :]
        squares = s0 * s0 + s1 * s1
        power = tree_sum(squares[:, t * LANES : (t + 1) * LANES] for t in range(ELEM_LOCAL // LANES))
        high, low = split(jnp.concatenate([s0, power], axis=1))
        both = bf_dot(re_buf[:, at], high)
        x0 = x0 + (both[0:BASIS] + both[BASIS:] + bf_dot(re_buf[0:BASIS, at], low))
        high, low = split(s1)
        both = bf_dot(im_buf[:, at], high)
        x1 = x1 + (both[0 : 2 * PAIRS] + both[2 * PAIRS :] + bf_dot(im_buf[0 : 2 * PAIRS, at], low))
    x0, q = x0[:, 0:ELEM_LOCAL], x0[0:ROWS, ELEM_LOCAL:]

    stacked = jnp.concatenate(
        [
            x0,
            jnp.zeros((64 - BASIS, ELEM_LOCAL), F32),
            x1,
            jnp.zeros((LANES - 64 - 2 * PAIRS, ELEM_LOCAL), F32),
        ],
        axis=0,
    )
    for tile in range(ELEM_LOCAL // LANES):
        at = slice(tile * LANES, (tile + 1) * LANES)
        xt_buf[at, :] = stacked[:, at].T
    count = ELEM_LOCAL // GROUP
    thirds = [xt_buf[pl.ds(q, count, stride=GROUP), :] for q in range(GROUP)]
    lane_c = iota((count, LANES), 1)

    def spread(shift):
        rolled = [
            pltpu.roll(thirds[q], (STRIDE * q + shift) % LANES, 1) if (STRIDE * q + shift) % LANES else thirds[q]
            for q in range(GROUP)
        ]
        return jnp.where(
            lane_c < STRIDE, rolled[0], jnp.where(lane_c < 2 * STRIDE, rolled[1], rolled[2])
        )

    part0, part1 = spread(0), spread(64)
    upper = iota((8, LANES), 0) < 4
    for k in range(NZY):
        v0, v1 = part0[8 * k : 8 * k + 8], part1[8 * k : 8 * k + 8]
        pieces[0, k] = jnp.where(upper, v0, pltpu.roll(v1, 4, 0))
        pieces[1, k] = jnp.where(upper, pltpu.roll(v0, 4, 0), v1)

    pl.semaphore_wait(barrier, greeted)

    copy_a = pltpu.make_async_remote_copy(
        src_ref=pieces.at[1 - core],
        dst_ref=recv_a,
        send_sem=send_sem.at[5],
        recv_sem=recv_sem.at[5],
        device_id=sibling,
        device_id_type=MESH,
    )
    copy_a.start()
    for step in range(1, QUAD):
        lo, c = wrap(z_lo + step // NC, NZL), wrap(core + step % NC, NC)
        pltpu.make_async_remote_copy(
            src_ref=buf_m.at[quad],
            dst_ref=buf_m.at[quad],
            send_sem=send_sem.at[4],
            recv_sem=recv_sem.at[4],
            device_id=at_freq((lo * NY + y) * NC + c),
            device_id_type=MESH,
        ).start()

    tables = coef_tables(c_col, d_col, pf, pd)
    copy_a.wait_recv()
    for k in range(NZY):
        sum_a[k] = pieces[core, k] + recv_a[k]
    for other in zy_peers:
        pltpu.make_async_remote_copy(
            src_ref=sum_a.at[other],
            dst_ref=recv_b.at[zy],
            send_sem=send_sem.at[0],
            recv_sem=recv_sem.at[0],
            device_id=at_freq(other * NC + core),
            device_id_type=MESH,
        ).start()
    recv_b[zy] = sum_a[zy]

    rest = buf_m.at[pl.ds(0, QUAD - 1)]
    pltpu.make_async_copy(rest, rest, recv_sem.at[4]).wait()
    mean = tree_sum(buf_m[k] for k in range(QUAD)) * INV_NF
    lane1 = iota((1, LANES), 1)
    mean = jnp.where(lane1 == 2 * PAIRS, 1.0, mean)
    r_row, e_row = rows_from(mean)
    gram = assemble(tables, r_row, e_row, row_to_col(mean, 0), row_to_col(mean, PAIRS))
    row, lane = iota((ROWS, LANES), 0), iota((ROWS, LANES), 1)
    work = gram + jnp.where((lane == row + 64) & (row < WIDTH), 1.0, 0.0)
    work = eliminate(work)
    pivots = jnp.sum(jnp.where((lane == row) & (row < WIDTH), work, 0.0), axis=1, keepdims=True)
    pivots = jnp.where(iota((ROWS, 1), 0) < WIDTH, pivots, 1.0)
    inverse = pltpu.roll(work, 64, 1) * (1.0 / jnp.sqrt(pivots))
    inverse = jnp.where(lane < WIDTH, inverse, 0.0)

    q = jnp.broadcast_to(jnp.sum(q, axis=1, keepdims=True), (ROWS, LANES))
    q_row = jnp.sum(jnp.where(lane == row, q, 0.0), axis=0, keepdims=True)

    triple = [
        v + pltpu.roll(v, STRIDE, 1) + pltpu.roll(v, 2 * STRIDE, 1) for v in tables
    ]

    rest_b = recv_b.at[pl.ds(0, NZY - 1)]
    pltpu.make_async_copy(rest_b, rest_b, recv_sem.at[0]).wait()
    owned = tree_sum(recv_b[k] for k in range(NZY))
    owned = owned * (-INV_NF)

    other_part = pltpu.roll(owned, 4, 0)
    plus, minus = owned + other_part, owned - other_part
    r_rows, e_rows = rows_from(minus)
    plus_t = jnp.concatenate([plus, jnp.zeros((LANES - 8, LANES), F32)], axis=0).T
    lane16 = iota((PAIRS, LANES), 1)

    def columns(g, first):
        spread_col = [
            jnp.broadcast_to(
                plus_t[STRIDE * q + first : STRIDE * q + first + PAIRS, g : g + 1], (PAIRS, LANES)
            )
            for q in range(GROUP)
        ]
        return jnp.where(
            lane16 < STRIDE, spread_col[0], jnp.where(lane16 < 2 * STRIDE, spread_col[1], spread_col[2])
        )

    coupling = jnp.concatenate(
        [
            assemble(triple, r_rows[g : g + 1, :], e_rows[g : g + 1, :], columns(g, 0), columns(g, PAIRS))
            for g in range(TILES)
        ],
        axis=1,
    )
    reduced = jnp.dot(
        inverse[:, 0:ROWS], coupling, precision=HIGH, preferred_element_type=F32
    )
    parts = [reduced[:, g * LANES : (g + 1) * LANES] for g in range(TILES)]
    tall = jnp.concatenate(parts, axis=0)
    wide = jnp.dot(tall.T, tall, precision=HIGH, preferred_element_type=F32)
    corr = wide[0:ROWS]
    for q in range(1, GROUP):
        at = STRIDE * q
        corr = corr + pltpu.roll(wide[at : at + ROWS], LANES - at, 1)

    sub8, ln8 = iota((8, LANES), 0), iota((8, LANES), 1)
    spread8 = lambda v: jnp.broadcast_to(v, (8, LANES))
    packed = pltpu.roll(corr[24:32], 48, 1)
    for g, first, shift in ((2, 72, 40), (1, 56, 24)):
        packed = jnp.where(ln8 < first, pltpu.roll(corr[8 * g : 8 * g + 8], shift, 1), packed)
    packed = jnp.where(ln8 < 32, corr[0:8], packed)
    behind = jnp.where(
        sub8 < 2,
        spread8(packed[6:7]),
        jnp.where(
            sub8 < 4,
            spread8(packed[7:8]),
            jnp.where(sub8 == 4, spread8(corr[32:33]), spread8(q_row)),
        ),
    )
    second = (sub8 == 1) | (sub8 == 3)
    behind = jnp.where(second, pltpu.roll(behind, 32, 1), pltpu.roll(behind, 80, 1))
    total = jnp.where(ln8 < 80, packed, behind)[0:SUMS]

    def send(source, target, peers, index):
        for device in peers:
            pltpu.make_async_remote_copy(
                src_ref=source,
                dst_ref=target,
                send_sem=send_sem.at[index],
                recv_sem=recv_sem.at[index],
                device_id=device,
                device_id_type=MESH,
            ).start()

    def arrived(buf, count, index):
        rest = buf.at[pl.ds(0, count - 1)]
        pltpu.make_async_copy(rest, rest, recv_sem.at[index]).wait()

    me = y * NC + core
    buf_y[me] = total
    send(buf_y.at[me], buf_y.at[me], y_peers, 1)

    for g in range(TILES):
        for q in range(GROUP):
            block = pltpu.roll(parts[g], LANES - STRIDE * q, 1) if q else parts[g]
            red_ref[GROUP * g + q] = block[0:WIDTH, 0:WIDTH]

    arrived(buf_y, NY * NC, 1)
    mine[0] = tree_sum(buf_y[k] for k in range(NY * NC))
    send(mine.at[0], buf_xz.at[elem], xz_peers, 2)
    copy_across = pltpu.make_async_remote_copy(
        src_ref=mine.at[0],
        dst_ref=buf_xz.at[elem],
        send_sem=send_sem.at[3],
        recv_sem=recv_sem.at[3],
        device_id=across,
        device_id_type=MESH,
    )

    @pl.when(core == 1)
    def _():
        copy_across.start()

    @pl.when(core == 0)
    def _():
        buf_xz[elem] = mine[0]

    arrived(buf_xz, NX * NZH, 2)

    @pl.when(core == 1)
    def _():
        copy_across.wait_recv()

    part = tree_sum(buf_xz[k] for k in range(NX * NZH))
    mine[1] = part
    copy_c = pltpu.make_async_remote_copy(
        src_ref=mine.at[1],
        dst_ref=recv_c.at[0],
        send_sem=send_sem.at[6],
        recv_sem=recv_sem.at[6],
        device_id=sibling,
        device_id_type=MESH,
    )
    copy_c.start()
    copy_c.wait_recv()
    total = part + recv_c[0]

    total = jnp.concatenate([total, jnp.zeros((8 - SUMS, LANES), F32)], axis=0)
    by_80, by_32 = pltpu.roll(total, LANES - 80, 1), pltpu.roll(total, LANES - 32, 1)
    row_6 = jnp.where(lane1 < 48, by_80[0:1], by_32[1:2])
    row_7 = jnp.where(lane1 < 48, by_80[2:3], by_32[3:4])
    total = jnp.where(sub8 == 6, spread8(row_6), jnp.where(sub8 == 7, spread8(row_7), total))
    border = by_80[4:5]
    moments = jnp.where(lane1 < WIDTH, by_80[5:6], 0.0) * INV_NF
    mean_sq = moments[:, 2 * PAIRS : 2 * PAIRS + 1]
    r_row, e_row = rows_from(moments)
    data_gram = assemble(
        tables, r_row, e_row, row_to_col(moments, 0), row_to_col(moments, PAIRS)
    )
    half = jnp.concatenate(
        [total]
        + [pltpu.roll(total, LANES - shift, 1) for shift in (24, 40, 48)]
        + [spread8(border)],
        axis=0,
    )
    square = jnp.concatenate([half, jnp.zeros((LANES - ROWS, LANES), F32)], axis=0)
    stored = ((lane < 2 * PAIRS) & (lane >= (row & ~7))) | (row >= 2 * PAIRS)
    correction = jnp.where(stored, half, square.T[0:ROWS])
    system = (data_gram - correction) * (1.0 / mean_sq)
    sys_ref[...] = system[0:WIDTH, 0:WIDTH]
    nrm_ref[...] = (mean * jnp.sqrt(mean_sq * (1.0 / ELEM_TOTAL)))[:, 0:WIDTH]

    copy_a.wait_send()
    copy_c.wait_send()

    @pl.when(core == 1)
    def _():
        copy_across.wait_send()

    for buf, count, index in (
        (sum_a, NZY, 0), (buf_y, NY * NC, 1), (buf_xz, NX * NZH, 2), (buf_m, QUAD, 4)
    ):
        rest = buf.at[pl.ds(0, count - 1)]
        pltpu.make_async_copy(rest, rest, send_sem.at[index]).wait()


def writer(red, sys, nrm, red_out, sys_out, nrm_out):
    red_out[...] = red[...]
    sys_out[...] = sys[...]
    nrm_out[...] = nrm[...]


def per_device(pole_freq, pole_damp, samples):
    vmem = lambda *shape: pltpu.VMEM(shape, F32)
    in_hbm = lambda v: pltpu.with_memory_space_constraint(v, pltpu.HBM)
    half = lambda *shape: pltpu.VMEM(shape, jnp.bfloat16)
    results = (
        vmem(OWN, WIDTH, WIDTH),
        vmem(WIDTH, WIDTH),
        vmem(1, WIDTH),
    )
    reduced, system, norm_row = pl.pallas_call(
        kernel,
        out_shape=results,
        in_specs=[pl.BlockSpec(memory_space=pltpu.HBM)] * 3,
        out_specs=(pl.BlockSpec(memory_space=pltpu.VMEM),) * 3,
        scratch_shapes=[
            pltpu.SMEM((PAIRS,), F32),
            pltpu.SMEM((PAIRS,), F32),
            vmem(2, FREQ_LOCAL, ELEM_LOCAL),
            half(2 * BASIS, FREQ_LOCAL),
            half(4 * PAIRS, FREQ_LOCAL),
            vmem(ELEM_LOCAL, LANES),
            vmem(NC, NZY, 8, LANES),
            vmem(NZY, 8, LANES),
            vmem(NZY, 8, LANES),
            vmem(NZY, 8, LANES),
            vmem(QUAD, 1, LANES),
            vmem(NY * NC, SUMS, LANES),
            vmem(NX * NZH, SUMS, LANES),
            vmem(2, SUMS, LANES),
            vmem(1, SUMS, LANES),
            pltpu.SemaphoreType.DMA((2,)),
            pltpu.SemaphoreType.DMA((2, CHUNKS)),
            pltpu.SemaphoreType.DMA((7,)),
            pltpu.SemaphoreType.DMA((7,)),
        ],
        compiler_params=pltpu.CompilerParams(
            collective_id=0, has_side_effects=True, vmem_limit_bytes=40 * 1024 * 1024
        ),
    )(*(in_hbm(v) for v in (pole_freq, pole_damp, samples)))
    in_vmem = lambda v: pltpu.with_memory_space_constraint(v, pltpu.VMEM)
    reduced, system, norm_row = pl.pallas_call(
        writer,
        out_shape=(
            jax.ShapeDtypeStruct((OWN, WIDTH, WIDTH), F32),
            jax.ShapeDtypeStruct((WIDTH, WIDTH), F32),
            jax.ShapeDtypeStruct((1, WIDTH), F32),
        ),
        in_specs=[pl.BlockSpec(memory_space=pltpu.VMEM)] * 3,
        out_specs=(pl.BlockSpec(memory_space=pltpu.VMEM),) * 3,
        compiler_params=pltpu.CompilerParams(vmem_limit_bytes=48 * 1024 * 1024),
    )(in_vmem(reduced), in_vmem(system), in_vmem(norm_row))
    return jnp.transpose(reduced, (1, 2, 0)), system, norm_row.reshape(WIDTH)


def solution(mesh):
    placed = (P(), P(), P(None, "freq", "elem"))
    return jax.shard_map(
        per_device,
        mesh=mesh,
        in_specs=placed,
        out_specs=(P(None, None, ("elem", "freq")), P(), P()),
        check_vma=False,
    )
```

```python
import jax
import jax.numpy as jnp
from jax import lax
from jax.experimental import pallas as pl
from jax.experimental.pallas import tpu as pltpu
from jax.sharding import PartitionSpec as P

HIGH = lax.Precision.HIGHEST
MESH = pl.DeviceIdType.MESH
F32 = jnp.float32

NX, NZH, NZL, NY, NC = 4, 4, 2, 8, 2
NZ = NZH * NZL
NZY = NZL * NY
NFREQ = NZY * NC
QUAD = NZL * 2
PAIRS = 16
WIDTH = 2 * PAIRS + 1
ROWS = 40
BASIS = 48
OWN = 12
GROUP = 3
STRIDE = 40
TILES = OWN // GROUP
SUMS = 6
CHUNK = 256
CHUNKS = 4
LANES = 128
FREQ_LOCAL = 1024
ELEM_LOCAL = OWN * NFREQ
FREQ_TOTAL = FREQ_LOCAL * NFREQ
ELEM_TOTAL = ELEM_LOCAL * NX * NZH
INV_NF = 1.0 / FREQ_TOTAL


def iota(shape, dim):
    return lax.broadcasted_iota(jnp.int32, shape, dim)


def omega_of(half_position):
    return 0.02 + 0.98 * half_position / FREQ_TOTAL


def inverse_of(value):
    r = pltpu.reciprocal(value, approx=True)
    r = r * (2.0 - value * r)
    return r * (2.0 - value * r)


def split(value):
    high = value.astype(jnp.bfloat16)
    return high, (value - high.astype(F32)).astype(jnp.bfloat16)


def bf_dot(a, b):
    return jnp.dot(a, b, preferred_element_type=F32)


def wrap(value, size):
    return jnp.where(value >= size, value - size, value)


def tree_sum(values):
    values = list(values)
    while len(values) > 1:
        values = [a + b for a, b in zip(values[::2], values[1::2])] + values[len(values) & ~1 :]
    return values[0]


def pick(ref, index, shape):
    out = jnp.zeros(shape, F32)
    for m in range(PAIRS):
        out = jnp.where(index == m, ref[m], out)
    return out


def over_rows(col):
    return jnp.concatenate([col, col, jnp.zeros((8, LANES), F32)], axis=0)


def pair_coefs(ci, di, cj, dj, row_sum, col_sum):
    both = di + dj
    gap = cj - ci
    tot = ci + cj
    sq = both * both
    r1 = inverse_of(sq + gap * gap)
    r2 = inverse_of(sq + tot * tot)
    alpha, beta = both * r1, gap * r1
    gamma, delta = both * r2, -tot * r2
    ap, am = alpha + gamma, alpha - gamma
    bm, bp = beta - delta, beta + delta

    def table(di, bm, bp, row_sum, col_sum):
        ss, bd, bs, da = di * ap, di * bm, di * bp, di * am
        cr = jnp.where(row_sum, jnp.where(col_sum, ss, -bd), jnp.where(col_sum, bs, da))
        ce = jnp.where(row_sum, jnp.where(col_sum, bd, ss), jnp.where(col_sum, -da, bs))
        return cr, ce

    return table(di, bm, bp, row_sum, col_sum) + table(dj, -bp, -bm, col_sum, row_sum)


def coef_tables(c_col, d_col, pf, pd):
    shape = (ROWS, LANES)
    row, col = iota(shape, 0), iota(shape, 1)
    small = iota((8, LANES), 1) & (PAIRS - 1)
    cj, dj = pick(pf, small, (8, LANES)), pick(pd, small, (8, LANES))
    tall = lambda v: jnp.concatenate([v] * (ROWS // 8), axis=0)
    inside = (row < 2 * PAIRS) & (col < 2 * PAIRS)
    cr, ce, crt, cet = pair_coefs(
        over_rows(c_col), over_rows(d_col), tall(cj), tall(dj), row < PAIRS, col < PAIRS
    )
    last_row = row == 2 * PAIRS
    last_col = col == 2 * PAIRS
    one = lambda cond: jnp.where(cond, 1.0, 0.0).astype(F32)
    cr = jnp.where(inside, cr, one(last_row & ((col < PAIRS) | last_col)))
    ce = jnp.where(inside, ce, one(last_row & (col >= PAIRS) & (col < 2 * PAIRS)))
    crt = jnp.where(inside, crt, one(last_col & (row < PAIRS)))
    cet = jnp.where(inside, cet, one(last_col & (row >= PAIRS) & (row < 2 * PAIRS)))
    return cr, ce, crt, cet


def assemble(tables, r_row, e_row, r_col, e_col):
    cr, ce, crt, cet = tables
    return cr * r_row + ce * e_row + crt * over_rows(r_col) + cet * over_rows(e_col)


def row_to_col(row_vec, first):
    row, lane = iota((PAIRS, LANES), 0), iota((PAIRS, LANES), 1)
    kept = jnp.where(lane == row + first, jnp.broadcast_to(row_vec, (PAIRS, LANES)), 0.0)
    return jnp.broadcast_to(jnp.sum(kept, axis=1, keepdims=True), (PAIRS, LANES))


def rows_from(values):
    lane = iota(values.shape, 1)
    j = lane - jnp.where(lane >= 2 * STRIDE, 2 * STRIDE, jnp.where(lane >= STRIDE, STRIDE, 0))
    r_row = jnp.where(
        j < PAIRS,
        values,
        jnp.where(j < 2 * PAIRS, pltpu.roll(values, PAIRS, 1), jnp.where(j == 2 * PAIRS, values, 0.0)),
    )
    e_row = jnp.where(
        j < PAIRS,
        pltpu.roll(values, LANES - PAIRS, 1),
        jnp.where(j < 2 * PAIRS, values, 0.0),
    )
    return r_row, e_row


def eliminate(work):
    parts = [work[8 * b : 8 * b + 8] for b in range(ROWS // 8)]
    sub = iota((8, LANES), 0)
    for first in range(0, WIDTH, 8):
        count = min(8, WIDTH - first)
        b0 = first // 8
        live = range(b0, len(parts))
        cols = [
            [jnp.broadcast_to(parts[b][:, first + t : first + t + 1], (8, LANES)) for b in live]
            for t in range(count)
        ]
        rows = [parts[b0][t : t + 1, :] for t in range(count)]
        for t in range(count):
            inv = inverse_of(cols[t][0][t : t + 1, :])
            factor = [v * inv for v in cols[t]]
            factor[0] = jnp.where(sub > t, factor[0], 0.0)
            for u in range(t + 1, count):
                lead = cols[u][0][t : t + 1, :]
                cols[u] = [v - f * lead for v, f in zip(cols[u], factor)]
                rows[u] = rows[u] - factor[0][u : u + 1, :] * rows[t]
            for n, b in enumerate(live):
                parts[b] = parts[b] - factor[n] * rows[t]
    return jnp.concatenate(parts, axis=0)


def kernel(
    pf_hbm, pd_hbm, s_hbm, red_ref, sys_ref, nrm_ref,
    pf, pd, s_buf, re_buf, im_buf, xt_buf, pieces, recv_a, sum_a, recv_b,
    buf_m, buf_x, buf_y, buf_z,
    pole_sem, load_sem, send_sem, recv_sem,
):
    elem, freq = lax.axis_index("elem"), lax.axis_index("freq")
    x, z_hi = elem // NZH, elem % NZH
    zy, core = freq // NC, freq % NC
    z_lo, y = zy // NY, zy % NY
    z = z_hi * NZL + z_lo

    def at_freq(other):
        return {"elem": elem, "freq": other}

    def at_y(other):
        return {"elem": elem, "freq": (z_lo * NY + other) * NC + core}

    def far_first(size):
        return sorted(range(size), key=lambda d: -min(d, size - d))

    sibling = at_freq(zy * NC + (1 - core))
    zy_peers = [
        wrap(z_lo + dz, NZL) * NY + wrap(y + dy, NY)
        for dy in far_first(NY)
        for dz in (1, 0)
        if dy or dz
    ]
    y_peers = [at_y(wrap(y + dy, NY)) for dy in far_first(NY) if dy]
    z_peers = []
    for dz in far_first(NZ):
        if dz:
            to = wrap(z + dz, NZ)
            hi = to // NZL
            z_peers.append({"elem": x * NZH + hi, "freq": ((to - hi * NZL) * NY + y) * NC + core})
    x_peers = []
    for dx in far_first(NX):
        for c in (1, 0):
            if dx or c:
                to = wrap(x + dx, NX)
                x_peers.append({"elem": to * NZH + z_hi, "freq": zy * NC + wrap(core + c, NC)})

    pole_loads = [
        pltpu.make_async_copy(pf_hbm, pf, pole_sem.at[0]),
        pltpu.make_async_copy(pd_hbm, pd, pole_sem.at[1]),
    ]
    for load in pole_loads:
        load.start()
    loads = []
    for k in range(CHUNKS):
        at = pl.ds(k * CHUNK, CHUNK)
        load = pltpu.make_async_copy(s_hbm.at[:, at], s_buf.at[:, at], load_sem.at[k])
        load.start()
        loads.append(load)

    barrier = pltpu.get_barrier_semaphore()

    def greet(device):
        pl.semaphore_signal(barrier, inc=1, device_id=device, device_id_type=MESH)

    z_rest = []
    for hi_step in range(1, NZH):
        hi = wrap(z_hi + hi_step, NZH)
        z_rest += [{"elem": x * NZH + hi, "freq": (lo * NY + y) * NC + core} for lo in range(NZL)]
    greets = [at_freq(zy_peer * NC + core) for zy_peer in zy_peers]
    greets += z_rest + x_peers
    for device in greets:
        greet(device)
    greeted = len(greets)

    for load in pole_loads:
        load.wait()

    column = iota((PAIRS, LANES), 0)
    c_col = pick(pf, column, (PAIRS, LANES))
    d_col = pick(pd, column, (PAIRS, LANES))
    d_sq = d_col * d_col
    half16 = iota((PAIRS, LANES), 1).astype(F32) + 0.5
    base = (freq * FREQ_LOCAL).astype(F32)
    ones = jnp.where(iota((PAIRS, FREQ_LOCAL), 0) == 0, 1.0, 0.0)
    re_buf[2 * PAIRS : BASIS, :] = ones.astype(jnp.bfloat16)
    re_buf[BASIS + 2 * PAIRS :, :] = jnp.zeros((PAIRS, FREQ_LOCAL), jnp.bfloat16)
    for tile in range(FREQ_LOCAL // LANES):
        at = pl.ds(tile * LANES, LANES)
        w = omega_of(half16 + (base + tile * LANES))
        below, above = w - c_col, w + c_col
        i1 = inverse_of(d_sq + below * below)
        i2 = inverse_of(d_sq + above * above)
        first, second = below * i1, above * i2
        re_buf[0:PAIRS, at], re_buf[BASIS : BASIS + PAIRS, at] = split(d_sq * (i1 + i2))
        re_buf[PAIRS : 2 * PAIRS, at], re_buf[BASIS + PAIRS : BASIS + 2 * PAIRS, at] = split(
            d_col * (first - second)
        )
        im_buf[0:PAIRS, at], im_buf[2 * PAIRS : 3 * PAIRS, at] = split(-d_col * (first + second))
        im_buf[PAIRS : 2 * PAIRS, at], im_buf[3 * PAIRS :, at] = split(d_sq * (i1 - i2))

    odd = y % 2
    quad = z_lo * 2 + odd
    share = NFREQ // QUAD
    halves = [slice(0, 8), slice(8, 16)]

    def mean_step(step, acc):
        acc = list(acc)
        start = ((quad * share + step) * FREQ_LOCAL).astype(F32)
        for tile in range(FREQ_LOCAL // LANES):
            w = omega_of(half16[0:8] + (start + tile * LANES))
            for h in range(2):
                below, above = w - c_col[halves[h]], w + c_col[halves[h]]
                n1 = d_sq[halves[h]] + below * below
                n2 = d_sq[halves[h]] + above * above
                r = inverse_of(n1 * n2)
                acc[2 * h] = acc[2 * h] + r * (n1 + n2)
                acc[2 * h + 1] = acc[2 * h + 1] + r * (below * n2 - above * n1)
        return tuple(acc)

    acc = lax.fori_loop(0, share, mean_step, (jnp.zeros((8, LANES), F32),) * 4)
    lane16 = iota((PAIRS, LANES), 1)
    sum_r = d_sq * jnp.sum(jnp.concatenate([acc[0], acc[2]], axis=0), axis=1, keepdims=True)
    sum_e = d_col * jnp.sum(jnp.concatenate([acc[1], acc[3]], axis=0), axis=1, keepdims=True)
    sums = jnp.where(lane16 == column, sum_r, jnp.where(lane16 == column + PAIRS, sum_e, 0.0))
    buf_m[quad] = jnp.sum(sums, axis=0, keepdims=True)

    x0 = jnp.zeros((BASIS, ELEM_LOCAL + LANES), F32)
    x1 = jnp.zeros((2 * PAIRS, ELEM_LOCAL), F32)
    for k in range(CHUNKS):
        at = pl.ds(k * CHUNK, CHUNK)
        loads[k].wait()
        s0, s1 = s_buf[0, at, :], s_buf[1, at, :]
        squares = s0 * s0 + s1 * s1
        power = tree_sum(squares[:, t * LANES : (t + 1) * LANES] for t in range(ELEM_LOCAL // LANES))
        high, low = split(jnp.concatenate([s0, power], axis=1))
        both = bf_dot(re_buf[:, at], high)
        x0 = x0 + (both[0:BASIS] + both[BASIS:] + bf_dot(re_buf[0:BASIS, at], low))
        high, low = split(s1)
        both = bf_dot(im_buf[:, at], high)
        x1 = x1 + (both[0 : 2 * PAIRS] + both[2 * PAIRS :] + bf_dot(im_buf[0 : 2 * PAIRS, at], low))
    x0, q = x0[:, 0:ELEM_LOCAL], x0[0:ROWS, ELEM_LOCAL:]

    stacked = jnp.concatenate(
        [
            x0,
            jnp.zeros((64 - BASIS, ELEM_LOCAL), F32),
            x1,
            jnp.zeros((LANES - 64 - 2 * PAIRS, ELEM_LOCAL), F32),
        ],
        axis=0,
    )
    for tile in range(ELEM_LOCAL // LANES):
        at = slice(tile * LANES, (tile + 1) * LANES)
        xt_buf[at, :] = stacked[:, at].T
    count = ELEM_LOCAL // GROUP
    thirds = [xt_buf[pl.ds(q, count, stride=GROUP), :] for q in range(GROUP)]
    lane_c = iota((count, LANES), 1)

    def spread(shift):
        rolled = [
            pltpu.roll(thirds[q], (STRIDE * q + shift) % LANES, 1) if (STRIDE * q + shift) % LANES else thirds[q]
            for q in range(GROUP)
        ]
        return jnp.where(
            lane_c < STRIDE, rolled[0], jnp.where(lane_c < 2 * STRIDE, rolled[1], rolled[2])
        )

    part0, part1 = spread(0), spread(64)
    upper = iota((8, LANES), 0) < 4
    for k in range(NZY):
        v0, v1 = part0[8 * k : 8 * k + 8], part1[8 * k : 8 * k + 8]
        pieces[0, k] = jnp.where(upper, v0, pltpu.roll(v1, 4, 0))
        pieces[1, k] = jnp.where(upper, pltpu.roll(v0, 4, 0), v1)

    pl.semaphore_wait(barrier, greeted)

    copy_a = pltpu.make_async_remote_copy(
        src_ref=pieces.at[1 - core],
        dst_ref=recv_a,
        send_sem=send_sem.at[5],
        recv_sem=recv_sem.at[5],
        device_id=sibling,
        device_id_type=MESH,
    )
    copy_a.start()
    for step in range(1, QUAD):
        lo, to = wrap(z_lo + step // 2, NZL), y - odd + wrap(odd + step % 2, 2)
        pltpu.make_async_remote_copy(
            src_ref=buf_m.at[quad],
            dst_ref=buf_m.at[quad],
            send_sem=send_sem.at[4],
            recv_sem=recv_sem.at[4],
            device_id=at_freq((lo * NY + to) * NC + core),
            device_id_type=MESH,
        ).start()

    tables = coef_tables(c_col, d_col, pf, pd)
    copy_a.wait_recv()
    for k in range(NZY):
        sum_a[k] = pieces[core, k] + recv_a[k]
    for other in zy_peers:
        pltpu.make_async_remote_copy(
            src_ref=sum_a.at[other],
            dst_ref=recv_b.at[zy],
            send_sem=send_sem.at[0],
            recv_sem=recv_sem.at[0],
            device_id=at_freq(other * NC + core),
            device_id_type=MESH,
        ).start()
    recv_b[zy] = sum_a[zy]

    rest = buf_m.at[pl.ds(0, QUAD - 1)]
    pltpu.make_async_copy(rest, rest, recv_sem.at[4]).wait()
    mean = tree_sum(buf_m[k] for k in range(QUAD)) * INV_NF
    lane1 = iota((1, LANES), 1)
    mean = jnp.where(lane1 == 2 * PAIRS, 1.0, mean)
    r_row, e_row = rows_from(mean)
    gram = assemble(tables, r_row, e_row, row_to_col(mean, 0), row_to_col(mean, PAIRS))
    row, lane = iota((ROWS, LANES), 0), iota((ROWS, LANES), 1)
    work = gram + jnp.where((lane == row + 64) & (row < WIDTH), 1.0, 0.0)
    work = eliminate(work)
    pivots = jnp.sum(jnp.where((lane == row) & (row < WIDTH), work, 0.0), axis=1, keepdims=True)
    pivots = jnp.where(iota((ROWS, 1), 0) < WIDTH, pivots, 1.0)
    inverse = pltpu.roll(work, 64, 1) * (1.0 / jnp.sqrt(pivots))
    inverse = jnp.where(lane < WIDTH, inverse, 0.0)

    q = jnp.broadcast_to(jnp.sum(q, axis=1, keepdims=True), (ROWS, LANES))
    q_row = jnp.sum(jnp.where(lane == row, q, 0.0), axis=0, keepdims=True)

    triple = [
        v + pltpu.roll(v, STRIDE, 1) + pltpu.roll(v, 2 * STRIDE, 1) for v in tables
    ]

    rest_b = recv_b.at[pl.ds(0, NZY - 1)]
    pltpu.make_async_copy(rest_b, rest_b, recv_sem.at[0]).wait()
    owned = tree_sum(recv_b[k] for k in range(NZY))
    owned = owned * (-INV_NF)

    other_part = pltpu.roll(owned, 4, 0)
    plus, minus = owned + other_part, owned - other_part
    r_rows, e_rows = rows_from(minus)
    plus_t = jnp.concatenate([plus, jnp.zeros((LANES - 8, LANES), F32)], axis=0).T
    lane16 = iota((PAIRS, LANES), 1)

    def columns(g, first):
        spread_col = [
            jnp.broadcast_to(
                plus_t[STRIDE * q + first : STRIDE * q + first + PAIRS, g : g + 1], (PAIRS, LANES)
            )
            for q in range(GROUP)
        ]
        return jnp.where(
            lane16 < STRIDE, spread_col[0], jnp.where(lane16 < 2 * STRIDE, spread_col[1], spread_col[2])
        )

    coupling = jnp.concatenate(
        [
            assemble(triple, r_rows[g : g + 1, :], e_rows[g : g + 1, :], columns(g, 0), columns(g, PAIRS))
            for g in range(TILES)
        ],
        axis=1,
    )
    reduced = jnp.dot(
        inverse[:, 0:ROWS], coupling, precision=HIGH, preferred_element_type=F32
    )
    parts = [reduced[:, g * LANES : (g + 1) * LANES] for g in range(TILES)]
    tall = jnp.concatenate(parts, axis=0)
    wide = jnp.dot(tall.T, tall, precision=HIGH, preferred_element_type=F32)
    corr = wide[0:ROWS]
    for q in range(1, GROUP):
        at = STRIDE * q
        corr = corr + pltpu.roll(wide[at : at + ROWS], LANES - at, 1)

    sub8, ln8 = iota((8, LANES), 0), iota((8, LANES), 1)
    spread8 = lambda v: jnp.broadcast_to(v, (8, LANES))
    packed = pltpu.roll(corr[24:32], 48, 1)
    for g, first, shift in ((2, 72, 40), (1, 56, 24)):
        packed = jnp.where(ln8 < first, pltpu.roll(corr[8 * g : 8 * g + 8], shift, 1), packed)
    packed = jnp.where(ln8 < 32, corr[0:8], packed)
    behind = jnp.where(
        sub8 < 2,
        spread8(packed[6:7]),
        jnp.where(
            sub8 < 4,
            spread8(packed[7:8]),
            jnp.where(sub8 == 4, spread8(corr[32:33]), spread8(q_row)),
        ),
    )
    second = (sub8 == 1) | (sub8 == 3)
    behind = jnp.where(second, pltpu.roll(behind, 32, 1), pltpu.roll(behind, 80, 1))
    total = jnp.where(ln8 < 80, packed, behind)[0:SUMS]

    def send(buf, me, peers, index, value):
        buf[me] = value
        for device in peers:
            pltpu.make_async_remote_copy(
                src_ref=buf.at[me],
                dst_ref=buf.at[me],
                send_sem=send_sem.at[index],
                recv_sem=recv_sem.at[index],
                device_id=device,
                device_id_type=MESH,
            ).start()

    def receive(buf, count, index):
        rest = buf.at[pl.ds(0, count - 1)]
        pltpu.make_async_copy(rest, rest, recv_sem.at[index]).wait()
        return tree_sum(buf[k] for k in range(count))

    send(buf_x, x * NC + core, x_peers, 1, total)

    for g in range(TILES):
        for q in range(GROUP):
            block = pltpu.roll(parts[g], LANES - STRIDE * q, 1) if q else parts[g]
            red_ref[GROUP * g + q] = block[0:WIDTH, 0:WIDTH]

    total = receive(buf_x, NX * NC, 1)
    send(buf_y, y, y_peers, 2, total)
    total = receive(buf_y, NY, 2)
    send(buf_z, z, z_peers, 3, total)
    total = receive(buf_z, NZ, 3)

    total = jnp.concatenate([total, jnp.zeros((8 - SUMS, LANES), F32)], axis=0)
    by_80, by_32 = pltpu.roll(total, LANES - 80, 1), pltpu.roll(total, LANES - 32, 1)
    row_6 = jnp.where(lane1 < 48, by_80[0:1], by_32[1:2])
    row_7 = jnp.where(lane1 < 48, by_80[2:3], by_32[3:4])
    total = jnp.where(sub8 == 6, spread8(row_6), jnp.where(sub8 == 7, spread8(row_7), total))
    border = by_80[4:5]
    moments = jnp.where(lane1 < WIDTH, by_80[5:6], 0.0) * INV_NF
    mean_sq = moments[:, 2 * PAIRS : 2 * PAIRS + 1]
    r_row, e_row = rows_from(moments)
    data_gram = assemble(
        tables, r_row, e_row, row_to_col(moments, 0), row_to_col(moments, PAIRS)
    )
    half = jnp.concatenate(
        [total]
        + [pltpu.roll(total, LANES - shift, 1) for shift in (24, 40, 48)]
        + [spread8(border)],
        axis=0,
    )
    square = jnp.concatenate([half, jnp.zeros((LANES - ROWS, LANES), F32)], axis=0)
    stored = ((lane < 2 * PAIRS) & (lane >= (row & ~7))) | (row >= 2 * PAIRS)
    correction = jnp.where(stored, half, square.T[0:ROWS])
    system = (data_gram - correction) * (1.0 / mean_sq)
    sys_ref[...] = system[0:WIDTH, 0:WIDTH]
    nrm_ref[...] = (mean * jnp.sqrt(mean_sq * (1.0 / ELEM_TOTAL)))[:, 0:WIDTH]

    copy_a.wait_send()
    for buf, count, index in (
        (sum_a, NZY, 0), (buf_x, NX * NC, 1), (buf_y, NY, 2), (buf_z, NZ, 3), (buf_m, QUAD, 4)
    ):
        rest = buf.at[pl.ds(0, count - 1)]
        pltpu.make_async_copy(rest, rest, send_sem.at[index]).wait()


def writer(red, sys, nrm, red_out, sys_out, nrm_out):
    red_out[...] = red[...]
    sys_out[...] = sys[...]
    nrm_out[...] = nrm[...]


def per_device(pole_freq, pole_damp, samples):
    vmem = lambda *shape: pltpu.VMEM(shape, F32)
    in_hbm = lambda v: pltpu.with_memory_space_constraint(v, pltpu.HBM)
    half = lambda *shape: pltpu.VMEM(shape, jnp.bfloat16)
    results = (
        vmem(OWN, WIDTH, WIDTH),
        vmem(WIDTH, WIDTH),
        vmem(1, WIDTH),
    )
    reduced, system, norm_row = pl.pallas_call(
        kernel,
        out_shape=results,
        in_specs=[pl.BlockSpec(memory_space=pltpu.HBM)] * 3,
        out_specs=(pl.BlockSpec(memory_space=pltpu.VMEM),) * 3,
        scratch_shapes=[
            pltpu.SMEM((PAIRS,), F32),
            pltpu.SMEM((PAIRS,), F32),
            vmem(2, FREQ_LOCAL, ELEM_LOCAL),
            half(2 * BASIS, FREQ_LOCAL),
            half(4 * PAIRS, FREQ_LOCAL),
            vmem(ELEM_LOCAL, LANES),
            vmem(NC, NZY, 8, LANES),
            vmem(NZY, 8, LANES),
            vmem(NZY, 8, LANES),
            vmem(NZY, 8, LANES),
            vmem(QUAD, 1, LANES),
            vmem(NX * NC, SUMS, LANES),
            vmem(NY, SUMS, LANES),
            vmem(NZ, SUMS, LANES),
            pltpu.SemaphoreType.DMA((2,)),
            pltpu.SemaphoreType.DMA((CHUNKS,)),
            pltpu.SemaphoreType.DMA((6,)),
            pltpu.SemaphoreType.DMA((6,)),
        ],
        compiler_params=pltpu.CompilerParams(
            collective_id=0, has_side_effects=True, vmem_limit_bytes=40 * 1024 * 1024
        ),
    )(*(in_hbm(v) for v in (pole_freq, pole_damp, samples)))
    in_vmem = lambda v: pltpu.with_memory_space_constraint(v, pltpu.VMEM)
    reduced, system, norm_row = pl.pallas_call(
        writer,
        out_shape=(
            jax.ShapeDtypeStruct((OWN, WIDTH, WIDTH), F32),
            jax.ShapeDtypeStruct((WIDTH, WIDTH), F32),
            jax.ShapeDtypeStruct((1, WIDTH), F32),
        ),
        in_specs=[pl.BlockSpec(memory_space=pltpu.VMEM)] * 3,
        out_specs=(pl.BlockSpec(memory_space=pltpu.VMEM),) * 3,
        compiler_params=pltpu.CompilerParams(vmem_limit_bytes=48 * 1024 * 1024),
    )(in_vmem(reduced), in_vmem(system), in_vmem(norm_row))
    return jnp.transpose(reduced, (1, 2, 0)), system, norm_row.reshape(WIDTH)


def solution(mesh):
    placed = (P(), P(), P(None, "freq", "elem"))
    return jax.shard_map(
        per_device,
        mesh=mesh,
        in_specs=placed,
        out_specs=(P(None, None, ("elem", "freq")), P(), P()),
        check_vma=False,
    )
```

```python
import jax
import jax.numpy as jnp
from jax import lax
from jax.experimental import pallas as pl
from jax.experimental.pallas import tpu as pltpu
from jax.sharding import PartitionSpec as P

HIGH = lax.Precision.HIGHEST
MESH = pl.DeviceIdType.MESH
F32 = jnp.float32

NX, NZH, NZL, NY, NC = 4, 4, 2, 8, 2
NZ = NZH * NZL
NZY = NZL * NY
NFREQ = NZY * NC
QUAD = NZL * 2
PAIRS = 16
WIDTH = 2 * PAIRS + 1
ROWS = 40
BASIS = 48
OWN = 12
GROUP = 3
STRIDE = 40
TILES = OWN // GROUP
SUMS = 6
CHUNK = 256
CHUNKS = 4
LANES = 128
FREQ_LOCAL = 1024
ELEM_LOCAL = OWN * NFREQ
FREQ_TOTAL = FREQ_LOCAL * NFREQ
ELEM_TOTAL = ELEM_LOCAL * NX * NZH
INV_NF = 1.0 / FREQ_TOTAL


def iota(shape, dim):
    return lax.broadcasted_iota(jnp.int32, shape, dim)


def omega_of(half_position):
    return 0.02 + 0.98 * half_position / FREQ_TOTAL


def inverse_of(value):
    r = pltpu.reciprocal(value, approx=True)
    r = r * (2.0 - value * r)
    return r * (2.0 - value * r)


def split(value):
    high = value.astype(jnp.bfloat16)
    return high, (value - high.astype(F32)).astype(jnp.bfloat16)


def bf_dot(a, b):
    return jnp.dot(a, b, preferred_element_type=F32)


def wrap(value, size):
    return jnp.where(value >= size, value - size, value)


def tree_sum(values):
    values = list(values)
    while len(values) > 1:
        values = [a + b for a, b in zip(values[::2], values[1::2])] + values[len(values) & ~1 :]
    return values[0]


def pick(ref, index, shape):
    out = jnp.zeros(shape, F32)
    for m in range(PAIRS):
        out = jnp.where(index == m, ref[m], out)
    return out


def over_rows(col):
    return jnp.concatenate([col, col, jnp.zeros((8, LANES), F32)], axis=0)


def pair_coefs(ci, di, cj, dj, row_sum, col_sum):
    both = di + dj
    gap = cj - ci
    tot = ci + cj
    sq = both * both
    r1 = inverse_of(sq + gap * gap)
    r2 = inverse_of(sq + tot * tot)
    alpha, beta = both * r1, gap * r1
    gamma, delta = both * r2, -tot * r2
    ap, am = alpha + gamma, alpha - gamma
    bm, bp = beta - delta, beta + delta

    def table(di, bm, bp, row_sum, col_sum):
        ss, bd, bs, da = di * ap, di * bm, di * bp, di * am
        cr = jnp.where(row_sum, jnp.where(col_sum, ss, -bd), jnp.where(col_sum, bs, da))
        ce = jnp.where(row_sum, jnp.where(col_sum, bd, ss), jnp.where(col_sum, -da, bs))
        return cr, ce

    return table(di, bm, bp, row_sum, col_sum) + table(dj, -bp, -bm, col_sum, row_sum)


def coef_tables(c_col, d_col, pf, pd):
    shape = (ROWS, LANES)
    row, col = iota(shape, 0), iota(shape, 1)
    small = iota((8, LANES), 1) & (PAIRS - 1)
    cj, dj = pick(pf, small, (8, LANES)), pick(pd, small, (8, LANES))
    tall = lambda v: jnp.concatenate([v] * (ROWS // 8), axis=0)
    inside = (row < 2 * PAIRS) & (col < 2 * PAIRS)
    cr, ce, crt, cet = pair_coefs(
        over_rows(c_col), over_rows(d_col), tall(cj), tall(dj), row < PAIRS, col < PAIRS
    )
    last_row = row == 2 * PAIRS
    last_col = col == 2 * PAIRS
    one = lambda cond: jnp.where(cond, 1.0, 0.0).astype(F32)
    cr = jnp.where(inside, cr, one(last_row & ((col < PAIRS) | last_col)))
    ce = jnp.where(inside, ce, one(last_row & (col >= PAIRS) & (col < 2 * PAIRS)))
    crt = jnp.where(inside, crt, one(last_col & (row < PAIRS)))
    cet = jnp.where(inside, cet, one(last_col & (row >= PAIRS) & (row < 2 * PAIRS)))
    return cr, ce, crt, cet


def assemble(tables, r_row, e_row, r_col, e_col):
    cr, ce, crt, cet = tables
    return cr * r_row + ce * e_row + crt * over_rows(r_col) + cet * over_rows(e_col)


def row_to_col(row_vec, first):
    row, lane = iota((PAIRS, LANES), 0), iota((PAIRS, LANES), 1)
    kept = jnp.where(lane == row + first, jnp.broadcast_to(row_vec, (PAIRS, LANES)), 0.0)
    return jnp.broadcast_to(jnp.sum(kept, axis=1, keepdims=True), (PAIRS, LANES))


def rows_from(values):
    lane = iota(values.shape, 1)
    j = lane - jnp.where(lane >= 2 * STRIDE, 2 * STRIDE, jnp.where(lane >= STRIDE, STRIDE, 0))
    r_row = jnp.where(
        j < PAIRS,
        values,
        jnp.where(j < 2 * PAIRS, pltpu.roll(values, PAIRS, 1), jnp.where(j == 2 * PAIRS, values, 0.0)),
    )
    e_row = jnp.where(
        j < PAIRS,
        pltpu.roll(values, LANES - PAIRS, 1),
        jnp.where(j < 2 * PAIRS, values, 0.0),
    )
    return r_row, e_row


def eliminate(work):
    parts = [work[8 * b : 8 * b + 8] for b in range(ROWS // 8)]
    sub = iota((8, LANES), 0)
    for first in range(0, WIDTH, 8):
        count = min(8, WIDTH - first)
        b0 = first // 8
        live = range(b0, len(parts))
        cols = [
            [jnp.broadcast_to(parts[b][:, first + t : first + t + 1], (8, LANES)) for b in live]
            for t in range(count)
        ]
        rows = [parts[b0][t : t + 1, :] for t in range(count)]
        for t in range(count):
            inv = inverse_of(cols[t][0][t : t + 1, :])
            factor = [v * inv for v in cols[t]]
            factor[0] = jnp.where(sub > t, factor[0], 0.0)
            for u in range(t + 1, count):
                lead = cols[u][0][t : t + 1, :]
                cols[u] = [v - f * lead for v, f in zip(cols[u], factor)]
                rows[u] = rows[u] - factor[0][u : u + 1, :] * rows[t]
            for n, b in enumerate(live):
                parts[b] = parts[b] - factor[n] * rows[t]
    return jnp.concatenate(parts, axis=0)


def kernel(
    pf_hbm, pd_hbm, s_hbm, red_ref, sys_ref, nrm_ref,
    pf, pd, s_buf, re_buf, im_buf, xt_buf, pieces, recv_a, sum_a, recv_b,
    buf_m, buf_x, buf_y, buf_z,
    pole_sem, load_sem, send_sem, recv_sem,
):
    elem, freq = lax.axis_index("elem"), lax.axis_index("freq")
    x, z_hi = elem // NZH, elem % NZH
    zy, core = freq // NC, freq % NC
    z_lo, y = zy // NY, zy % NY
    z = z_hi * NZL + z_lo

    def at_freq(other):
        return {"elem": elem, "freq": other}

    def at_y(other):
        return {"elem": elem, "freq": (z_lo * NY + other) * NC + core}

    def far_first(size):
        return sorted(range(size), key=lambda d: -min(d, size - d))

    sibling = at_freq(zy * NC + (1 - core))
    zy_peers = [
        wrap(z_lo + dz, NZL) * NY + wrap(y + dy, NY)
        for dy in far_first(NY)
        for dz in (1, 0)
        if dy or dz
    ]
    y_peers = [at_y(wrap(y + dy, NY)) for dy in far_first(NY) if dy]
    z_peers = []
    for dz in far_first(NZ):
        if dz:
            to = wrap(z + dz, NZ)
            hi = to // NZL
            z_peers.append({"elem": x * NZH + hi, "freq": ((to - hi * NZL) * NY + y) * NC + core})
    x_peers = []
    for dx in far_first(NX):
        for c in (1, 0):
            if dx or c:
                to = wrap(x + dx, NX)
                x_peers.append({"elem": to * NZH + z_hi, "freq": zy * NC + wrap(core + c, NC)})

    pole_loads = [
        pltpu.make_async_copy(pf_hbm, pf, pole_sem.at[0]),
        pltpu.make_async_copy(pd_hbm, pd, pole_sem.at[1]),
    ]
    for load in pole_loads:
        load.start()
    loads = []
    for k in range(CHUNKS):
        at = pl.ds(k * CHUNK, CHUNK)
        load = pltpu.make_async_copy(s_hbm.at[:, at], s_buf.at[:, at], load_sem.at[k])
        load.start()
        loads.append(load)

    barrier = pltpu.get_barrier_semaphore()

    def greet(device):
        pl.semaphore_signal(barrier, inc=1, device_id=device, device_id_type=MESH)

    z_rest = []
    for hi_step in range(1, NZH):
        hi = wrap(z_hi + hi_step, NZH)
        z_rest += [{"elem": x * NZH + hi, "freq": (lo * NY + y) * NC + core} for lo in range(NZL)]
    greets = [at_freq(zy_peer * NC + core) for zy_peer in zy_peers]
    greets += z_rest + x_peers
    for device in greets:
        greet(device)
    greeted = len(greets)

    for load in pole_loads:
        load.wait()

    column = iota((PAIRS, LANES), 0)
    c_col = pick(pf, column, (PAIRS, LANES))
    d_col = pick(pd, column, (PAIRS, LANES))
    d_sq = d_col * d_col
    half16 = iota((PAIRS, LANES), 1).astype(F32) + 0.5
    base = (freq * FREQ_LOCAL).astype(F32)
    ones = jnp.where(iota((PAIRS, FREQ_LOCAL), 0) == 0, 1.0, 0.0)
    re_buf[2 * PAIRS : BASIS, :] = ones.astype(jnp.bfloat16)
    re_buf[BASIS + 2 * PAIRS :, :] = jnp.zeros((PAIRS, FREQ_LOCAL), jnp.bfloat16)
    for tile in range(FREQ_LOCAL // LANES):
        at = pl.ds(tile * LANES, LANES)
        w = omega_of(half16 + (base + tile * LANES))
        below, above = w - c_col, w + c_col
        i1 = inverse_of(d_sq + below * below)
        i2 = inverse_of(d_sq + above * above)
        first, second = below * i1, above * i2
        re_buf[0:PAIRS, at], re_buf[BASIS : BASIS + PAIRS, at] = split(d_sq * (i1 + i2))
        re_buf[PAIRS : 2 * PAIRS, at], re_buf[BASIS + PAIRS : BASIS + 2 * PAIRS, at] = split(
            d_col * (first - second)
        )
        im_buf[0:PAIRS, at], im_buf[2 * PAIRS : 3 * PAIRS, at] = split(-d_col * (first + second))
        im_buf[PAIRS : 2 * PAIRS, at], im_buf[3 * PAIRS :, at] = split(d_sq * (i1 - i2))

    odd = y % 2
    quad = z_lo * 2 + odd
    share = NFREQ // QUAD
    halves = [slice(0, 8), slice(8, 16)]

    def mean_step(step, acc):
        acc = list(acc)
        start = ((quad * share + step) * FREQ_LOCAL).astype(F32)
        for tile in range(FREQ_LOCAL // LANES):
            w = omega_of(half16[0:8] + (start + tile * LANES))
            for h in range(2):
                below, above = w - c_col[halves[h]], w + c_col[halves[h]]
                n1 = d_sq[halves[h]] + below * below
                n2 = d_sq[halves[h]] + above * above
                r = inverse_of(n1 * n2)
                acc[2 * h] = acc[2 * h] + r * (n1 + n2)
                acc[2 * h + 1] = acc[2 * h + 1] + r * (below * n2 - above * n1)
        return tuple(acc)

    acc = lax.fori_loop(0, share, mean_step, (jnp.zeros((8, LANES), F32),) * 4)
    lane16 = iota((PAIRS, LANES), 1)
    sum_r = d_sq * jnp.sum(jnp.concatenate([acc[0], acc[2]], axis=0), axis=1, keepdims=True)
    sum_e = d_col * jnp.sum(jnp.concatenate([acc[1], acc[3]], axis=0), axis=1, keepdims=True)
    sums = jnp.where(lane16 == column, sum_r, jnp.where(lane16 == column + PAIRS, sum_e, 0.0))
    buf_m[quad] = jnp.sum(sums, axis=0, keepdims=True)

    x0 = jnp.zeros((BASIS, ELEM_LOCAL + LANES), F32)
    x1 = jnp.zeros((2 * PAIRS, ELEM_LOCAL), F32)
    for k in range(CHUNKS):
        at = pl.ds(k * CHUNK, CHUNK)
        loads[k].wait()
        s0, s1 = s_buf[0, at, :], s_buf[1, at, :]
        squares = s0 * s0 + s1 * s1
        power = tree_sum(squares[:, t * LANES : (t + 1) * LANES] for t in range(ELEM_LOCAL // LANES))
        high, low = split(jnp.concatenate([s0, power], axis=1))
        both = bf_dot(re_buf[:, at], high)
        x0 = x0 + (both[0:BASIS] + both[BASIS:] + bf_dot(re_buf[0:BASIS, at], low))
        high, low = split(s1)
        both = bf_dot(im_buf[:, at], high)
        x1 = x1 + (both[0 : 2 * PAIRS] + both[2 * PAIRS :] + bf_dot(im_buf[0 : 2 * PAIRS, at], low))
    x0, q = x0[:, 0:ELEM_LOCAL], x0[0:ROWS, ELEM_LOCAL:]

    stacked = jnp.concatenate(
        [
            x0,
            jnp.zeros((64 - BASIS, ELEM_LOCAL), F32),
            x1,
            jnp.zeros((LANES - 64 - 2 * PAIRS, ELEM_LOCAL), F32),
        ],
        axis=0,
    )
    for tile in range(ELEM_LOCAL // LANES):
        at = slice(tile * LANES, (tile + 1) * LANES)
        xt_buf[at, :] = stacked[:, at].T
    count = ELEM_LOCAL // GROUP
    thirds = [xt_buf[pl.ds(q, count, stride=GROUP), :] for q in range(GROUP)]
    lane_c = iota((count, LANES), 1)

    def spread(shift):
        rolled = [
            pltpu.roll(thirds[q], (STRIDE * q + shift) % LANES, 1) if (STRIDE * q + shift) % LANES else thirds[q]
            for q in range(GROUP)
        ]
        return jnp.where(
            lane_c < STRIDE, rolled[0], jnp.where(lane_c < 2 * STRIDE, rolled[1], rolled[2])
        )

    part0, part1 = spread(0), spread(64)
    upper = iota((8, LANES), 0) < 4
    for k in range(NZY):
        v0, v1 = part0[8 * k : 8 * k + 8], part1[8 * k : 8 * k + 8]
        pieces[0, k] = jnp.where(upper, v0, pltpu.roll(v1, 4, 0))
        pieces[1, k] = jnp.where(upper, pltpu.roll(v0, 4, 0), v1)

    pl.semaphore_wait(barrier, greeted)

    copy_a = pltpu.make_async_remote_copy(
        src_ref=pieces.at[1 - core],
        dst_ref=recv_a,
        send_sem=send_sem.at[5],
        recv_sem=recv_sem.at[5],
        device_id=sibling,
        device_id_type=MESH,
    )
    copy_a.start()
    for step in range(1, QUAD):
        lo, to = wrap(z_lo + step // 2, NZL), y - odd + wrap(odd + step % 2, 2)
        pltpu.make_async_remote_copy(
            src_ref=buf_m.at[quad],
            dst_ref=buf_m.at[quad],
            send_sem=send_sem.at[4],
            recv_sem=recv_sem.at[4],
            device_id=at_freq((lo * NY + to) * NC + core),
            device_id_type=MESH,
        ).start()

    copy_a.wait_recv()
    for k in range(NZY):
        sum_a[k] = pieces[core, k] + recv_a[k]
    for other in zy_peers:
        pltpu.make_async_remote_copy(
            src_ref=sum_a.at[other],
            dst_ref=recv_b.at[zy],
            send_sem=send_sem.at[0],
            recv_sem=recv_sem.at[0],
            device_id=at_freq(other * NC + core),
            device_id_type=MESH,
        ).start()
    recv_b[zy] = sum_a[zy]

    tables = coef_tables(c_col, d_col, pf, pd)
    rest = buf_m.at[pl.ds(0, QUAD - 1)]
    pltpu.make_async_copy(rest, rest, recv_sem.at[4]).wait()
    mean = tree_sum(buf_m[k] for k in range(QUAD)) * INV_NF
    lane1 = iota((1, LANES), 1)
    mean = jnp.where(lane1 == 2 * PAIRS, 1.0, mean)
    r_row, e_row = rows_from(mean)
    gram = assemble(tables, r_row, e_row, row_to_col(mean, 0), row_to_col(mean, PAIRS))
    row, lane = iota((ROWS, LANES), 0), iota((ROWS, LANES), 1)
    work = gram + jnp.where((lane == row + 64) & (row < WIDTH), 1.0, 0.0)
    work = eliminate(work)
    pivots = jnp.sum(jnp.where((lane == row) & (row < WIDTH), work, 0.0), axis=1, keepdims=True)
    pivots = jnp.where(iota((ROWS, 1), 0) < WIDTH, pivots, 1.0)
    inverse = pltpu.roll(work, 64, 1) * (1.0 / jnp.sqrt(pivots))
    inverse = jnp.where(lane < WIDTH, inverse, 0.0)

    q = jnp.broadcast_to(jnp.sum(q, axis=1, keepdims=True), (ROWS, LANES))
    q_row = jnp.sum(jnp.where(lane == row, q, 0.0), axis=0, keepdims=True)

    triple = [
        v + pltpu.roll(v, STRIDE, 1) + pltpu.roll(v, 2 * STRIDE, 1) for v in tables
    ]

    rest_b = recv_b.at[pl.ds(0, NZY - 1)]
    pltpu.make_async_copy(rest_b, rest_b, recv_sem.at[0]).wait()
    owned = tree_sum(recv_b[k] for k in range(NZY))
    owned = owned * (-INV_NF)

    other_part = pltpu.roll(owned, 4, 0)
    plus, minus = owned + other_part, owned - other_part
    r_rows, e_rows = rows_from(minus)
    plus_t = jnp.concatenate([plus, jnp.zeros((LANES - 8, LANES), F32)], axis=0).T
    lane16 = iota((PAIRS, LANES), 1)

    def columns(g, first):
        spread_col = [
            jnp.broadcast_to(
                plus_t[STRIDE * q + first : STRIDE * q + first + PAIRS, g : g + 1], (PAIRS, LANES)
            )
            for q in range(GROUP)
        ]
        return jnp.where(
            lane16 < STRIDE, spread_col[0], jnp.where(lane16 < 2 * STRIDE, spread_col[1], spread_col[2])
        )

    coupling = jnp.concatenate(
        [
            assemble(triple, r_rows[g : g + 1, :], e_rows[g : g + 1, :], columns(g, 0), columns(g, PAIRS))
            for g in range(TILES)
        ],
        axis=1,
    )
    reduced = jnp.dot(
        inverse[:, 0:ROWS], coupling, precision=HIGH, preferred_element_type=F32
    )
    parts = [reduced[:, g * LANES : (g + 1) * LANES] for g in range(TILES)]
    tall = jnp.concatenate(parts, axis=0)
    wide = jnp.dot(tall.T, tall, precision=HIGH, preferred_element_type=F32)
    corr = wide[0:ROWS]
    for q in range(1, GROUP):
        at = STRIDE * q
        corr = corr + pltpu.roll(wide[at : at + ROWS], LANES - at, 1)

    sub8, ln8 = iota((8, LANES), 0), iota((8, LANES), 1)
    spread8 = lambda v: jnp.broadcast_to(v, (8, LANES))
    packed = pltpu.roll(corr[24:32], 48, 1)
    for g, first, shift in ((2, 72, 40), (1, 56, 24)):
        packed = jnp.where(ln8 < first, pltpu.roll(corr[8 * g : 8 * g + 8], shift, 1), packed)
    packed = jnp.where(ln8 < 32, corr[0:8], packed)
    behind = jnp.where(
        sub8 < 2,
        spread8(packed[6:7]),
        jnp.where(
            sub8 < 4,
            spread8(packed[7:8]),
            jnp.where(sub8 == 4, spread8(corr[32:33]), spread8(q_row)),
        ),
    )
    second = (sub8 == 1) | (sub8 == 3)
    behind = jnp.where(second, pltpu.roll(behind, 32, 1), pltpu.roll(behind, 80, 1))
    total = jnp.where(ln8 < 80, packed, behind)[0:SUMS]

    def send(buf, me, peers, index, value):
        buf[me] = value
        for device in peers:
            pltpu.make_async_remote_copy(
                src_ref=buf.at[me],
                dst_ref=buf.at[me],
                send_sem=send_sem.at[index],
                recv_sem=recv_sem.at[index],
                device_id=device,
                device_id_type=MESH,
            ).start()

    def receive(buf, count, index):
        rest = buf.at[pl.ds(0, count - 1)]
        pltpu.make_async_copy(rest, rest, recv_sem.at[index]).wait()
        return tree_sum(buf[k] for k in range(count))

    send(buf_x, x * NC + core, x_peers, 1, total)

    for g in range(TILES):
        for q in range(GROUP):
            block = pltpu.roll(parts[g], LANES - STRIDE * q, 1) if q else parts[g]
            red_ref[GROUP * g + q] = block[0:WIDTH, 0:WIDTH]

    total = receive(buf_x, NX * NC, 1)
    send(buf_y, y, y_peers, 2, total)
    total = receive(buf_y, NY, 2)
    send(buf_z, z, z_peers, 3, total)
    total = receive(buf_z, NZ, 3)

    total = jnp.concatenate([total, jnp.zeros((8 - SUMS, LANES), F32)], axis=0)
    by_80, by_32 = pltpu.roll(total, LANES - 80, 1), pltpu.roll(total, LANES - 32, 1)
    row_6 = jnp.where(lane1 < 48, by_80[0:1], by_32[1:2])
    row_7 = jnp.where(lane1 < 48, by_80[2:3], by_32[3:4])
    total = jnp.where(sub8 == 6, spread8(row_6), jnp.where(sub8 == 7, spread8(row_7), total))
    border = by_80[4:5]
    moments = jnp.where(lane1 < WIDTH, by_80[5:6], 0.0) * INV_NF
    mean_sq = moments[:, 2 * PAIRS : 2 * PAIRS + 1]
    r_row, e_row = rows_from(moments)
    data_gram = assemble(
        tables, r_row, e_row, row_to_col(moments, 0), row_to_col(moments, PAIRS)
    )
    half = jnp.concatenate(
        [total]
        + [pltpu.roll(total, LANES - shift, 1) for shift in (24, 40, 48)]
        + [spread8(border)],
        axis=0,
    )
    square = jnp.concatenate([half, jnp.zeros((LANES - ROWS, LANES), F32)], axis=0)
    stored = ((lane < 2 * PAIRS) & (lane >= (row & ~7))) | (row >= 2 * PAIRS)
    correction = jnp.where(stored, half, square.T[0:ROWS])
    system = (data_gram - correction) * (1.0 / mean_sq)
    sys_ref[...] = system[0:WIDTH, 0:WIDTH]
    nrm_ref[...] = (mean * jnp.sqrt(mean_sq * (1.0 / ELEM_TOTAL)))[:, 0:WIDTH]

    copy_a.wait_send()
    for buf, count, index in (
        (sum_a, NZY, 0), (buf_x, NX * NC, 1), (buf_y, NY, 2), (buf_z, NZ, 3), (buf_m, QUAD, 4)
    ):
        rest = buf.at[pl.ds(0, count - 1)]
        pltpu.make_async_copy(rest, rest, send_sem.at[index]).wait()


def writer(red, sys, nrm, red_out, sys_out, nrm_out):
    red_out[...] = red[...]
    sys_out[...] = sys[...]
    nrm_out[...] = nrm[...]


def per_device(pole_freq, pole_damp, samples):
    vmem = lambda *shape: pltpu.VMEM(shape, F32)
    in_hbm = lambda v: pltpu.with_memory_space_constraint(v, pltpu.HBM)
    half = lambda *shape: pltpu.VMEM(shape, jnp.bfloat16)
    results = (
        vmem(OWN, WIDTH, WIDTH),
        vmem(WIDTH, WIDTH),
        vmem(1, WIDTH),
    )
    reduced, system, norm_row = pl.pallas_call(
        kernel,
        out_shape=results,
        in_specs=[pl.BlockSpec(memory_space=pltpu.HBM)] * 3,
        out_specs=(pl.BlockSpec(memory_space=pltpu.VMEM),) * 3,
        scratch_shapes=[
            pltpu.SMEM((PAIRS,), F32),
            pltpu.SMEM((PAIRS,), F32),
            vmem(2, FREQ_LOCAL, ELEM_LOCAL),
            half(2 * BASIS, FREQ_LOCAL),
            half(4 * PAIRS, FREQ_LOCAL),
            vmem(ELEM_LOCAL, LANES),
            vmem(NC, NZY, 8, LANES),
            vmem(NZY, 8, LANES),
            vmem(NZY, 8, LANES),
            vmem(NZY, 8, LANES),
            vmem(QUAD, 1, LANES),
            vmem(NX * NC, SUMS, LANES),
            vmem(NY, SUMS, LANES),
            vmem(NZ, SUMS, LANES),
            pltpu.SemaphoreType.DMA((2,)),
            pltpu.SemaphoreType.DMA((CHUNKS,)),
            pltpu.SemaphoreType.DMA((6,)),
            pltpu.SemaphoreType.DMA((6,)),
        ],
        compiler_params=pltpu.CompilerParams(
            collective_id=0, has_side_effects=True, vmem_limit_bytes=40 * 1024 * 1024
        ),
    )(*(in_hbm(v) for v in (pole_freq, pole_damp, samples)))
    in_vmem = lambda v: pltpu.with_memory_space_constraint(v, pltpu.VMEM)
    reduced, system, norm_row = pl.pallas_call(
        writer,
        out_shape=(
            jax.ShapeDtypeStruct((OWN, WIDTH, WIDTH), F32),
            jax.ShapeDtypeStruct((WIDTH, WIDTH), F32),
            jax.ShapeDtypeStruct((1, WIDTH), F32),
        ),
        in_specs=[pl.BlockSpec(memory_space=pltpu.VMEM)] * 3,
        out_specs=(pl.BlockSpec(memory_space=pltpu.VMEM),) * 3,
        compiler_params=pltpu.CompilerParams(vmem_limit_bytes=48 * 1024 * 1024),
    )(in_vmem(reduced), in_vmem(system), in_vmem(norm_row))
    return jnp.transpose(reduced, (1, 2, 0)), system, norm_row.reshape(WIDTH)


def solution(mesh):
    placed = (P(), P(), P(None, "freq", "elem"))
    return jax.shard_map(
        per_device,
        mesh=mesh,
        in_specs=placed,
        out_specs=(P(None, None, ("elem", "freq")), P(), P()),
        check_vma=False,
    )
```
